512 devices in a mesh: dp: 64 (over z, y_hi, core), tensor: 8 (over x, y_lo).
Axes of the slice: x: 4, y: 4 (y_hi: 2, y_lo: 2; y = y_hi * 2 + y_lo), z: 16, core: 2. Of those that a mesh axis runs over, the one named last changes fastest.
Arguments:
- text_hidden: bfloat16 [10240, 1152], P('dp'), may hold values from -6 to 6
- ln_gain: float32 [1152], replicated, may hold values from 0.25 to 1.75
- up_weight: bfloat16 [1152, 4304], P(None, 'tensor'), may hold values from -0.1875 to 0.1875
- down_weight: bfloat16 [4304, 1152], P('tensor'), may hold values from -0.09375 to 0.09375
- final_gain: float32 [1152], replicated, may hold values from 0.1 to 1.9
- head_weight: bfloat16 [1152, 1152], P('tensor'), may hold values from -0.1875 to 0.1875
- image_features: bfloat16 [10240, 1152], P('dp'), may hold values from -16 to 16
- vision_weight: bfloat16 [1152, 1152], P(None, 'tensor'), may hold values from -0.1875 to 0.1875
Outputs:
- text_grad: float32 [10240, 1152], P(('dp', 'tensor'))
- vision_grad: float32 [1152, 1152], P('dp', 'tensor')
The draws below stay inside these ranges and needn't reach their ends.
All inputs are finite; a program needn't handle non-finite values.
Results may differ from the reference program's by a relative error of at most 0.0065.
Values may be sent and summed in bfloat16 or wider, within the bound.
A program may use at most 64 MiB of HBM per device.

```python
import jax
import jax.numpy as jnp
from jax import lax

D = 1152
FF = 4304
E = 1152
ROWS_DEV = 160
PAIRS = 10240


def raised(values, own_key, source, target, shards_of, factor):
    owner, partner = [(jnp.arange(values.shape[axis_at]) // (values.shape[axis_at] // shards_of)).reshape([-1 if axis == axis_at else 1 for axis in range(values.ndim)]) for axis_at in (source, target)]
    chosen = jax.random.permutation(own_key, shards_of)[partner]
    strong = (owner == chosen) | (owner == (partner + shards_of // 2) % shards_of)
    return jnp.where(strong, factor * values, values)


def block_levels(own_key, shape, shards, least, high):
    level = 1.0
    for axis_at, blocks in shards:
        draws = jax.random.uniform(jax.random.fold_in(jax.random.fold_in(own_key, 6), axis_at), (blocks,), jnp.float32, least / len(shards), high / len(shards))
        level = level * jnp.repeat(jnp.exp(draws), shape[axis_at] // blocks).reshape((-1,) + (1,) * (len(shape) - 1 - axis_at))
    return level


def scatter_about(rng, shape, scale, reach, shards=(), kind=jnp.bfloat16):
    result = jax.random.normal(rng, shape, jnp.float32) * scale
    if len(shards) > 0:
        result = block_levels(rng, shape, shards, -0.22, 0.18) * result
    return jnp.clip(result, min=-reach, max=reach).astype(kind)


def noise_with(own_key, extent, scale, limit, cuts, heavy, kind=jnp.bfloat16):
    drawn = scale * jax.random.normal(own_key, extent, jnp.float32)
    if cuts:
        drawn = drawn * block_levels(own_key, extent, cuts, -0.22, 0.18)
    return jnp.clip(raised(drawn, jax.random.fold_in(own_key, 3), *heavy), -limit, limit).astype(kind)


def setup_inputs(seed: int = 0) -> dict:
    seeds = jax.random.split(jax.random.key(seed), 9)
    text_hidden = scatter_about(seeds[0], (PAIRS, D), 1.0, 6.0, ((0, 64),))
    ln_gain = jnp.clip(1.0 + 0.15 * jax.random.normal(seeds[1], (D,), jnp.float32), 0.25, 1.75)
    up_weight = scatter_about(seeds[2], (D, FF), D ** -0.5, 0.1875, ((1, 8),))
    down_weight = scatter_about(seeds[3], (FF, D), FF ** -0.5, 0.09375, ((0, 8),))
    final_gain = jnp.clip(1.0 + 0.18 * jax.random.normal(seeds[4], (D,), jnp.float32), 0.1, 1.9)
    head_weight = scatter_about(seeds[5], (D, E), D ** -0.5, 0.1875, ((0, 8),))
    image_features = noise_with(seeds[6], (PAIRS, D), 1.0, 16.0, ((0, 64),), (0, 1, 64, 4.0))
    vision_weight = scatter_about(seeds[7], (D, E), D ** -0.5, 0.1875, ((1, 8),))
    return dict(text_hidden=text_hidden, ln_gain=ln_gain, up_weight=up_weight, down_weight=down_weight, final_gain=final_gain, head_weight=head_weight, image_features=image_features, vision_weight=vision_weight)


logit_scale = 100.0
logit_bias = -4.0
norm_eps = 1e-06

def contract(left_side, right_side, left_dim, right_dim):
    return lax.dot_general(left_side.astype(jnp.float32), right_side.astype(jnp.float32), (((left_dim,), (right_dim,)), ((), ())), preferred_element_type=jnp.float32)

def layer_norm(values, gain_row):
    center = values - lax.optimization_barrier(jnp.mean(values, axis=1, keepdims=True))
    spread = lax.optimization_barrier(jnp.mean(center * center, axis=1, keepdims=True))
    return center * lax.rsqrt(spread + norm_eps) * gain_row

def unit_rows(values):
    inverse = lax.rsqrt(lax.optimization_barrier(jnp.sum(values * values, axis=1, keepdims=True)) + norm_eps)
    return (values * inverse, inverse)

def reference(text_hidden, ln_gain, up_weight, down_weight, final_gain, head_weight, image_features, vision_weight):
    hidden = text_hidden.astype(jnp.float32)
    lifted = layer_norm(hidden, ln_gain).astype(jnp.bfloat16)
    active = jax.nn.gelu(jnp.dot(lifted, up_weight, preferred_element_type=jnp.float32), approximate=True).astype(jnp.bfloat16)
    mixed = jnp.dot(active, down_weight, preferred_element_type=jnp.float32)
    normed = layer_norm(hidden + mixed, final_gain).astype(jnp.bfloat16)
    text_emb = jnp.dot(normed, head_weight, preferred_element_type=jnp.float32)
    text_unit = unit_rows(text_emb)[0].astype(jnp.bfloat16)
    image_emb = jnp.dot(image_features, vision_weight, preferred_element_type=jnp.float32)
    image_float, inverse = unit_rows(image_emb)
    image_unit = image_float.astype(jnp.bfloat16)
    total_pairs = text_unit.shape[0]
    block_count = total_pairs // ROWS_DEV
    image_blocks = image_unit.reshape(block_count, ROWS_DEV, image_unit.shape[1])
    text_ids = jnp.arange(total_pairs, dtype=jnp.int32)
    local_ids = jnp.arange(ROWS_DEV, dtype=jnp.int32)

    def one_block(carried, packed):
        block_index, image_block = packed
        logits = logit_scale * contract(image_block, text_unit, 1, 1) + logit_bias
        image_ids = block_index * ROWS_DEV + local_ids
        positive = (image_ids[:, None] == text_ids[None, :]).astype(jnp.float32)
        weights = ((jax.nn.sigmoid(logits) - positive) * (logit_scale / ROWS_DEV)).astype(jnp.bfloat16)
        image_grad = contract(weights, text_unit, 1, 0)
        return (carried + contract(weights, image_block, 0, 0), image_grad)
    start_grad = jnp.zeros((total_pairs, text_unit.shape[1]), jnp.float32)
    text_grad, image_grads = lax.scan(one_block, start_grad, (jnp.arange(block_count, dtype=jnp.int32), image_blocks))
    image_grad = image_grads.reshape(total_pairs, image_unit.shape[1])
    radial = lax.optimization_barrier(jnp.sum(image_float * image_grad, axis=1, keepdims=True))
    emb_grad = ((image_grad - image_float * radial) * inverse).astype(jnp.bfloat16)
    vision_grad = contract(image_features, emb_grad, 0, 0)
    return (text_grad, vision_grad)
```

```python
import functools

import jax
import jax.numpy as jnp
from jax import lax
from jax.experimental import pallas as pl
from jax.experimental.pallas import tpu as pltpu
from jax.sharding import PartitionSpec as P

logit_scale = 100.0
logit_bias = -4.0
norm_eps = 1e-06
MESH = pl.DeviceIdType.MESH
F32 = jnp.float32
BF16 = jnp.bfloat16

D = 1152
E = 1152
ROWS = 160
TS = 8
ZS = 16
HALF = ZS // 2
TEXTS = ROWS // TS
CHUNK = 2 * TEXTS
IMGS = 2 * ROWS
PIECE = E // (2 * TS)
COLS = E // TS
ZROWS = D // ZS


def mm(a, b):
    return jnp.dot(a, b, preferred_element_type=F32)


def layer_norm(values, gain_row):
    center = values - jnp.mean(values, axis=1, keepdims=True)
    spread = jnp.mean(center * center, axis=1, keepdims=True)
    return center * lax.rsqrt(spread + norm_eps) * gain_row


S_FEAT = 0
S_IMG = 1
S_IMGC = S_IMG + TS
S_MIX = S_IMGC + 1
S_NRM = S_MIX + TS
S_HEAD = S_NRM + TS
S_YH = S_HEAD + TS
S_AGP = S_YH + 1
S_AGM = S_AGP + HALF
S_RSP = S_AGM + HALF
S_RSM = S_RSP + HALF
S_YG = S_RSM + HALF
S_CX = S_YG + 1
S_PX = S_CX + 1
S_VRP = S_PX + TS
S_VRM = S_VRP + HALF
S_FX = S_VRM + HALF
S_ALL = S_FX + 4


def kernel(
    text_ref,
    ln_ref,
    up_ref,
    down_ref,
    fg_ref,
    head_ref,
    feat_ref,
    vis_ref,
    tg_ref,
    vg_ref,
    feats,
    part_t,
    img_s,
    img_r,
    img_f,
    img_ut,
    img_u,
    inv_ref,
    mix_s,
    mix_f,
    mix_r,
    nrm_s,
    nrm_r,
    nrm_a,
    head_s,
    head_f,
    head_r,
    yh_s,
    yh_r,
    chunk_f,
    texts,
    grads,
    eg,
    rs_s,
    rs_r,
    yg_s,
    yg_r,
    cx_s,
    cx_r,
    px_f,
    px_s,
    px_r,
    vg_all,
    vr_s,
    vr_r,
    fx,
    send_sem,
    recv_sem,
):
    d = lax.axis_index("dp")
    t = lax.axis_index("tensor")
    z = d // 4
    yh = (d // 2) % 2
    c = d % 2
    base = d - 4 * z
    z_next = (lax.rem(z + 1, ZS) * 4 + base, t)
    z_prev = (lax.rem(z + ZS - 1, ZS) * 4 + base, t)
    yh_peer = (d + 2 - 4 * yh, t)
    c_peer = (d + 1 - 2 * c, t)
    q = 2 * yh + c

    def zmod(v):
        return lax.rem(v + 2 * ZS, ZS)

    def tpeer(k):
        return lax.rem(t + k, TS)

    def rcopy(src, dst, i_send, i_recv, dev):
        return pltpu.make_async_remote_copy(
            src_ref=src,
            dst_ref=dst,
            send_sem=send_sem.at[i_send],
            recv_sem=recv_sem.at[i_recv],
            device_id=dev,
            device_id_type=MESH,
        )

    barrier = pltpu.get_barrier_semaphore()
    greeted = [z_next, z_prev] + [(d, tpeer(k)) for k in range(1, TS)]
    fx_peers = [(4 * z + lax.rem(q + k, 4), t) for k in range(1, 4)]
    greeted = greeted + fx_peers
    for dev in greeted:
        pl.semaphore_signal(barrier, inc=1, device_id=dev, device_id_type=MESH)

    own_rows = pl.ds(pl.multiple_of(ROWS * c, 32), ROWS)
    feats[own_rows, :] = feat_ref[...]
    hidden = text_ref[...].astype(F32)
    lifted = layer_norm(hidden, ln_ref[...]).astype(BF16)

    pl.semaphore_wait(barrier, len(greeted))
    feat_copy = rcopy(feats.at[own_rows], feats.at[own_rows], S_FEAT, S_FEAT, c_peer)
    feat_copy.start()

    active = jax.nn.gelu(mm(lifted, up_ref[...]), approximate=True).astype(BF16)

    other_rows = pl.ds(pl.multiple_of(ROWS * (1 - c), 32), ROWS)
    feat_copy.wait_send()
    rcopy(feats.at[other_rows], feats.at[other_rows], S_FEAT, S_FEAT, c_peer).wait_recv()

    part_t[...] = mm(feats[...], vis_ref[...]).T
    img_s[...] = part_t[pl.ds(pl.multiple_of(PIECE * c, 8), PIECE), :].astype(BF16)
    for k in range(1, TS):
        rcopy(img_s, img_r.at[c, t], S_IMG + k, S_IMG + t, (d, tpeer(k))).start()
    img_r[c, t] = img_s[...]

    mixed = mm(active, down_ref[...])
    with_hidden = mixed + hidden
    for j in range(TS):
        mix_s[j] = mixed[TEXTS * j : TEXTS * (j + 1)].astype(BF16)
        mix_f[j] = with_hidden[TEXTS * j : TEXTS * (j + 1)]

    def exchange_start(src, dst, sem):
        for k in range(1, TS):
            rcopy(src.at[tpeer(k)], dst.at[t], sem + k, sem + t, (d, tpeer(k))).start()

    def exchange_wait(src, dst, sem):
        for k in range(1, TS):
            j = tpeer(k)
            rcopy(src.at[j], dst.at[t], sem + k, sem + t, (d, j)).wait_send()
            rcopy(src.at[j], dst.at[j], sem + k, sem + j, (d, j)).wait_recv()

    exchange_start(mix_s, mix_r, S_MIX)
    mix_r[t] = jnp.zeros((TEXTS, D), BF16)

    for k in range(1, TS):
        j = tpeer(k)
        rcopy(img_s, img_r.at[c, t], S_IMG + k, S_IMG + t, (d, j)).wait_send()
        rcopy(img_s, img_r.at[c, j], S_IMG + k, S_IMG + j, (d, j)).wait_recv()
    imgc_copy = rcopy(img_r.at[c], img_r.at[c], S_IMGC, S_IMGC, c_peer)
    imgc_copy.start()

    exchange_wait(mix_s, mix_r, S_MIX)
    total = mix_f[t]
    for j in range(TS):
        total = total + mix_r[j].astype(F32)
    normed = layer_norm(total, fg_ref[...]).astype(BF16).astype(F32)
    for j in range(TS):
        nrm_s[j] = normed[:, COLS * j : COLS * (j + 1)].astype(BF16)
    exchange_start(nrm_s, nrm_r, S_NRM)
    nrm_r[t] = nrm_s[t]
    exchange_wait(nrm_s, nrm_r, S_NRM)
    for j in range(TS):
        nrm_a[TEXTS * j : TEXTS * (j + 1), :] = nrm_r[j].astype(F32)
    head_part = mm(nrm_a[...].astype(BF16), head_ref[...])
    for j in range(TS):
        head_f[j] = head_part[TEXTS * j : TEXTS * (j + 1)]
        head_s[j] = head_part[TEXTS * j : TEXTS * (j + 1)].astype(BF16)
    exchange_start(head_s, head_r, S_HEAD)
    head_r[t] = jnp.zeros((TEXTS, E), BF16)

    imgc_copy.wait_send()
    rcopy(img_r.at[1 - c], img_r.at[1 - c], S_IMGC, S_IMGC, c_peer).wait_recv()
    for j in range(TS):
        for h in range(2):
            at = COLS * j + PIECE * h
            img_f[at : at + PIECE, :] = img_r[h, j].astype(F32)
    emb_t = img_f[...]
    inverse = lax.rsqrt(jnp.sum(emb_t * emb_t, axis=0, keepdims=True) + norm_eps)
    inv_ref[...] = inverse
    unit_t = emb_t * inverse
    img_f[...] = unit_t
    img_ut[...] = unit_t.astype(BF16)
    img_u[...] = unit_t.T.astype(BF16)
    eg[...] = jnp.zeros_like(eg)

    exchange_wait(head_s, head_r, S_HEAD)
    text_emb = head_f[t]
    for j in range(TS):
        text_emb = text_emb + head_r[j].astype(F32)
    text_unit = text_emb * lax.rsqrt(
        jnp.sum(text_emb * text_emb, axis=1, keepdims=True) + norm_eps
    )
    text_unit = text_unit.astype(BF16)
    yh_s[...] = text_unit
    yh_copy = rcopy(yh_s, yh_r, S_YH, S_YH, yh_peer)
    yh_copy.start()
    chunk_f[0:TEXTS, :] = text_unit.astype(F32)
    yh_copy.wait()
    chunk_f[TEXTS:CHUNK, :] = yh_r[...].astype(F32)
    texts[z] = chunk_f[...].astype(BF16)

    def ag_plus(s):
        at = zmod(z - s + 1)
        return rcopy(texts.at[at], texts.at[at], S_AGP + s - 1, S_AGP + s - 1, z_next)

    def ag_minus(s):
        at = zmod(z + s - 1)
        return rcopy(texts.at[at], texts.at[at], S_AGM + s - 1, S_AGM + s - 1, z_prev)

    def ag_plus_in(s):
        at = zmod(z - s)
        return rcopy(texts.at[at], texts.at[at], S_AGP + s - 1, S_AGP + s - 1, z_next)

    def ag_minus_in(s):
        at = zmod(z + s)
        return rcopy(texts.at[at], texts.at[at], S_AGM + s - 1, S_AGM + s - 1, z_prev)

    row_ids = lax.broadcasted_iota(jnp.int32, (CHUNK, IMGS), 0)
    col_ids = lax.broadcasted_iota(jnp.int32, (CHUNK, IMGS), 1)
    diagonal = ((row_ids < TEXTS) & (col_ids == row_ids + ROWS * c + TEXTS * t)).astype(F32)

    def process(origin, own):
        block = texts[origin]
        logits = logit_scale * mm(block, img_ut[...]) + logit_bias
        weights = jax.nn.sigmoid(logits)
        if own:
            weights = weights - diagonal
        weights = (weights * (logit_scale / ROWS)).astype(BF16)
        grads[origin] = mm(weights, img_u[...])
        eg[...] += lax.dot_general(
            block, weights, (((0,), (0,)), ((), ())), preferred_element_type=F32
        )

    ag_plus(1).start()
    ag_minus(1).start()
    process(z, True)

    def ag_step(s, _):
        ag_plus_in(s).wait_recv()
        ag_plus(s + 1).start()
        process(zmod(z - s), False)
        ag_minus_in(s).wait_recv()

        @pl.when(s < HALF - 1)
        def _():
            ag_minus(s + 1).start()

        process(zmod(z + s), False)
        return 0

    lax.fori_loop(1, HALF, ag_step, 0)

    def rs_copy(way, s):
        sem = (S_RSP, S_RSM)[way] + s - 1
        return rcopy(rs_s.at[way, s - 1], rs_r.at[way, s - 1], sem, sem, (z_next, z_prev)[way])

    def rs_step(way, s):
        owner = zmod(z + HALF + 1 - s) if way == 0 else zmod(z - HALF + s)
        value = grads[owner]
        if s > 1:
            rs_copy(way, s - 1).wait_recv()
            value = value + rs_r[way, s - 2].astype(F32)
        rs_s[way, s - 1] = value.astype(BF16)
        rs_copy(way, s).start()

    rs_step(1, 1)
    ag_plus_in(HALF).wait_recv()
    process(zmod(z - HALF), False)
    rs_step(0, 1)

    image_grad = eg[...]
    unit_t = img_f[...]
    radial = jnp.sum(unit_t * image_grad, axis=0, keepdims=True)
    eg[...] = (image_grad - unit_t * radial) * inv_ref[...]
    for j in range(TS):
        theirs = pl.ds(pl.multiple_of(COLS * j + PIECE * (1 - c), 8), PIECE)
        cx_s[j] = eg[theirs, :].astype(BF16)
    cx_copy = rcopy(cx_s, cx_r, S_CX, S_CX, c_peer)
    cx_copy.start()
    rs_step(1, 2)
    rs_step(0, 2)
    cx_copy.wait()
    for j in range(TS):
        mine = pl.ds(pl.multiple_of(COLS * j + PIECE * c, 8), PIECE)
        value = eg[mine, :] + cx_r[j].astype(F32)
        px_f[j] = value
        px_s[j] = value.astype(BF16)
    exchange_start(px_s, px_r, S_PX)
    px_r[t] = jnp.zeros((PIECE, IMGS), BF16)
    rs_step(1, 3)
    rs_step(0, 3)
    rs_step(1, 4)
    rs_step(0, 4)
    exchange_wait(px_s, px_r, S_PX)
    emb_grad = px_f[t]
    for j in range(TS):
        emb_grad = emb_grad + px_r[j].astype(F32)
    vg_all[...] = mm(emb_grad.astype(BF16), feats[...]).T

    def vr_copy(way, s):
        sem = (S_VRP, S_VRM)[way] + s - 1
        return rcopy(vr_s.at[way, s - 1], vr_r.at[way, s - 1], sem, sem, (z_next, z_prev)[way])

    def vg_chunk(owner):
        return vg_all[pl.ds(pl.multiple_of(ZROWS * owner, 8), ZROWS), :]

    def vr_step(way, s):
        owner = zmod(z + HALF + 1 - s) if way == 0 else zmod(z - HALF + s)
        value = vg_chunk(owner)
        if s > 1:
            vr_copy(way, s - 1).wait_recv()
            value = value + vr_r[way, s - 2]
        vr_s[way, s - 1] = value
        vr_copy(way, s).start()

    for s in range(1, HALF + 1):
        vr_step(0, s)
        if s < HALF:
            vr_step(1, s)
        r = s + 4
        if r <= HALF:
            if r < HALF:
                rs_step(1, r)
            rs_step(0, r)
        if r == HALF + 1:
            rs_copy(0, HALF).wait_recv()
            rs_copy(1, HALF - 1).wait_recv()
            chunk_f[...] = (
                grads[z] + rs_r[0, HALF - 1].astype(F32) + rs_r[1, HALF - 2].astype(F32)
            )
            yg_s[...] = chunk_f[TEXTS:CHUNK, :]
            rcopy(yg_s, yg_r, S_YG, S_YG, yh_peer).start()

    rcopy(yg_s, yg_r, S_YG, S_YG, yh_peer).wait()
    tg_ref[...] = chunk_f[0:TEXTS, :] + yg_r[...]

    vr_copy(0, HALF).wait_recv()
    vr_copy(1, HALF - 1).wait_recv()
    fx[q] = vg_chunk(z) + vr_r[0, HALF - 1] + vr_r[1, HALF - 2]
    for k in range(1, 4):
        rcopy(fx.at[q], fx.at[q], S_FX + k, S_FX + q, fx_peers[k - 1]).start()

    def ag_drain(s, _):
        ag_plus(s).wait_send()

        @pl.when(s < HALF)
        def _():
            ag_minus(s).wait_send()

        return 0

    lax.fori_loop(1, HALF + 1, ag_drain, 0)
    for s in range(1, HALF + 1):
        for way in range(2):
            if s < HALF or way == 0:
                rs_copy(way, s).wait_send()
                vr_copy(way, s).wait_send()

    for k in range(1, 4):
        o = lax.rem(q + k, 4)
        rcopy(fx.at[q], fx.at[q], S_FX + k, S_FX + q, fx_peers[k - 1]).wait_send()
        rcopy(fx.at[o], fx.at[o], S_FX + k, S_FX + o, fx_peers[k - 1]).wait_recv()
    left = fx[0] + fx[2]
    right = fx[1] + fx[3]
    for k in range(4):

        @pl.when(q == k)
        def _():
            vg_ref[:, 0:PIECE] = left[18 * k : 18 * (k + 1), :]
            vg_ref[:, PIECE:COLS] = right[18 * k : 18 * (k + 1), :]


def local(
    text_hidden,
    ln_gain,
    up_weight,
    down_weight,
    final_gain,
    head_weight,
    image_features,
    vision_weight,
):
    vmem = pl.BlockSpec(memory_space=pltpu.VMEM)
    scratch = [
        ((IMGS, D), BF16),
        ((COLS, IMGS), F32),
        ((PIECE, IMGS), BF16),
        ((2, TS, PIECE, IMGS), BF16),
        ((E, IMGS), F32),
        ((E, IMGS), BF16),
        ((IMGS, E), BF16),
        ((1, IMGS), F32),
        ((TS, TEXTS, D), BF16),
        ((TS, TEXTS, D), F32),
        ((TS, TEXTS, D), BF16),
        ((TS, TEXTS, COLS), BF16),
        ((TS, TEXTS, COLS), BF16),
        ((ROWS, COLS), F32),
        ((TS, TEXTS, E), BF16),
        ((TS, TEXTS, E), F32),
        ((TS, TEXTS, E), BF16),
        ((TEXTS, E), BF16),
        ((TEXTS, E), BF16),
        ((CHUNK, E), F32),
        ((ZS, CHUNK, E), BF16),
        ((ZS, CHUNK, E), F32),
        ((E, IMGS), F32),
        ((2, HALF, CHUNK, E), BF16),
        ((2, HALF, CHUNK, E), BF16),
        ((TEXTS, E), F32),
        ((TEXTS, E), F32),
        ((TS, PIECE, IMGS), BF16),
        ((TS, PIECE, IMGS), BF16),
        ((TS, PIECE, IMGS), F32),
        ((TS, PIECE, IMGS), BF16),
        ((TS, PIECE, IMGS), BF16),
        ((D, PIECE), F32),
        ((2, HALF, ZROWS, PIECE), F32),
        ((2, HALF, ZROWS, PIECE), F32),
        ((4, ZROWS, PIECE), F32),
    ]
    return pl.pallas_call(
        kernel,
        out_shape=(
            jax.ShapeDtypeStruct((TEXTS, E), F32),
            jax.ShapeDtypeStruct((D // 64, COLS), F32),
        ),
        in_specs=[vmem] * 8,
        out_specs=(vmem, vmem),
        scratch_shapes=[pltpu.VMEM(shape, kind) for shape, kind in scratch]
        + [pltpu.SemaphoreType.DMA((S_ALL,)), pltpu.SemaphoreType.DMA((S_ALL,))],
        compiler_params=pltpu.CompilerParams(
            collective_id=0, has_side_effects=True, vmem_limit_bytes=56 * 1024 * 1024
        ),
    )(
        text_hidden,
        ln_gain.reshape(1, D),
        up_weight,
        down_weight,
        final_gain.reshape(1, D),
        head_weight,
        image_features,
        vision_weight,
    )


def solution(mesh):
    placed = (
        P("dp", None),
        P(),
        P(None, "tensor"),
        P("tensor", None),
        P(),
        P("tensor", None),
        P("dp", None),
        P(None, "tensor"),
    )
    return jax.shard_map(
        local,
        mesh=mesh,
        in_specs=placed,
        out_specs=(P(("dp", "tensor"), None), P("dp", "tensor")),
        check_vma=False,
    )
```

```python
import functools

import jax
import jax.numpy as jnp
from jax import lax
from jax.experimental import pallas as pl
from jax.experimental.pallas import tpu as pltpu
from jax.sharding import PartitionSpec as P

logit_scale = 100.0
logit_bias = -4.0
norm_eps = 1e-06
MESH = pl.DeviceIdType.MESH
F32 = jnp.float32
BF16 = jnp.bfloat16

D = 1152
E = 1152
ROWS = 160
TS = 8
ZS = 16
HALF = ZS // 2
FF_DEV = 4304 // TS
TEXTS = ROWS // TS
CHUNK = 2 * TEXTS
IMGS = 2 * ROWS
PIECE = E // (2 * TS)
COLS = E // TS
ZROWS = D // ZS


def mm(a, b):
    return jnp.dot(a, b, preferred_element_type=F32)


def mm_t(a, b):
    return lax.dot_general(a, b, (((1,), (1,)), ((), ())), preferred_element_type=F32)


def layer_norm(values, gain_row):
    center = values - jnp.mean(values, axis=1, keepdims=True)
    spread = jnp.mean(center * center, axis=1, keepdims=True)
    return center * lax.rsqrt(spread + norm_eps) * gain_row


S_FEAT = 0
S_IMG = 1
S_IMGC = S_IMG + TS
S_MIX = S_IMGC + 1
S_NRM = S_MIX + TS
S_HEAD = S_NRM + TS
S_YH = S_HEAD + TS
S_AG = S_YH + 1
S_RS = S_AG + 4 * HALF
S_YG = S_RS + 4 * HALF
S_CX = S_YG + 1
S_PX = S_CX + 1
S_VRP = S_PX + TS
S_VRM = S_VRP + HALF
S_FX = S_VRM + HALF
S_ALL = S_FX + 4
L_FEAT, L_UP, L_DOWN, L_HEAD, L_VIS = range(5)


def kernel(
    text_ref,
    ln_ref,
    up_ref,
    down_ref,
    fg_ref,
    head_ref,
    feat_ref,
    vis_ref,
    tg_ref,
    vg_ref,
    up_v,
    down_v,
    head_v,
    vis_v,
    feats,
    part_t,
    img_s,
    img_r,
    img_f,
    img_ut,
    img_u,
    inv_ref,
    mix_s,
    mix_f,
    mix_r,
    nrm_s,
    nrm_r,
    nrm_a,
    head_s,
    head_f,
    head_r,
    block_f,
    texts,
    grads,
    eg,
    rs_s,
    rs_r,
    yg_s,
    yg_r,
    cx_s,
    cx_r,
    px_f,
    px_s,
    px_r,
    vg_all,
    vr_s,
    vr_r,
    fx,
    send_sem,
    recv_sem,
    load_sem,
):
    d = lax.axis_index("dp")
    t = lax.axis_index("tensor")
    z = d // 4
    yh = (d // 2) % 2
    c = d % 2
    base = d - 4 * z
    z_next = (lax.rem(z + 1, ZS) * 4 + base, t)
    z_prev = (lax.rem(z + ZS - 1, ZS) * 4 + base, t)
    yh_peer = (d + 2 - 4 * yh, t)
    c_peer = (d + 1 - 2 * c, t)
    q = 2 * yh + c

    def zmod(v):
        return lax.rem(v + 2 * ZS, ZS)

    def tpeer(k):
        return lax.rem(t + k, TS)

    def rcopy(src, dst, i_send, i_recv, dev):
        return pltpu.make_async_remote_copy(
            src_ref=src,
            dst_ref=dst,
            send_sem=send_sem.at[i_send],
            recv_sem=recv_sem.at[i_recv],
            device_id=dev,
            device_id_type=MESH,
        )

    barrier = pltpu.get_barrier_semaphore()
    greeted = [z_next, z_prev] + [(d, tpeer(k)) for k in range(1, TS)]
    fx_peers = [(4 * z + lax.rem(q + k, 4), t) for k in range(1, 4)]
    greeted = greeted + fx_peers
    for dev in greeted:
        pl.semaphore_signal(barrier, inc=1, device_id=dev, device_id_type=MESH)

    own_rows = pl.ds(pl.multiple_of(ROWS * c, 32), ROWS)
    other_rows = pl.ds(pl.multiple_of(ROWS * (1 - c), 32), ROWS)
    loads = [
        pltpu.make_async_copy(src, dst, load_sem.at[at])
        for at, (src, dst) in enumerate(
            [
                (feat_ref, feats.at[own_rows]),
                (up_ref, up_v),
                (down_ref, down_v),
                (head_ref, head_v),
                (vis_ref, vis_v),
            ]
        )
    ]
    for at in (L_UP, L_DOWN, L_FEAT, L_VIS, L_HEAD):
        loads[at].start()

    hidden = text_ref[...].astype(F32)
    lifted = layer_norm(hidden, ln_ref[...].reshape(1, D)).astype(BF16)
    loads[L_UP].wait()
    active = jax.nn.gelu(mm_t(lifted, up_v[...]), approximate=True).astype(BF16)
    loads[L_DOWN].wait()
    mixed = mm(active, down_v[...])
    for j in range(TS):
        mix_s[j] = mixed[TEXTS * j : TEXTS * (j + 1)].astype(BF16)

    pl.semaphore_wait(barrier, len(greeted))

    def exchange_start(src, dst, sem):
        for k in range(1, TS):
            rcopy(src.at[tpeer(k)], dst.at[t], sem + k, sem + t, (d, tpeer(k))).start()

    def exchange_wait(src, dst, sem):
        for k in range(1, TS):
            j = tpeer(k)
            rcopy(src.at[j], dst.at[t], sem + k, sem + t, (d, j)).wait_send()
            rcopy(src.at[j], dst.at[j], sem + k, sem + j, (d, j)).wait_recv()

    exchange_start(mix_s, mix_r, S_MIX)
    loads[L_FEAT].wait()
    feat_copy = rcopy(feats.at[own_rows], feats.at[own_rows], S_FEAT, S_FEAT, c_peer)
    feat_copy.start()
    mix_r[t] = jnp.zeros((TEXTS, D), BF16)
    with_hidden = mixed + hidden
    for j in range(TS):
        mix_f[j] = with_hidden[TEXTS * j : TEXTS * (j + 1)]

    loads[L_VIS].wait()
    feat_copy.wait_send()
    rcopy(feats.at[other_rows], feats.at[other_rows], S_FEAT, S_FEAT, c_peer).wait_recv()
    part_t[...] = mm_t(vis_v[...], feats[...])
    img_s[...] = part_t[pl.ds(pl.multiple_of(PIECE * c, 8), PIECE), :].astype(BF16)
    for k in range(1, TS):
        rcopy(img_s, img_r.at[c, t], S_IMG + k, S_IMG + t, (d, tpeer(k))).start()
    img_r[c, t] = img_s[...]

    exchange_wait(mix_s, mix_r, S_MIX)
    total = mix_f[t]
    for j in range(TS):
        total = total + mix_r[j].astype(F32)
    normed = layer_norm(total, fg_ref[...].reshape(1, D)).astype(BF16).astype(F32)
    for j in range(TS):
        nrm_s[j] = normed[:, COLS * j : COLS * (j + 1)].astype(BF16)
    exchange_start(nrm_s, nrm_r, S_NRM)
    nrm_r[t] = nrm_s[t]

    for k in range(1, TS):
        j = tpeer(k)
        rcopy(img_s, img_r.at[c, t], S_IMG + k, S_IMG + t, (d, j)).wait_send()
        rcopy(img_s, img_r.at[c, j], S_IMG + k, S_IMG + j, (d, j)).wait_recv()
    imgc_copy = rcopy(img_r.at[c], img_r.at[c], S_IMGC, S_IMGC, c_peer)
    imgc_copy.start()

    exchange_wait(nrm_s, nrm_r, S_NRM)
    for j in range(TS):
        nrm_a[TEXTS * j : TEXTS * (j + 1), :] = nrm_r[j].astype(F32)
    loads[L_HEAD].wait()
    head_part = mm(nrm_a[...].astype(BF16), head_v[...])
    for j in range(TS):
        head_f[j] = head_part[TEXTS * j : TEXTS * (j + 1)]
        head_s[j] = head_part[TEXTS * j : TEXTS * (j + 1)].astype(BF16)
    exchange_start(head_s, head_r, S_HEAD)
    head_r[t] = jnp.zeros((TEXTS, E), BF16)

    imgc_copy.wait_send()
    rcopy(img_r.at[1 - c], img_r.at[1 - c], S_IMGC, S_IMGC, c_peer).wait_recv()
    for j in range(TS):
        for h in range(2):
            at = COLS * j + PIECE * h
            img_f[at : at + PIECE, :] = img_r[h, j].astype(F32)
    emb_t = img_f[...]
    inverse = lax.rsqrt(jnp.sum(emb_t * emb_t, axis=0, keepdims=True) + norm_eps)
    inv_ref[...] = inverse
    unit_t = emb_t * inverse
    img_f[...] = unit_t
    img_ut[...] = unit_t.astype(BF16)
    img_u[...] = unit_t.T.astype(BF16)
    eg[...] = jnp.zeros_like(eg)

    exchange_wait(head_s, head_r, S_HEAD)
    text_emb = head_f[t]
    for j in range(TS):
        text_emb = text_emb + head_r[j].astype(F32)
    text_unit = text_emb * lax.rsqrt(
        jnp.sum(text_emb * text_emb, axis=1, keepdims=True) + norm_eps
    )
    texts[0, 0, 0] = text_unit.astype(BF16)

    def ag_copy(s, way, half):
        source = texts.at[0, 0, half] if isinstance(s, int) and s == 1 else texts.at[s - 1, way, half]
        sem = S_AG + 4 * (s - 1) + 2 * way + half
        return rcopy(source, texts.at[s, way, half], sem, sem, (z_next, z_prev)[way])

    yh_copy = rcopy(texts.at[0, 0, 0], texts.at[0, 0, 1], S_YH, S_YH, yh_peer)
    ag_copy(1, 0, 0).start()
    ag_copy(1, 1, 0).start()
    yh_copy.start()

    row_ids = lax.broadcasted_iota(jnp.int32, (CHUNK, IMGS), 0)
    col_ids = lax.broadcasted_iota(jnp.int32, (CHUNK, IMGS), 1)
    diagonal = ((row_ids < TEXTS) & (col_ids == row_ids + ROWS * c + TEXTS * t)).astype(F32)

    def process(s, pieces):
        rows = TEXTS * len(pieces)
        for at, (way, half) in enumerate(pieces):
            block_f[TEXTS * at : TEXTS * (at + 1), :] = texts[s, way, half].astype(F32)
        block = block_f[0:rows, :].astype(BF16)
        logits = logit_scale * mm(block, img_ut[...]) + logit_bias
        weights = jax.nn.sigmoid(logits)
        if isinstance(s, int) and s == 0:
            weights = weights - diagonal
        weights = (weights * (logit_scale / ROWS)).astype(BF16)
        eg[...] += lax.dot_general(
            block, weights, (((0,), (0,)), ((), ())), preferred_element_type=F32
        )
        grads[s, 0:rows, :] = mm(weights, img_u[...])

    yh_copy.wait()
    ag_copy(1, 0, 1).start()
    ag_copy(1, 1, 1).start()
    process(0, ((0, 0), (0, 1)))

    def ag_step(s, _):
        for half in range(2):
            for way in range(2):
                ag_copy(s, way, half).wait_recv()
                if half == way:
                    ag_copy(s + 1, way, half).start()
                else:

                    @pl.when(s < HALF - 1)
                    def _():
                        ag_copy(s + 1, way, half).start()

        process(s, ((0, 0), (0, 1), (1, 0), (1, 1)))
        return 0

    lax.fori_loop(1, HALF, ag_step, 0)

    def rs_copy(way, s, half):
        sem = S_RS + 4 * (s - 1) + 2 * way + half
        return rcopy(
            rs_s.at[way, s - 1, half], rs_r.at[way, s - 1, half], sem, sem, (z_next, z_prev)[way]
        )

    def rs_halves(way, s):
        return (way,) if s == 1 else (1, 0)

    def rs_step(way, s):
        for half in rs_halves(way, s):
            first = TEXTS * half if s == 1 else CHUNK * (1 - way) + TEXTS * half
            value = grads[HALF + 1 - s, first : first + TEXTS, :]
            if s > 1 and half in rs_halves(way, s - 1):
                rs_copy(way, s - 1, half).wait_recv()
                value = value + rs_r[way, s - 2, half].astype(F32)
            rs_s[way, s - 1, half] = value.astype(BF16)
            rs_copy(way, s, half).start()

    def rs_last(half):
        value = grads[0, TEXTS * half : TEXTS * (half + 1), :]
        for way in range(2):
            rs_copy(way, HALF, half).wait_recv()
            value = value + rs_r[way, HALF - 1, half].astype(F32)
        return value

    ag_copy(HALF, 0, 0).wait_recv()
    ag_copy(HALF, 1, 1).wait_recv()
    process(HALF, ((0, 0), (1, 1)))
    rs_step(0, 1)
    rs_step(1, 1)

    image_grad = eg[...]
    unit_t = img_f[...]
    radial = jnp.sum(unit_t * image_grad, axis=0, keepdims=True)
    eg[...] = (image_grad - unit_t * radial) * inv_ref[...]
    for j in range(TS):
        theirs = pl.ds(pl.multiple_of(COLS * j + PIECE * (1 - c), 8), PIECE)
        cx_s[j] = eg[theirs, :].astype(BF16)
    cx_copy = rcopy(cx_s, cx_r, S_CX, S_CX, c_peer)
    cx_copy.start()
    rs_step(1, 2)
    rs_step(0, 2)
    cx_copy.wait()
    for j in range(TS):
        mine = pl.ds(pl.multiple_of(COLS * j + PIECE * c, 8), PIECE)
        value = eg[mine, :] + cx_r[j].astype(F32)
        px_f[j] = value
        px_s[j] = value.astype(BF16)
    exchange_start(px_s, px_r, S_PX)
    px_r[t] = jnp.zeros((PIECE, IMGS), BF16)
    rs_step(1, 3)
    rs_step(0, 3)
    rs_step(1, 4)
    rs_step(0, 4)
    exchange_wait(px_s, px_r, S_PX)
    emb_grad = px_f[t]
    for j in range(TS):
        emb_grad = emb_grad + px_r[j].astype(F32)
    vg_all[...] = mm(emb_grad.astype(BF16), feats[...]).T

    def vr_copy(way, s):
        sem = (S_VRP, S_VRM)[way] + s - 1
        return rcopy(vr_s.at[way, s - 1], vr_r.at[way, s - 1], sem, sem, (z_next, z_prev)[way])

    def vg_chunk(owner):
        return vg_all[pl.ds(pl.multiple_of(ZROWS * owner, 8), ZROWS), :]

    def vr_step(way, s):
        owner = zmod(z + HALF + 1 - s) if way == 0 else zmod(z - HALF + s)
        value = vg_chunk(owner)
        if s > 1:
            vr_copy(way, s - 1).wait_recv()
            value = value + vr_r[way, s - 2]
        vr_s[way, s - 1] = value
        vr_copy(way, s).start()

    for s in range(1, HALF + 1):
        vr_step(0, s)
        if s < HALF:
            vr_step(1, s)
        r = s + 4
        if r <= HALF:
            rs_step(1, r)
            rs_step(0, r)
        if r == HALF + 1:
            yg_s[...] = rs_last(1)
            rcopy(yg_s, yg_r, S_YG, S_YG, yh_peer).start()

    own_grad = rs_last(0)
    rcopy(yg_s, yg_r, S_YG, S_YG, yh_peer).wait()
    tg_ref[...] = own_grad + yg_r[...]

    vr_copy(0, HALF).wait_recv()
    vr_copy(1, HALF - 1).wait_recv()
    fx[q] = vg_chunk(z) + vr_r[0, HALF - 1] + vr_r[1, HALF - 2]
    for k in range(1, 4):
        rcopy(fx.at[q], fx.at[q], S_FX + k, S_FX + q, fx_peers[k - 1]).start()

    for half in range(2):
        for way in range(2):
            ag_copy(1, way, half).wait_send()

    def ag_drain(s, _):
        for half in range(2):
            for way in range(2):
                if half == way:
                    ag_copy(s, way, half).wait_send()
                else:

                    @pl.when(s < HALF)
                    def _():
                        ag_copy(s, way, half).wait_send()

        return 0

    lax.fori_loop(2, HALF + 1, ag_drain, 0)
    for s in range(1, HALF + 1):
        for way in range(2):
            for half in rs_halves(way, s):
                rs_copy(way, s, half).wait_send()
            if s < HALF or way == 0:
                vr_copy(way, s).wait_send()

    for k in range(1, 4):
        o = lax.rem(q + k, 4)
        rcopy(fx.at[q], fx.at[q], S_FX + k, S_FX + q, fx_peers[k - 1]).wait_send()
        rcopy(fx.at[o], fx.at[o], S_FX + k, S_FX + o, fx_peers[k - 1]).wait_recv()
    left = fx[0] + fx[2]
    right = fx[1] + fx[3]
    for k in range(4):

        @pl.when(q == k)
        def _():
            vg_ref[:, 0:PIECE] = left[18 * k : 18 * (k + 1), :]
            vg_ref[:, PIECE:COLS] = right[18 * k : 18 * (k + 1), :]


def local(
    text_hidden,
    ln_gain,
    up_weight,
    down_weight,
    final_gain,
    head_weight,
    image_features,
    vision_weight,
):
    vmem = pl.BlockSpec(memory_space=pltpu.VMEM)
    hbm = pl.BlockSpec(memory_space=pl.ANY)
    scratch = [
        ((FF_DEV, D), BF16),
        ((FF_DEV, D), BF16),
        ((COLS, E), BF16),
        ((COLS, D), BF16),
        ((IMGS, D), BF16),
        ((COLS, IMGS), F32),
        ((PIECE, IMGS), BF16),
        ((2, TS, PIECE, IMGS), BF16),
        ((E, IMGS), F32),
        ((E, IMGS), BF16),
        ((IMGS, E), BF16),
        ((1, IMGS), F32),
        ((TS, TEXTS, D), BF16),
        ((TS, TEXTS, D), F32),
        ((TS, TEXTS, D), BF16),
        ((TS, TEXTS, COLS), BF16),
        ((TS, TEXTS, COLS), BF16),
        ((ROWS, COLS), F32),
        ((TS, TEXTS, E), BF16),
        ((TS, TEXTS, E), F32),
        ((TS, TEXTS, E), BF16),
        ((2 * CHUNK, E), F32),
        ((HALF + 1, 2, 2, TEXTS, E), BF16),
        ((HALF + 1, 2 * CHUNK, E), F32),
        ((E, IMGS), F32),
        ((2, HALF, 2, TEXTS, E), BF16),
        ((2, HALF, 2, TEXTS, E), BF16),
        ((TEXTS, E), F32),
        ((TEXTS, E), F32),
        ((TS, PIECE, IMGS), BF16),
        ((TS, PIECE, IMGS), BF16),
        ((TS, PIECE, IMGS), F32),
        ((TS, PIECE, IMGS), BF16),
        ((TS, PIECE, IMGS), BF16),
        ((D, PIECE), F32),
        ((2, HALF, ZROWS, PIECE), F32),
        ((2, HALF, ZROWS, PIECE), F32),
        ((4, ZROWS, PIECE), F32),
    ]
    return pl.pallas_call(
        kernel,
        out_shape=(
            jax.ShapeDtypeStruct((TEXTS, E), F32),
            jax.ShapeDtypeStruct((D // 64, COLS), F32),
        ),
        in_specs=[vmem, vmem, hbm, hbm, vmem, hbm, hbm, hbm],
        out_specs=(vmem, vmem),
        scratch_shapes=[pltpu.VMEM(shape, kind) for shape, kind in scratch]
        + [pltpu.SemaphoreType.DMA((size,)) for size in (S_ALL, S_ALL, 5)],
        compiler_params=pltpu.CompilerParams(
            collective_id=0, has_side_effects=True, vmem_limit_bytes=56 * 1024 * 1024
        ),
    )(
        text_hidden,
        ln_gain,
        up_weight.T,
        down_weight,
        final_gain,
        head_weight,
        image_features,
        vision_weight.T,
    )


def solution(mesh):
    placed = (
        P("dp", None),
        P(),
        P(None, "tensor"),
        P("tensor", None),
        P(),
        P("tensor", None),
        P("dp", None),
        P(None, "tensor"),
    )
    return jax.shard_map(
        local,
        mesh=mesh,
        in_specs=placed,
        out_specs=(P(("dp", "tensor"), None), P("dp", "tensor")),
        check_vma=False,
    )
```

```python
import functools

import jax
import jax.numpy as jnp
from jax import lax
from jax.experimental import pallas as pl
from jax.experimental.pallas import tpu as pltpu
from jax.sharding import PartitionSpec as P

logit_scale = 100.0
logit_bias = -4.0
norm_eps = 1e-06
MESH = pl.DeviceIdType.MESH
F32 = jnp.float32
BF16 = jnp.bfloat16

D = 1152
E = 1152
ROWS = 160
TS = 8
ZS = 16
HALF = ZS // 2
FF_DEV = 4304 // TS
TEXTS = ROWS // TS
CHUNK = 2 * TEXTS
IMGS = 384
PIECE = E // (2 * TS)
COLS = E // TS
WIDE = 128
ZROWS = D // ZS


def mm(a, b):
    return jnp.dot(a, b, preferred_element_type=F32)


def mm_t(a, b):
    return lax.dot_general(a, b, (((1,), (1,)), ((), ())), preferred_element_type=F32)


def layer_norm(values, gain_row):
    center = values - jnp.mean(values, axis=1, keepdims=True)
    spread = jnp.mean(center * center, axis=1, keepdims=True)
    return center * lax.rsqrt(spread + norm_eps) * gain_row


S_FEAT = 0
S_IMG = 1
S_IMGC = S_IMG + TS
S_MIX = S_IMGC + 1
S_NRM = S_MIX + TS
S_HEAD = S_NRM + TS
S_YH = S_HEAD + TS
S_AG = S_YH + 1
S_RS = S_AG + 4 * HALF
S_YG = S_RS + 4 * HALF
S_CX = S_YG + 1
S_PX = S_CX + TS
S_VRP = S_PX + TS
S_VRM = S_VRP + HALF
S_FX = S_VRM + HALF
S_ALL = S_FX + 4
L_FEAT, L_UP, L_DOWN, L_HEAD, L_VIS = range(5)


def kernel(
    text_ref,
    ln_ref,
    up_ref,
    down_ref,
    fg_ref,
    head_ref,
    feat_ref,
    vis_ref,
    tg_ref,
    vg_ref,
    up_v,
    down_v,
    head_v,
    vis_v,
    feats,
    part_t,
    img_s,
    img_r,
    img_f,
    img_ut,
    img_u,
    inv_ref,
    rad_ref,
    mix_s,
    mix_f,
    mix_r,
    nrm_s,
    nrm_r,
    nrm_a,
    head_s,
    head_f,
    head_r,
    block_f,
    texts,
    grads,
    eg,
    rs_s,
    rs_r,
    yg_s,
    yg_r,
    cx_s,
    cx_r,
    px_f,
    px_s,
    px_r,
    emb_b,
    vg_all,
    vr_s,
    vr_r,
    fx,
    send_sem,
    recv_sem,
    load_sem,
):
    d = lax.axis_index("dp")
    t = lax.axis_index("tensor")
    z = d // 4
    yh = (d // 2) % 2
    c = d % 2
    base = d - 4 * z
    z_next = (lax.rem(z + 1, ZS) * 4 + base, t)
    z_prev = (lax.rem(z + ZS - 1, ZS) * 4 + base, t)
    yh_peer = (d + 2 - 4 * yh, t)
    c_peer = (d + 1 - 2 * c, t)
    q = 2 * yh + c

    def zmod(v):
        return lax.rem(v + 2 * ZS, ZS)

    def tpeer(k):
        return lax.rem(t + k, TS)

    def rcopy(src, dst, i_send, i_recv, dev):
        return pltpu.make_async_remote_copy(
            src_ref=src,
            dst_ref=dst,
            send_sem=send_sem.at[i_send],
            recv_sem=recv_sem.at[i_recv],
            device_id=dev,
            device_id_type=MESH,
        )

    barrier = pltpu.get_barrier_semaphore()
    greeted = [z_next, z_prev] + [(d, tpeer(k)) for k in range(1, TS)]
    fx_peers = [(4 * z + lax.rem(q + k, 4), t) for k in range(1, 4)]
    greeted = greeted + fx_peers
    for dev in greeted:
        pl.semaphore_signal(barrier, inc=1, device_id=dev, device_id_type=MESH)

    own_rows = pl.ds(pl.multiple_of(ROWS * c, 32), ROWS)
    other_rows = pl.ds(pl.multiple_of(ROWS * (1 - c), 32), ROWS)
    feats[2 * ROWS : IMGS, :] = jnp.zeros((IMGS - 2 * ROWS, D), BF16)
    loads = [
        pltpu.make_async_copy(src, dst, load_sem.at[at])
        for at, (src, dst) in enumerate(
            [
                (feat_ref, feats.at[own_rows]),
                (up_ref, up_v),
                (down_ref, down_v),
                (head_ref, head_v),
                (vis_ref, vis_v),
            ]
        )
    ]
    for at in (L_UP, L_DOWN, L_FEAT, L_VIS, L_HEAD):
        loads[at].start()

    hidden = text_ref[...].astype(F32)
    lifted = layer_norm(hidden, ln_ref[...].reshape(1, D)).astype(BF16)
    loads[L_UP].wait()
    active = jax.nn.gelu(mm_t(lifted, up_v[...]), approximate=True).astype(BF16)
    loads[L_DOWN].wait()
    mixed = mm(active, down_v[...])
    for j in range(TS):
        mix_s[j] = mixed[TEXTS * j : TEXTS * (j + 1)].astype(BF16)

    pl.semaphore_wait(barrier, len(greeted))

    def exchange_start(src, dst, sem):
        for k in range(1, TS):
            rcopy(src.at[tpeer(k)], dst.at[t], sem + k, sem + t, (d, tpeer(k))).start()

    def exchange_wait(src, dst, sem):
        for k in range(1, TS):
            j = tpeer(k)
            rcopy(src.at[j], dst.at[t], sem + k, sem + t, (d, j)).wait_send()
            rcopy(src.at[j], dst.at[j], sem + k, sem + j, (d, j)).wait_recv()

    exchange_start(mix_s, mix_r, S_MIX)
    loads[L_FEAT].wait()
    feat_copy = rcopy(feats.at[own_rows], feats.at[own_rows], S_FEAT, S_FEAT, c_peer)
    feat_copy.start()
    mix_r[t] = jnp.zeros((TEXTS, D), BF16)
    with_hidden = mixed + hidden
    for j in range(TS):
        mix_f[j] = with_hidden[TEXTS * j : TEXTS * (j + 1)]

    loads[L_VIS].wait()
    feat_copy.wait_send()
    rcopy(feats.at[other_rows], feats.at[other_rows], S_FEAT, S_FEAT, c_peer).wait_recv()
    part_t[...] = mm_t(vis_v[...], feats[...])
    img_s[...] = part_t[pl.ds(pl.multiple_of(PIECE * c, 8), PIECE), :].astype(BF16)
    for k in range(1, TS):
        rcopy(img_s, img_r.at[c, t], S_IMG + k, S_IMG + t, (d, tpeer(k))).start()
    img_r[c, t] = img_s[...]

    exchange_wait(mix_s, mix_r, S_MIX)
    total = mix_f[t]
    for j in range(TS):
        total = total + mix_r[j].astype(F32)
    normed = layer_norm(total, fg_ref[...].reshape(1, D)).astype(BF16).astype(F32)
    for j in range(TS):
        nrm_s[j] = normed[:, COLS * j : COLS * (j + 1)].astype(BF16)
    exchange_start(nrm_s, nrm_r, S_NRM)
    nrm_r[t] = nrm_s[t]

    exchange_wait(nrm_s, nrm_r, S_NRM)
    for j in range(TS):
        nrm_a[TEXTS * j : TEXTS * (j + 1), :] = nrm_r[j].astype(F32)
    loads[L_HEAD].wait()
    head_part = mm(nrm_a[...].astype(BF16), head_v[...])
    for j in range(TS):
        head_f[j] = head_part[TEXTS * j : TEXTS * (j + 1)]
        head_s[j] = head_part[TEXTS * j : TEXTS * (j + 1)].astype(BF16)
    exchange_start(head_s, head_r, S_HEAD)
    head_r[t] = jnp.zeros((TEXTS, E), BF16)

    for k in range(1, TS):
        j = tpeer(k)
        rcopy(img_s, img_r.at[c, t], S_IMG + k, S_IMG + t, (d, j)).wait_send()
        rcopy(img_s, img_r.at[c, j], S_IMG + k, S_IMG + j, (d, j)).wait_recv()
    imgc_copy = rcopy(img_r.at[c], img_r.at[c], S_IMGC, S_IMGC, c_peer)
    imgc_copy.start()

    imgc_copy.wait_send()
    rcopy(img_r.at[1 - c], img_r.at[1 - c], S_IMGC, S_IMGC, c_peer).wait_recv()
    for j in range(TS):
        for h in range(2):
            at = COLS * j + PIECE * h
            img_f[at : at + PIECE, :] = img_r[h, j].astype(F32)
    emb_t = img_f[...]
    inverse = lax.rsqrt(jnp.sum(emb_t * emb_t, axis=0, keepdims=True) + norm_eps)
    inv_ref[...] = inverse
    unit_t = emb_t * inverse
    img_f[...] = unit_t
    img_ut[...] = unit_t.astype(BF16)

    exchange_wait(head_s, head_r, S_HEAD)
    text_emb = head_f[t]
    for j in range(TS):
        text_emb = text_emb + head_r[j].astype(F32)
    text_unit = text_emb * lax.rsqrt(
        jnp.sum(text_emb * text_emb, axis=1, keepdims=True) + norm_eps
    )
    texts[0, 0, 0] = text_unit.astype(BF16)

    def ag_copy(s, way, half):
        source = texts.at[0, 0, half] if isinstance(s, int) and s == 1 else texts.at[s - 1, way, half]
        sem = S_AG + 4 * (s - 1) + 2 * way + half
        return rcopy(source, texts.at[s, way, half], sem, sem, (z_next, z_prev)[way])

    yh_copy = rcopy(texts.at[0, 0, 0], texts.at[0, 0, 1], S_YH, S_YH, yh_peer)
    ag_copy(1, 0, 0).start()
    ag_copy(1, 1, 0).start()
    yh_copy.start()

    row_ids = lax.broadcasted_iota(jnp.int32, (CHUNK, IMGS), 0)
    col_ids = lax.broadcasted_iota(jnp.int32, (CHUNK, IMGS), 1)
    diagonal = ((row_ids < TEXTS) & (col_ids == row_ids + ROWS * c + TEXTS * t)).astype(F32)

    def process(s, pieces):
        rows = TEXTS * len(pieces)
        for at, (way, half) in enumerate(pieces):
            block_f[TEXTS * at : TEXTS * (at + 1), :] = texts[s, way, half].astype(F32)
        block = block_f[0:rows, :].astype(BF16)
        dots = mm(block, img_ut[...])
        weights = jax.nn.sigmoid(logit_scale * dots + logit_bias)
        if isinstance(s, int) and s == 0:
            weights = weights - diagonal
        weights = (weights * (logit_scale / ROWS)).astype(BF16)
        radial = jnp.sum(weights.astype(F32) * dots, axis=0, keepdims=True)
        terms = lax.dot_general(
            block, weights, (((0,), (0,)), ((), ())), preferred_element_type=F32
        )
        if isinstance(s, int) and s == 0:
            rad_ref[...] = radial
            eg[...] = terms
        else:
            rad_ref[...] += radial
            eg[...] += terms
        grads[s, 0:rows, :] = mm(weights, img_u[...])

    img_u[...] = img_f[...].T.astype(BF16)
    yh_copy.wait()
    ag_copy(1, 0, 1).start()
    ag_copy(1, 1, 1).start()
    process(0, ((0, 0), (0, 1)))

    def ag_step(s, _):
        for half in range(2):
            for way in range(2):
                ag_copy(s, way, half).wait_recv()
                if half == way:
                    ag_copy(s + 1, way, half).start()
                else:

                    @pl.when(s < HALF - 1)
                    def _():
                        ag_copy(s + 1, way, half).start()

        process(s, ((0, 0), (0, 1), (1, 0), (1, 1)))
        return 0

    lax.fori_loop(1, HALF, ag_step, 0)

    def rs_copy(way, s, half):
        sem = S_RS + 4 * (s - 1) + 2 * way + half
        return rcopy(
            rs_s.at[way, s - 1, half], rs_r.at[way, s - 1, half], sem, sem, (z_next, z_prev)[way]
        )

    def rs_halves(way, s):
        return (way,) if s == 1 else (1, 0)

    def rs_step(way, s):
        for half in rs_halves(way, s):
            first = TEXTS * half if s == 1 else CHUNK * (1 - way) + TEXTS * half
            value = grads[HALF + 1 - s, first : first + TEXTS, :]
            if s > 1 and half in rs_halves(way, s - 1):
                rs_copy(way, s - 1, half).wait_recv()
                value = value + rs_r[way, s - 2, half].astype(F32)
            rs_s[way, s - 1, half] = value.astype(BF16)
            rs_copy(way, s, half).start()

    def rs_last(half):
        value = grads[0, TEXTS * half : TEXTS * (half + 1), :]
        for way in range(2):
            rs_copy(way, HALF, half).wait_recv()
            value = value + rs_r[way, HALF - 1, half].astype(F32)
        return value

    ag_copy(HALF, 0, 0).wait_recv()
    ag_copy(HALF, 1, 1).wait_recv()
    process(HALF, ((0, 0), (1, 1)))
    rs_step(0, 1)
    rs_step(1, 1)

    radial = rad_ref[...]
    inverse = inv_ref[...]

    def emb_piece(j, half):
        rows = pl.ds(pl.multiple_of(COLS * j + PIECE * half, 8), PIECE)
        return (eg[rows, :] - img_f[rows, :] * radial) * inverse

    def cx_copy(k):
        j = tpeer(k)
        return rcopy(cx_s.at[j], cx_r.at[j], S_CX + k % TS, S_CX + k % TS, c_peer)

    for k in range(1, TS + 1):
        cx_s[tpeer(k)] = emb_piece(tpeer(k), 1 - c).astype(BF16)
        cx_copy(k).start()
    for k in range(1, TS + 1):
        j = tpeer(k)
        value = emb_piece(j, c)
        cx_copy(k).wait()
        value = value + cx_r[j].astype(F32)
        if k < TS:
            px_s[j] = value.astype(BF16)
            rcopy(px_s.at[j], px_r.at[t], S_PX + k, S_PX + t, (d, j)).start()
        else:
            px_f[...] = value
    px_r[t] = jnp.zeros((PIECE, IMGS), BF16)
    emb_b[PIECE:WIDE, :] = jnp.zeros((WIDE - PIECE, IMGS), F32)
    for s in range(2, 5):
        rs_step(1, s)
        rs_step(0, s)
    exchange_wait(px_s, px_r, S_PX)
    emb_grad = px_f[...]
    for j in range(TS):
        emb_grad = emb_grad + px_r[j].astype(F32)
    emb_b[0:PIECE, :] = emb_grad
    vg_all[...] = mm(emb_b[...].astype(BF16), feats[...]).T

    def vr_copy(way, s):
        sem = (S_VRP, S_VRM)[way] + s - 1
        return rcopy(vr_s.at[way, s - 1], vr_r.at[way, s - 1], sem, sem, (z_next, z_prev)[way])

    def vg_chunk(owner):
        return vg_all[pl.ds(pl.multiple_of(ZROWS * owner, 8), ZROWS), :]

    def vr_step(way, s):
        owner = zmod(z + HALF + 1 - s) if way == 0 else zmod(z - HALF + s)
        value = vg_chunk(owner)
        if s > 1:
            vr_copy(way, s - 1).wait_recv()
            value = value + vr_r[way, s - 2]
        vr_s[way, s - 1] = value
        vr_copy(way, s).start()

    for s in range(1, HALF + 1):
        vr_step(0, s)
        if s < HALF:
            vr_step(1, s)
        r = s + 4
        if r <= HALF:
            rs_step(1, r)
            rs_step(0, r)
        if r == HALF + 1:
            yg_s[...] = rs_last(1)
            rcopy(yg_s, yg_r, S_YG, S_YG, yh_peer).start()

    own_grad = rs_last(0)
    rcopy(yg_s, yg_r, S_YG, S_YG, yh_peer).wait()
    tg_ref[...] = own_grad + yg_r[...]

    vr_copy(0, HALF).wait_recv()
    vr_copy(1, HALF - 1).wait_recv()
    fx[q] = vg_chunk(z) + vr_r[0, HALF - 1] + vr_r[1, HALF - 2]
    for k in range(1, 4):
        rcopy(fx.at[q], fx.at[q], S_FX + k, S_FX + q, fx_peers[k - 1]).start()

    for half in range(2):
        for way in range(2):
            ag_copy(1, way, half).wait_send()

    def ag_drain(s, _):
        for half in range(2):
            for way in range(2):
                if half == way:
                    ag_copy(s, way, half).wait_send()
                else:

                    @pl.when(s < HALF)
                    def _():
                        ag_copy(s, way, half).wait_send()

        return 0

    lax.fori_loop(2, HALF + 1, ag_drain, 0)
    for s in range(1, HALF + 1):
        for way in range(2):
            for half in rs_halves(way, s):
                rs_copy(way, s, half).wait_send()
            if s < HALF or way == 0:
                vr_copy(way, s).wait_send()

    for k in range(1, 4):
        o = lax.rem(q + k, 4)
        rcopy(fx.at[q], fx.at[q], S_FX + k, S_FX + q, fx_peers[k - 1]).wait_send()
        rcopy(fx.at[o], fx.at[o], S_FX + k, S_FX + o, fx_peers[k - 1]).wait_recv()
    left = fx[0] + fx[2]
    right = fx[1] + fx[3]
    for k in range(4):

        @pl.when(q == k)
        def _():
            vg_ref[:, 0:PIECE] = left[18 * k : 18 * (k + 1), 0:PIECE]
            vg_ref[:, PIECE:COLS] = right[18 * k : 18 * (k + 1), 0:PIECE]


def hand_over(tg_in, vg_in, tg_out, vg_out, sem):
    copies = [
        pltpu.make_async_copy(tg_in, tg_out, sem.at[0]),
        pltpu.make_async_copy(vg_in, vg_out, sem.at[1]),
    ]
    for copy in copies:
        copy.start()
    for copy in copies:
        copy.wait()


def local(
    text_hidden,
    ln_gain,
    up_weight,
    down_weight,
    final_gain,
    head_weight,
    image_features,
    vision_weight,
):
    vmem = pl.BlockSpec(memory_space=pltpu.VMEM)
    hbm = pl.BlockSpec(memory_space=pl.ANY)
    scratch = [
        ((FF_DEV, D), BF16),
        ((FF_DEV, D), BF16),
        ((COLS, E), BF16),
        ((COLS, D), BF16),
        ((IMGS, D), BF16),
        ((COLS, IMGS), F32),
        ((PIECE, IMGS), BF16),
        ((2, TS, PIECE, IMGS), BF16),
        ((E, IMGS), F32),
        ((E, IMGS), BF16),
        ((IMGS, E), BF16),
        ((1, IMGS), F32),
        ((1, IMGS), F32),
        ((TS, TEXTS, D), BF16),
        ((TS, TEXTS, D), F32),
        ((TS, TEXTS, D), BF16),
        ((TS, TEXTS, COLS), BF16),
        ((TS, TEXTS, COLS), BF16),
        ((ROWS, COLS), F32),
        ((TS, TEXTS, E), BF16),
        ((TS, TEXTS, E), F32),
        ((TS, TEXTS, E), BF16),
        ((2 * CHUNK, E), F32),
        ((HALF + 1, 2, 2, TEXTS, E), BF16),
        ((HALF + 1, 2 * CHUNK, E), F32),
        ((E, IMGS), F32),
        ((2, HALF, 2, TEXTS, E), BF16),
        ((2, HALF, 2, TEXTS, E), BF16),
        ((TEXTS, E), F32),
        ((TEXTS, E), F32),
        ((TS, PIECE, IMGS), BF16),
        ((TS, PIECE, IMGS), BF16),
        ((PIECE, IMGS), F32),
        ((TS, PIECE, IMGS), BF16),
        ((TS, PIECE, IMGS), BF16),
        ((WIDE, IMGS), F32),
        ((D, WIDE), F32),
        ((2, HALF, ZROWS, WIDE), F32),
        ((2, HALF, ZROWS, WIDE), F32),
        ((4, ZROWS, WIDE), F32),
    ]
    results = pl.pallas_call(
        kernel,
        out_shape=(
            jax.ShapeDtypeStruct((TEXTS, E), F32),
            jax.ShapeDtypeStruct((D // 64, COLS), F32),
        ),
        in_specs=[vmem, vmem, hbm, hbm, vmem, hbm, hbm, hbm],
        out_specs=(vmem, vmem),
        scratch_shapes=[pltpu.VMEM(shape, kind) for shape, kind in scratch]
        + [pltpu.SemaphoreType.DMA((size,)) for size in (S_ALL, S_ALL, 5)],
        compiler_params=pltpu.CompilerParams(
            collective_id=0, has_side_effects=True, vmem_limit_bytes=56 * 1024 * 1024
        ),
    )(
        text_hidden,
        ln_gain,
        up_weight.T,
        down_weight,
        final_gain,
        head_weight,
        image_features,
        vision_weight.T,
    )
    return pl.pallas_call(
        hand_over,
        out_shape=tuple(jax.ShapeDtypeStruct(r.shape, F32) for r in results),
        in_specs=[hbm] * 2,
        out_specs=(hbm, hbm),
        scratch_shapes=[pltpu.SemaphoreType.DMA((2,))],
        compiler_params=pltpu.CompilerParams(vmem_limit_bytes=60 * 1024 * 1024),
    )(*results)


def solution(mesh):
    placed = (
        P("dp", None),
        P(),
        P(None, "tensor"),
        P("tensor", None),
        P(),
        P("tensor", None),
        P("dp", None),
        P(None, "tensor"),
    )
    return jax.shard_map(
        local,
        mesh=mesh,
        in_specs=placed,
        out_specs=(P(("dp", "tensor"), None), P("dp", "tensor")),
        check_vma=False,
    )
```

```python
import functools

import jax
import jax.numpy as jnp
from jax import lax
from jax.experimental import pallas as pl
from jax.experimental.pallas import tpu as pltpu
from jax.sharding import PartitionSpec as P

logit_scale = 100.0
logit_bias = -4.0
norm_eps = 1e-06
MESH = pl.DeviceIdType.MESH
F32 = jnp.float32
BF16 = jnp.bfloat16

D = 1152
E = 1152
ROWS = 160
TS = 8
ZS = 16
HALF = ZS // 2
FF_DEV = 4304 // TS
TEXTS = ROWS // TS
CHUNK = 2 * TEXTS
IMGS = 384
PIECE = E // (2 * TS)
COLS = E // TS
WIDE = 128
ZROWS = D // ZS


def mm(a, b):
    return jnp.dot(a, b, preferred_element_type=F32)


def mm_t(a, b):
    return lax.dot_general(a, b, (((1,), (1,)), ((), ())), preferred_element_type=F32)


def layer_norm(values, gain_row):
    center = values - jnp.mean(values, axis=1, keepdims=True)
    spread = jnp.mean(center * center, axis=1, keepdims=True)
    return center * lax.rsqrt(spread + norm_eps) * gain_row


S_FEAT = 0
S_IMG = 1
S_IMGC = S_IMG + TS
S_MIX = S_IMGC + 1
S_NRM = S_MIX + TS
S_HEAD = S_NRM + TS
S_YH = S_HEAD + TS
S_AG = S_YH + 1
S_RS = S_AG + 4 * HALF
S_GY = S_RS + 2 * HALF
S_CX = S_GY + 2 * HALF + 2
S_PX = S_CX + TS
S_VRP = S_PX + TS
S_VRM = S_VRP + HALF
S_FX = S_VRM + HALF
S_ALL = S_FX + 4
L_FEAT, L_UP, L_DOWN, L_HEAD, L_VIS = range(5)


def kernel(
    text_ref,
    ln_ref,
    up_ref,
    down_ref,
    fg_ref,
    head_ref,
    feat_ref,
    vis_ref,
    tg_ref,
    vg_ref,
    up_v,
    down_v,
    head_v,
    vis_v,
    feats,
    part_t,
    img_s,
    img_r,
    img_f,
    img_ut,
    img_u,
    inv_ref,
    rad_ref,
    mix_s,
    mix_f,
    mix_r,
    nrm_s,
    nrm_r,
    nrm_a,
    head_s,
    head_f,
    head_r,
    block_f,
    texts,
    grads,
    eg,
    rs_s,
    rs_r,
    gy_s,
    gy_r,
    cx_s,
    cx_r,
    px_f,
    px_s,
    px_r,
    emb_b,
    vg_all,
    vr_s,
    vr_r,
    fx,
    send_sem,
    recv_sem,
    load_sem,
):
    d = lax.axis_index("dp")
    t = lax.axis_index("tensor")
    z = d // 4
    yh = (d // 2) % 2
    c = d % 2
    base = d - 4 * z
    z_next = (lax.rem(z + 1, ZS) * 4 + base, t)
    z_prev = (lax.rem(z + ZS - 1, ZS) * 4 + base, t)
    yh_peer = (d + 2 - 4 * yh, t)
    c_peer = (d + 1 - 2 * c, t)
    q = 2 * yh + c

    def zmod(v):
        return lax.rem(v + 2 * ZS, ZS)

    def tpeer(k):
        return lax.rem(t + k, TS)

    def rcopy(src, dst, i_send, i_recv, dev):
        return pltpu.make_async_remote_copy(
            src_ref=src,
            dst_ref=dst,
            send_sem=send_sem.at[i_send],
            recv_sem=recv_sem.at[i_recv],
            device_id=dev,
            device_id_type=MESH,
        )

    barrier = pltpu.get_barrier_semaphore()
    greeted = [z_next, z_prev] + [(d, tpeer(k)) for k in range(1, TS)]
    fx_peers = [(4 * z + lax.rem(q + k, 4), t) for k in range(1, 4)]
    greeted = greeted + fx_peers
    for dev in greeted:
        pl.semaphore_signal(barrier, inc=1, device_id=dev, device_id_type=MESH)

    own_rows = pl.ds(pl.multiple_of(ROWS * c, 32), ROWS)
    other_rows = pl.ds(pl.multiple_of(ROWS * (1 - c), 32), ROWS)
    feats[2 * ROWS : IMGS, :] = jnp.zeros((IMGS - 2 * ROWS, D), BF16)
    loads = [
        pltpu.make_async_copy(src, dst, load_sem.at[at])
        for at, (src, dst) in enumerate(
            [
                (feat_ref, feats.at[own_rows]),
                (up_ref, up_v),
                (down_ref, down_v),
                (head_ref, head_v),
                (vis_ref, vis_v),
            ]
        )
    ]
    for at in (L_UP, L_DOWN, L_FEAT, L_VIS, L_HEAD):
        loads[at].start()

    hidden = text_ref[...].astype(F32)
    lifted = layer_norm(hidden, ln_ref[...].reshape(1, D)).astype(BF16)
    loads[L_UP].wait()
    active = jax.nn.gelu(mm_t(lifted, up_v[...]), approximate=True).astype(BF16)
    loads[L_DOWN].wait()
    mixed = mm(active, down_v[...])
    for j in range(TS):
        mix_s[j] = mixed[TEXTS * j : TEXTS * (j + 1)].astype(BF16)

    pl.semaphore_wait(barrier, len(greeted))

    def exchange_start(src, dst, sem):
        for k in range(1, TS):
            rcopy(src.at[tpeer(k)], dst.at[t], sem + k, sem + t, (d, tpeer(k))).start()

    def exchange_wait(src, dst, sem):
        for k in range(1, TS):
            j = tpeer(k)
            rcopy(src.at[j], dst.at[t], sem + k, sem + t, (d, j)).wait_send()
            rcopy(src.at[j], dst.at[j], sem + k, sem + j, (d, j)).wait_recv()

    exchange_start(mix_s, mix_r, S_MIX)
    loads[L_FEAT].wait()
    feat_copy = rcopy(feats.at[own_rows], feats.at[own_rows], S_FEAT, S_FEAT, c_peer)
    feat_copy.start()
    mix_r[t] = jnp.zeros((TEXTS, D), BF16)
    with_hidden = mixed + hidden
    for j in range(TS):
        mix_f[j] = with_hidden[TEXTS * j : TEXTS * (j + 1)]

    loads[L_VIS].wait()
    feat_copy.wait_send()
    rcopy(feats.at[other_rows], feats.at[other_rows], S_FEAT, S_FEAT, c_peer).wait_recv()
    part_t[...] = mm_t(vis_v[...], feats[...])
    img_s[...] = part_t[pl.ds(pl.multiple_of(PIECE * c, 8), PIECE), :].astype(BF16)
    for k in range(1, TS):
        rcopy(img_s, img_r.at[c, t], S_IMG + k, S_IMG + t, (d, tpeer(k))).start()
    img_r[c, t] = img_s[...]

    exchange_wait(mix_s, mix_r, S_MIX)
    total = mix_f[t]
    for j in range(TS):
        total = total + mix_r[j].astype(F32)
    normed = layer_norm(total, fg_ref[...].reshape(1, D)).astype(BF16).astype(F32)
    for j in range(TS):
        nrm_s[j] = normed[:, COLS * j : COLS * (j + 1)].astype(BF16)
    exchange_start(nrm_s, nrm_r, S_NRM)
    nrm_r[t] = nrm_s[t]

    exchange_wait(nrm_s, nrm_r, S_NRM)
    for j in range(TS):
        nrm_a[TEXTS * j : TEXTS * (j + 1), :] = nrm_r[j].astype(F32)
    loads[L_HEAD].wait()
    head_part = mm(nrm_a[...].astype(BF16), head_v[...])
    for j in range(TS):
        head_f[j] = head_part[TEXTS * j : TEXTS * (j + 1)]
        head_s[j] = head_part[TEXTS * j : TEXTS * (j + 1)].astype(BF16)
    exchange_start(head_s, head_r, S_HEAD)
    head_r[t] = jnp.zeros((TEXTS, E), BF16)

    for k in range(1, TS):
        j = tpeer(k)
        rcopy(img_s, img_r.at[c, t], S_IMG + k, S_IMG + t, (d, j)).wait_send()
        rcopy(img_s, img_r.at[c, j], S_IMG + k, S_IMG + j, (d, j)).wait_recv()
    imgc_copy = rcopy(img_r.at[c], img_r.at[c], S_IMGC, S_IMGC, c_peer)
    imgc_copy.start()

    imgc_copy.wait_send()
    rcopy(img_r.at[1 - c], img_r.at[1 - c], S_IMGC, S_IMGC, c_peer).wait_recv()
    for j in range(TS):
        for h in range(2):
            at = COLS * j + PIECE * h
            img_f[at : at + PIECE, :] = img_r[h, j].astype(F32)
    emb_t = img_f[...]
    inverse = lax.rsqrt(jnp.sum(emb_t * emb_t, axis=0, keepdims=True) + norm_eps)
    inv_ref[...] = inverse
    unit_t = emb_t * inverse
    img_f[...] = unit_t
    img_ut[...] = unit_t.astype(BF16)

    exchange_wait(head_s, head_r, S_HEAD)
    text_emb = head_f[t]
    for j in range(TS):
        text_emb = text_emb + head_r[j].astype(F32)
    text_unit = text_emb * lax.rsqrt(
        jnp.sum(text_emb * text_emb, axis=1, keepdims=True) + norm_eps
    )
    texts[0, 0, 0] = text_unit.astype(BF16)

    def is_first(s):
        return isinstance(s, int) and s == 1

    def ag_copy(s, way, half):
        source = texts.at[0, 0, half] if is_first(s) else texts.at[s - 1, way, half]
        sem = S_AG + 4 * (s - 1) + 2 * way + half
        return rcopy(source, texts.at[s, way, half], sem, sem, (z_next, z_prev)[way])

    yh_copy = rcopy(texts.at[0, 0, 0], texts.at[0, 0, 1], S_YH, S_YH, yh_peer)
    ag_copy(1, 0, 0).start()
    ag_copy(1, 1, 0).start()
    yh_copy.start()

    row_ids = lax.broadcasted_iota(jnp.int32, (CHUNK, IMGS), 0)
    col_ids = lax.broadcasted_iota(jnp.int32, (CHUNK, IMGS), 1)
    diagonal = ((row_ids < TEXTS) & (col_ids == row_ids + ROWS * c + TEXTS * t)).astype(F32)

    def gy_copy(s, way):
        sem = S_GY + 2 * s + way
        return rcopy(gy_s.at[s, way], gy_r.at[s, way], sem, sem, yh_peer)

    own_pieces = ((0, 0), (0, 1))
    far_pieces = ((0, 0), (1, 1))
    pair_pieces = ((0, 0), (0, 1), (1, 0), (1, 1))

    def weigh(s, pieces):
        rows = TEXTS * len(pieces)
        for at, (way, half) in enumerate(pieces):
            block_f[TEXTS * at : TEXTS * (at + 1), :] = texts[s, way, half].astype(F32)
        block = block_f[0:rows, :].astype(BF16)
        dots = mm(block, img_ut[...])
        weights = jax.nn.sigmoid(logit_scale * dots + logit_bias)
        if pieces is own_pieces:
            weights = weights - diagonal
        weights = (weights * (logit_scale / ROWS)).astype(BF16)
        radial = jnp.sum(weights.astype(F32) * dots, axis=0, keepdims=True)
        terms = lax.dot_general(
            block, weights, (((0,), (0,)), ((), ())), preferred_element_type=F32
        )
        if pieces is own_pieces:
            rad_ref[...] = radial
            eg[...] = terms
        else:
            rad_ref[...] += radial
            eg[...] += terms
        return weights

    def text_terms(s, pieces, weights):
        terms = mm(weights, img_u[...])
        for at, (way, half) in enumerate(pieces):
            part = terms[TEXTS * at : TEXTS * (at + 1)]
            slot = way if pieces is pair_pieces else 0
            if half == 0:
                grads[s, slot] = part
            else:
                gy_s[s, slot] = part.astype(BF16)
                gy_copy(s, slot).start()

    def forward(s, half):
        for way in range(2):
            ag_copy(s, way, half).wait_recv()
            if half == way:
                ag_copy(s + 1, way, half).start()
            else:

                @pl.when(s < HALF - 1)
                def _():
                    ag_copy(s + 1, way, half).start()

    yh_copy.wait()
    ag_copy(1, 0, 1).start()
    ag_copy(1, 1, 1).start()
    img_u[...] = img_f[...].T.astype(BF16)
    first_step = jnp.int32(1)
    forward(first_step, 0)
    own_weights = weigh(0, own_pieces)
    forward(first_step, 1)
    text_terms(0, own_pieces, own_weights)

    def ag_step(s, _):
        forward(s, 0)
        weights = weigh(s - 1, pair_pieces)
        forward(s, 1)
        text_terms(s - 1, pair_pieces, weights)
        return 0

    lax.fori_loop(2, HALF, ag_step, 0)
    text_terms(HALF - 1, pair_pieces, weigh(HALF - 1, pair_pieces))

    def rs_copy(way, s):
        sem = S_RS + 2 * (s - 1) + way
        return rcopy(rs_s.at[way, s - 1], rs_r.at[way, s - 1], sem, sem, (z_next, z_prev)[way])

    def rs_first(way):
        return 1 + way

    def rs_step(way, s):
        left = HALF + 1 - s
        slot = 0 if s == 1 else 1 - way
        gy_copy(left, slot).wait_recv()
        value = grads[left, slot] + gy_r[left, slot].astype(F32)
        if s > rs_first(way):
            rs_copy(way, s - 1).wait_recv()
            value = value + rs_r[way, s - 2].astype(F32)
        rs_s[way, s - 1] = value.astype(BF16)
        rs_copy(way, s).start()

    ag_copy(HALF, 0, 0).wait_recv()
    ag_copy(HALF, 1, 1).wait_recv()
    text_terms(HALF, far_pieces, weigh(HALF, far_pieces))

    radial = rad_ref[...]
    inverse = inv_ref[...]

    def emb_piece(j, half):
        rows = pl.ds(pl.multiple_of(COLS * j + PIECE * half, 8), PIECE)
        return (eg[rows, :] - img_f[rows, :] * radial) * inverse

    def cx_copy(k):
        j = tpeer(k)
        return rcopy(cx_s.at[j], cx_r.at[j], S_CX + k % TS, S_CX + k % TS, c_peer)

    for k in range(1, TS + 1):
        cx_s[tpeer(k)] = emb_piece(tpeer(k), 1 - c).astype(BF16)
        cx_copy(k).start()
    rs_step(0, 1)
    rs_step(1, 2)
    for k in range(1, TS + 1):
        j = tpeer(k)
        value = emb_piece(j, c)
        cx_copy(k).wait()
        value = value + cx_r[j].astype(F32)
        if k < TS:
            px_s[j] = value.astype(BF16)
            rcopy(px_s.at[j], px_r.at[t], S_PX + k, S_PX + t, (d, j)).start()
        else:
            px_f[...] = value
    px_r[t] = jnp.zeros((PIECE, IMGS), BF16)
    emb_b[PIECE:WIDE, :] = jnp.zeros((WIDE - PIECE, IMGS), F32)
    for s in range(2, 4):
        rs_step(0, s)
        rs_step(1, s + 1)
    exchange_wait(px_s, px_r, S_PX)
    emb_grad = px_f[...]
    for j in range(TS):
        emb_grad = emb_grad + px_r[j].astype(F32)
    emb_b[0:PIECE, :] = emb_grad
    vg_all[...] = mm(emb_b[...].astype(BF16), feats[...]).T

    def vr_copy(way, s):
        sem = (S_VRP, S_VRM)[way] + s - 1
        return rcopy(vr_s.at[way, s - 1], vr_r.at[way, s - 1], sem, sem, (z_next, z_prev)[way])

    def vg_chunk(owner):
        return vg_all[pl.ds(pl.multiple_of(ZROWS * owner, 8), ZROWS), :]

    def vr_step(way, s):
        owner = zmod(z + HALF + 1 - s) if way == 0 else zmod(z - HALF + s)
        value = vg_chunk(owner)
        if s > 1:
            vr_copy(way, s - 1).wait_recv()
            value = value + vr_r[way, s - 2]
        vr_s[way, s - 1] = value
        vr_copy(way, s).start()

    for s in range(1, HALF + 1):
        vr_step(0, s)
        if s < HALF:
            vr_step(1, s)
        if s + 3 <= HALF:
            rs_step(0, s + 3)
        if s + 4 <= HALF:
            rs_step(1, s + 4)
        if s == HALF - 2:
            gy_copy(0, 0).wait_recv()
            rs_copy(0, HALF).wait_recv()
            rs_copy(1, HALF).wait_recv()
            tg_ref[...] = (
                grads[0, 0]
                + gy_r[0, 0].astype(F32)
                + rs_r[0, HALF - 1].astype(F32)
                + rs_r[1, HALF - 1].astype(F32)
            )

    vr_copy(0, HALF).wait_recv()
    vr_copy(1, HALF - 1).wait_recv()
    fx[q] = vg_chunk(z) + vr_r[0, HALF - 1] + vr_r[1, HALF - 2]
    for k in range(1, 4):
        rcopy(fx.at[q], fx.at[q], S_FX + k, S_FX + q, fx_peers[k - 1]).start()

    for half in range(2):
        for way in range(2):
            ag_copy(1, way, half).wait_send()

    def ag_drain(s, _):
        for half in range(2):
            for way in range(2):
                if half == way:
                    ag_copy(s, way, half).wait_send()
                else:

                    @pl.when(s < HALF)
                    def _():
                        ag_copy(s, way, half).wait_send()

        return 0

    lax.fori_loop(2, HALF + 1, ag_drain, 0)

    def gy_drain(s, _):
        gy_copy(s, 0).wait_send()
        gy_copy(s, 1).wait_send()
        return 0

    gy_copy(0, 0).wait_send()
    lax.fori_loop(1, HALF, gy_drain, 0)
    gy_copy(HALF, 0).wait_send()
    for s in range(1, HALF + 1):
        for way in range(2):
            if s >= rs_first(way):
                rs_copy(way, s).wait_send()
            if s < HALF or way == 0:
                vr_copy(way, s).wait_send()

    for k in range(1, 4):
        o = lax.rem(q + k, 4)
        rcopy(fx.at[q], fx.at[q], S_FX + k, S_FX + q, fx_peers[k - 1]).wait_send()
        rcopy(fx.at[o], fx.at[o], S_FX + k, S_FX + o, fx_peers[k - 1]).wait_recv()
    left = fx[0] + fx[2]
    right = fx[1] + fx[3]
    for k in range(4):

        @pl.when(q == k)
        def _():
            vg_ref[:, 0:PIECE] = left[18 * k : 18 * (k + 1), 0:PIECE]
            vg_ref[:, PIECE:COLS] = right[18 * k : 18 * (k + 1), 0:PIECE]


def local(
    text_hidden,
    ln_gain,
    up_weight,
    down_weight,
    final_gain,
    head_weight,
    image_features,
    vision_weight,
):
    vmem = pl.BlockSpec(memory_space=pltpu.VMEM)
    hbm = pl.BlockSpec(memory_space=pl.ANY)
    scratch = [
        ((FF_DEV, D), BF16),
        ((FF_DEV, D), BF16),
        ((COLS, E), BF16),
        ((COLS, D), BF16),
        ((IMGS, D), BF16),
        ((COLS, IMGS), F32),
        ((PIECE, IMGS), BF16),
        ((2, TS, PIECE, IMGS), BF16),
        ((E, IMGS), F32),
        ((E, IMGS), BF16),
        ((IMGS, E), BF16),
        ((1, IMGS), F32),
        ((1, IMGS), F32),
        ((TS, TEXTS, D), BF16),
        ((TS, TEXTS, D), F32),
        ((TS, TEXTS, D), BF16),
        ((TS, TEXTS, COLS), BF16),
        ((TS, TEXTS, COLS), BF16),
        ((ROWS, COLS), F32),
        ((TS, TEXTS, E), BF16),
        ((TS, TEXTS, E), F32),
        ((TS, TEXTS, E), BF16),
        ((2 * CHUNK, E), F32),
        ((HALF + 1, 2, 2, TEXTS, E), BF16),
        ((HALF + 1, 2, TEXTS, E), F32),
        ((E, IMGS), F32),
        ((2, HALF, TEXTS, E), BF16),
        ((2, HALF, TEXTS, E), BF16),
        ((HALF + 1, 2, TEXTS, E), BF16),
        ((HALF + 1, 2, TEXTS, E), BF16),
        ((TS, PIECE, IMGS), BF16),
        ((TS, PIECE, IMGS), BF16),
        ((PIECE, IMGS), F32),
        ((TS, PIECE, IMGS), BF16),
        ((TS, PIECE, IMGS), BF16),
        ((WIDE, IMGS), F32),
        ((D, WIDE), F32),
        ((2, HALF, ZROWS, WIDE), F32),
        ((2, HALF, ZROWS, WIDE), F32),
        ((4, ZROWS, WIDE), F32),
    ]
    return pl.pallas_call(
        kernel,
        out_shape=(
            jax.ShapeDtypeStruct((TEXTS, E), F32),
            jax.ShapeDtypeStruct((D // 64, COLS), F32),
        ),
        in_specs=[vmem, vmem, hbm, hbm, vmem, hbm, hbm, hbm],
        out_specs=(vmem, vmem),
        scratch_shapes=[pltpu.VMEM(shape, kind) for shape, kind in scratch]
        + [pltpu.SemaphoreType.DMA((size,)) for size in (S_ALL, S_ALL, 5)],
        compiler_params=pltpu.CompilerParams(
            collective_id=0, has_side_effects=True, vmem_limit_bytes=56 * 1024 * 1024
        ),
    )(
        text_hidden,
        ln_gain,
        up_weight.T,
        down_weight,
        final_gain,
        head_weight,
        image_features,
        vision_weight.T,
    )


def solution(mesh):
    placed = (
        P("dp", None),
        P(),
        P(None, "tensor"),
        P("tensor", None),
        P(),
        P("tensor", None),
        P("dp", None),
        P(None, "tensor"),
    )
    return jax.shard_map(
        local,
        mesh=mesh,
        in_specs=placed,
        out_specs=(P(("dp", "tensor"), None), P("dp", "tensor")),
        check_vma=False,
    )
```

```python
import functools

import jax
import jax.numpy as jnp
from jax import lax
from jax.experimental import pallas as pl
from jax.experimental.pallas import tpu as pltpu
from jax.sharding import PartitionSpec as P

logit_scale = 100.0
logit_bias = -4.0
norm_eps = 1e-06
MESH = pl.DeviceIdType.MESH
F32 = jnp.float32
BF16 = jnp.bfloat16

D = 1152
E = 1152
ROWS = 160
TS = 8
ZS = 16
HALF = ZS // 2
FF_DEV = 4304 // TS
TEXTS = ROWS // TS
CHUNK = 2 * TEXTS
IMGS = 384
PIECE = E // (2 * TS)
COLS = E // TS
WIDE = 128
ZROWS = D // ZS


def mm(a, b):
    return jnp.dot(a, b, preferred_element_type=F32)


def mm_t(a, b):
    return lax.dot_general(a, b, (((1,), (1,)), ((), ())), preferred_element_type=F32)


def layer_norm(values, gain_row):
    center = values - jnp.mean(values, axis=1, keepdims=True)
    spread = jnp.mean(center * center, axis=1, keepdims=True)
    return center * lax.rsqrt(spread + norm_eps) * gain_row


S_FEAT = 0
S_IMG = 1
S_IMGC = S_IMG + TS
S_MIX = S_IMGC + 1
S_NRM = S_MIX + TS
S_HEAD = S_NRM + TS
S_YH = S_HEAD + TS
S_AG = S_YH + 1
S_RS = S_AG + 4 * HALF
S_GY = S_RS + 2 * HALF
S_CX = S_GY + 2 * HALF + 2
S_PX = S_CX + TS
S_VR = S_PX + TS
S_FX = S_VR + ZS
S_ALL = S_FX + 4
L_FEAT, L_UP, L_DOWN, L_HEAD, L_VIS = range(5)


def kernel(
    text_ref,
    ln_ref,
    up_ref,
    down_ref,
    fg_ref,
    head_ref,
    feat_ref,
    vis_ref,
    tg_ref,
    vg_ref,
    up_v,
    down_v,
    head_v,
    vis_v,
    feats,
    part_t,
    img_s,
    img_r,
    img_f,
    img_ut,
    img_u,
    inv_ref,
    rad_ref,
    mix_s,
    mix_f,
    mix_r,
    nrm_s,
    nrm_r,
    nrm_a,
    head_s,
    head_f,
    head_r,
    block_f,
    ends_f,
    texts,
    grads,
    w_pad,
    w_ends,
    wt_all,
    text_all,
    eg_n,
    eg,
    rs_s,
    rs_r,
    gy_s,
    gy_r,
    cx_s,
    cx_r,
    px_f,
    px_s,
    px_r,
    emb_b,
    vg_all,
    vr_s,
    vr_r,
    fx,
    send_sem,
    recv_sem,
    load_sem,
):
    d = lax.axis_index("dp")
    t = lax.axis_index("tensor")
    z = d // 4
    yh = (d // 2) % 2
    c = d % 2
    base = d - 4 * z
    z_next = (lax.rem(z + 1, ZS) * 4 + base, t)
    z_prev = (lax.rem(z + ZS - 1, ZS) * 4 + base, t)
    yh_peer = (d + 2 - 4 * yh, t)
    c_peer = (d + 1 - 2 * c, t)
    q = 2 * yh + c

    def zmod(v):
        return lax.rem(v + 2 * ZS, ZS)

    def tpeer(k):
        return lax.rem(t + k, TS)

    def rcopy(src, dst, i_send, i_recv, dev):
        return pltpu.make_async_remote_copy(
            src_ref=src,
            dst_ref=dst,
            send_sem=send_sem.at[i_send],
            recv_sem=recv_sem.at[i_recv],
            device_id=dev,
            device_id_type=MESH,
        )

    barrier = pltpu.get_barrier_semaphore()
    z_peers = [(lax.rem(z + k, ZS) * 4 + base, t) for k in range(1, ZS)]
    greeted = z_peers + [(d, tpeer(k)) for k in range(1, TS)]
    fx_peers = [(4 * z + lax.rem(q + k, 4), t) for k in range(1, 4)]
    greeted = greeted + fx_peers
    for dev in greeted:
        pl.semaphore_signal(barrier, inc=1, device_id=dev, device_id_type=MESH)

    own_rows = pl.ds(pl.multiple_of(ROWS * c, 32), ROWS)
    other_rows = pl.ds(pl.multiple_of(ROWS * (1 - c), 32), ROWS)
    feats[2 * ROWS : IMGS, :] = jnp.zeros((IMGS - 2 * ROWS, D), BF16)
    w_pad[2 * CHUNK : WIDE, :] = jnp.zeros((WIDE - 2 * CHUNK, IMGS), F32)
    w_ends[2 * CHUNK : WIDE, :] = jnp.zeros((WIDE - 2 * CHUNK, IMGS), F32)
    text_all[...] = jnp.zeros_like(text_all)
    loads = [
        pltpu.make_async_copy(src, dst, load_sem.at[at])
        for at, (src, dst) in enumerate(
            [
                (feat_ref, feats.at[own_rows]),
                (up_ref, up_v),
                (down_ref, down_v),
                (head_ref, head_v),
                (vis_ref, vis_v),
            ]
        )
    ]
    for at in (L_UP, L_DOWN, L_FEAT, L_VIS, L_HEAD):
        loads[at].start()

    hidden = text_ref[...].astype(F32)
    lifted = layer_norm(hidden, ln_ref[...].reshape(1, D)).astype(BF16)
    loads[L_UP].wait()
    active = jax.nn.gelu(mm_t(lifted, up_v[...]), approximate=True).astype(BF16)
    loads[L_DOWN].wait()
    mixed = mm(active, down_v[...])
    for j in range(TS):
        mix_s[j] = mixed[TEXTS * j : TEXTS * (j + 1)].astype(BF16)

    pl.semaphore_wait(barrier, len(greeted))

    def exchange_start(src, dst, sem):
        for k in range(1, TS):
            rcopy(src.at[tpeer(k)], dst.at[t], sem + k, sem + t, (d, tpeer(k))).start()

    def exchange_wait(src, dst, sem):
        for k in range(1, TS):
            j = tpeer(k)
            rcopy(src.at[j], dst.at[t], sem + k, sem + t, (d, j)).wait_send()
            rcopy(src.at[j], dst.at[j], sem + k, sem + j, (d, j)).wait_recv()

    exchange_start(mix_s, mix_r, S_MIX)
    loads[L_FEAT].wait()
    feat_copy = rcopy(feats.at[own_rows], feats.at[own_rows], S_FEAT, S_FEAT, c_peer)
    feat_copy.start()
    mix_r[t] = jnp.zeros((TEXTS, D), BF16)
    with_hidden = mixed + hidden
    for j in range(TS):
        mix_f[j] = with_hidden[TEXTS * j : TEXTS * (j + 1)]

    loads[L_VIS].wait()
    feat_copy.wait_send()
    rcopy(feats.at[other_rows], feats.at[other_rows], S_FEAT, S_FEAT, c_peer).wait_recv()
    part_t[...] = mm_t(vis_v[...], feats[...])
    img_s[...] = part_t[pl.ds(pl.multiple_of(PIECE * c, 8), PIECE), :].astype(BF16)
    for k in range(1, TS):
        rcopy(img_s, img_r.at[c, t], S_IMG + k, S_IMG + t, (d, tpeer(k))).start()
    img_r[c, t] = img_s[...]

    exchange_wait(mix_s, mix_r, S_MIX)
    total = mix_f[t]
    for j in range(TS):
        total = total + mix_r[j].astype(F32)
    normed = layer_norm(total, fg_ref[...].reshape(1, D)).astype(BF16).astype(F32)
    for j in range(TS):
        nrm_s[j] = normed[:, COLS * j : COLS * (j + 1)].astype(BF16)
    exchange_start(nrm_s, nrm_r, S_NRM)
    nrm_r[t] = nrm_s[t]

    exchange_wait(nrm_s, nrm_r, S_NRM)
    for j in range(TS):
        nrm_a[TEXTS * j : TEXTS * (j + 1), :] = nrm_r[j].astype(F32)
    loads[L_HEAD].wait()
    head_part = mm(nrm_a[...].astype(BF16), head_v[...])
    for j in range(TS):
        head_f[j] = head_part[TEXTS * j : TEXTS * (j + 1)]
        head_s[j] = head_part[TEXTS * j : TEXTS * (j + 1)].astype(BF16)
    exchange_start(head_s, head_r, S_HEAD)
    head_r[t] = jnp.zeros((TEXTS, E), BF16)

    for k in range(1, TS):
        j = tpeer(k)
        rcopy(img_s, img_r.at[c, t], S_IMG + k, S_IMG + t, (d, j)).wait_send()
        rcopy(img_s, img_r.at[c, j], S_IMG + k, S_IMG + j, (d, j)).wait_recv()
    imgc_copy = rcopy(img_r.at[c], img_r.at[c], S_IMGC, S_IMGC, c_peer)
    imgc_copy.start()

    imgc_copy.wait_send()
    rcopy(img_r.at[1 - c], img_r.at[1 - c], S_IMGC, S_IMGC, c_peer).wait_recv()
    for j in range(TS):
        for h in range(2):
            at = COLS * j + PIECE * h
            img_f[at : at + PIECE, :] = img_r[h, j].astype(F32)
    emb_t = img_f[...]
    inverse = lax.rsqrt(jnp.sum(emb_t * emb_t, axis=0, keepdims=True) + norm_eps)
    inv_ref[...] = inverse
    unit_t = emb_t * inverse
    img_f[...] = unit_t
    img_ut[...] = unit_t.astype(BF16)

    exchange_wait(head_s, head_r, S_HEAD)
    text_emb = head_f[t]
    for j in range(TS):
        text_emb = text_emb + head_r[j].astype(F32)
    text_unit = text_emb * lax.rsqrt(
        jnp.sum(text_emb * text_emb, axis=1, keepdims=True) + norm_eps
    )
    texts[0, 0, 0] = text_unit.astype(BF16)

    def is_first(s):
        return isinstance(s, int) and s == 1

    def ag_copy(s, way, half):
        source = texts.at[0, 0, half] if is_first(s) else texts.at[s - 1, way, half]
        sem = S_AG + 4 * (s - 1) + 2 * way + half
        return rcopy(source, texts.at[s, way, half], sem, sem, (z_next, z_prev)[way])

    yh_copy = rcopy(texts.at[0, 0, 0], texts.at[0, 0, 1], S_YH, S_YH, yh_peer)
    ag_copy(1, 0, 0).start()
    ag_copy(1, 1, 0).start()
    yh_copy.start()

    row_ids = lax.broadcasted_iota(jnp.int32, (CHUNK, IMGS), 0)
    col_ids = lax.broadcasted_iota(jnp.int32, (CHUNK, IMGS), 1)
    diagonal = ((row_ids < TEXTS) & (col_ids == row_ids + ROWS * c + TEXTS * t)).astype(F32)

    def gy_copy(s, way):
        sem = S_GY + 2 * s + way
        return rcopy(gy_s.at[s, way], gy_r.at[s, way], sem, sem, yh_peer)

    own_pieces = ((0, 0), (0, 1))
    far_pieces = ((0, 0), (1, 1))
    pair_pieces = ((0, 0), (0, 1), (1, 0), (1, 1))

    def weigh(s, pieces):
        rows = TEXTS * len(pieces)
        first = CHUNK if pieces is far_pieces else 0
        rows_f = block_f if pieces is pair_pieces else ends_f
        weights_f = w_pad if pieces is pair_pieces else w_ends
        for at, (way, half) in enumerate(pieces):
            rows_f[first + TEXTS * at : first + TEXTS * (at + 1), :] = texts[s, way, half].astype(F32)
        block = rows_f[first : first + rows, :].astype(BF16)
        dots = mm(block, img_ut[...])
        weights = jax.nn.sigmoid(logit_scale * dots + logit_bias)
        if pieces is own_pieces:
            weights = weights - diagonal
        weights = (weights * (logit_scale / ROWS)).astype(BF16)
        wide_weights = weights.astype(F32)
        radial = jnp.sum(wide_weights * dots, axis=0, keepdims=True)
        weights_f[first : first + rows, :] = wide_weights
        if pieces is own_pieces:
            rad_ref[...] = radial
        else:
            rad_ref[...] += radial
        if pieces is pair_pieces:
            keep(s - 1, block_f, w_pad)
        return weights

    def keep(place, rows_f, weights_f):
        at = WIDE * place
        if not isinstance(place, int):
            at = pl.multiple_of(at, WIDE)
        text_all[pl.ds(at, 2 * CHUNK), :] = rows_f[...].astype(BF16)
        wt_all[:, pl.ds(at, WIDE)] = weights_f[...].T.astype(BF16)

    def text_terms(s, pieces, weights):
        terms = mm(weights, img_u[...])
        for at, (way, half) in enumerate(pieces):
            part = terms[TEXTS * at : TEXTS * (at + 1)]
            slot = way if pieces is pair_pieces else 0
            if half == 0:
                grads[s, slot] = part
            else:
                gy_s[s, slot] = part.astype(BF16)
                gy_copy(s, slot).start()

    def forward(s, half):
        for way in range(2):
            ag_copy(s, way, half).wait_recv()
            if half == way:
                ag_copy(s + 1, way, half).start()
            else:

                @pl.when(s < HALF - 1)
                def _():
                    ag_copy(s + 1, way, half).start()

    yh_copy.wait()
    ag_copy(1, 0, 1).start()
    ag_copy(1, 1, 1).start()
    img_u[...] = img_f[...].T.astype(BF16)
    first_step = jnp.int32(1)
    forward(first_step, 0)
    own_weights = weigh(0, own_pieces)
    forward(first_step, 1)
    text_terms(0, own_pieces, own_weights)

    def ag_step(s, _):
        forward(s, 0)
        weights = weigh(s - 1, pair_pieces)
        forward(s, 1)
        text_terms(s - 1, pair_pieces, weights)
        return 0

    lax.fori_loop(2, HALF, ag_step, 0)
    text_terms(HALF - 1, pair_pieces, weigh(HALF - 1, pair_pieces))
    most = WIDE * (HALF - 1)
    eg_n[...] = mm(wt_all[:, 0:most], text_all[0:most, :])

    def rs_copy(way, s):
        sem = S_RS + 2 * (s - 1) + way
        return rcopy(rs_s.at[way, s - 1], rs_r.at[way, s - 1], sem, sem, (z_next, z_prev)[way])

    def rs_first(way):
        return 1 + way

    def rs_step(way, s):
        left = HALF + 1 - s
        slot = 0 if s == 1 else 1 - way
        gy_copy(left, slot).wait_recv()
        value = grads[left, slot] + gy_r[left, slot].astype(F32)
        if s > rs_first(way):
            rs_copy(way, s - 1).wait_recv()
            value = value + rs_r[way, s - 2].astype(F32)
        rs_s[way, s - 1] = value.astype(BF16)
        rs_copy(way, s).start()

    ag_copy(HALF, 0, 0).wait_recv()
    ag_copy(HALF, 1, 1).wait_recv()
    far_weights = weigh(HALF, far_pieces)
    keep(HALF - 1, ends_f, w_ends)
    eg[...] = (eg_n[...] + mm(wt_all[:, most:], text_all[most:, :])).T

    radial = rad_ref[...]
    inverse = inv_ref[...]

    def emb_piece(j, half):
        rows = pl.ds(pl.multiple_of(COLS * j + PIECE * half, 8), PIECE)
        return (eg[rows, :] - img_f[rows, :] * radial) * inverse

    def cx_copy(k):
        j = tpeer(k)
        return rcopy(cx_s.at[j], cx_r.at[j], S_CX + k % TS, S_CX + k % TS, c_peer)

    for k in range(1, TS + 1):
        cx_s[tpeer(k)] = emb_piece(tpeer(k), 1 - c).astype(BF16)
        cx_copy(k).start()
    text_terms(HALF, far_pieces, far_weights)
    rs_step(1, 2)
    for k in range(1, TS + 1):
        j = tpeer(k)
        value = emb_piece(j, c)
        cx_copy(k).wait()
        value = value + cx_r[j].astype(F32)
        if k < TS:
            px_s[j] = value.astype(BF16)
            rcopy(px_s.at[j], px_r.at[t], S_PX + k, S_PX + t, (d, j)).start()
        else:
            px_f[...] = value
    px_r[t] = jnp.zeros((PIECE, IMGS), BF16)
    emb_b[PIECE:WIDE, :] = jnp.zeros((WIDE - PIECE, IMGS), F32)
    rs_step(0, 1)
    for s in range(2, 4):
        rs_step(0, s)
        rs_step(1, s + 1)
    exchange_wait(px_s, px_r, S_PX)
    emb_grad = px_f[...]
    for j in range(TS):
        emb_grad = emb_grad + px_r[j].astype(F32)
    emb_b[0:PIECE, :] = emb_grad
    vg_all[...] = mm(emb_b[...].astype(BF16), feats[...]).T

    def vr_copy(k):
        o = zmod(z + k)
        return rcopy(vr_s.at[o], vr_r.at[z], S_VR + k, S_VR + z, z_peers[k - 1])

    def vr_in(k):
        o = zmod(z + k)
        return rcopy(vr_s.at[o], vr_r.at[o], S_VR + k, S_VR + o, z_peers[k - 1])

    for o in range(ZS):
        vr_s[o] = vg_all[ZROWS * o : ZROWS * (o + 1), 0:PIECE].astype(BF16)
    far_first = sorted(range(1, ZS), key=lambda k: -min(k, ZS - k))
    for k in far_first:
        vr_copy(k).start()
    vr_r[z] = jnp.zeros((ZROWS, PIECE), BF16)

    for s in range(4, HALF + 1):
        rs_step(0, s)
        if s < HALF:
            rs_step(1, s + 1)
    gy_copy(0, 0).wait_recv()
    rs_copy(0, HALF).wait_recv()
    rs_copy(1, HALF).wait_recv()
    tg_ref[...] = (
        grads[0, 0]
        + gy_r[0, 0].astype(F32)
        + rs_r[0, HALF - 1].astype(F32)
        + rs_r[1, HALF - 1].astype(F32)
    )

    total_vg = vg_all[pl.ds(pl.multiple_of(ZROWS * z, 8), ZROWS), :][:, 0:PIECE]
    for k in far_first:
        vr_copy(k).wait_send()
        vr_in(k).wait_recv()
    for o in range(ZS):
        total_vg = total_vg + vr_r[o].astype(F32)
    fx[q] = total_vg
    for k in range(1, 4):
        rcopy(fx.at[q], fx.at[q], S_FX + k, S_FX + q, fx_peers[k - 1]).start()

    for half in range(2):
        for way in range(2):
            ag_copy(1, way, half).wait_send()

    def ag_drain(s, _):
        for half in range(2):
            for way in range(2):
                if half == way:
                    ag_copy(s, way, half).wait_send()
                else:

                    @pl.when(s < HALF)
                    def _():
                        ag_copy(s, way, half).wait_send()

        return 0

    lax.fori_loop(2, HALF + 1, ag_drain, 0)

    def gy_drain(s, _):
        gy_copy(s, 0).wait_send()
        gy_copy(s, 1).wait_send()
        return 0

    gy_copy(0, 0).wait_send()
    lax.fori_loop(1, HALF, gy_drain, 0)
    gy_copy(HALF, 0).wait_send()
    for s in range(1, HALF + 1):
        for way in range(2):
            if s >= rs_first(way):
                rs_copy(way, s).wait_send()

    for k in range(1, 4):
        o = lax.rem(q + k, 4)
        rcopy(fx.at[q], fx.at[q], S_FX + k, S_FX + q, fx_peers[k - 1]).wait_send()
        rcopy(fx.at[o], fx.at[o], S_FX + k, S_FX + o, fx_peers[k - 1]).wait_recv()
    left = fx[0] + fx[2]
    right = fx[1] + fx[3]
    for k in range(4):

        @pl.when(q == k)
        def _():
            vg_ref[:, 0:PIECE] = left[18 * k : 18 * (k + 1), 0:PIECE]
            vg_ref[:, PIECE:COLS] = right[18 * k : 18 * (k + 1), 0:PIECE]


def local(
    text_hidden,
    ln_gain,
    up_weight,
    down_weight,
    final_gain,
    head_weight,
    image_features,
    vision_weight,
):
    vmem = pl.BlockSpec(memory_space=pltpu.VMEM)
    hbm = pl.BlockSpec(memory_space=pl.ANY)
    scratch = [
        ((FF_DEV, D), BF16),
        ((FF_DEV, D), BF16),
        ((COLS, E), BF16),
        ((COLS, D), BF16),
        ((IMGS, D), BF16),
        ((COLS, IMGS), F32),
        ((PIECE, IMGS), BF16),
        ((2, TS, PIECE, IMGS), BF16),
        ((E, IMGS), F32),
        ((E, IMGS), BF16),
        ((IMGS, E), BF16),
        ((1, IMGS), F32),
        ((1, IMGS), F32),
        ((TS, TEXTS, D), BF16),
        ((TS, TEXTS, D), F32),
        ((TS, TEXTS, D), BF16),
        ((TS, TEXTS, COLS), BF16),
        ((TS, TEXTS, COLS), BF16),
        ((ROWS, COLS), F32),
        ((TS, TEXTS, E), BF16),
        ((TS, TEXTS, E), F32),
        ((TS, TEXTS, E), BF16),
        ((2 * CHUNK, E), F32),
        ((2 * CHUNK, E), F32),
        ((HALF + 1, 2, 2, TEXTS, E), BF16),
        ((HALF + 1, 2, TEXTS, E), F32),
        ((WIDE, IMGS), F32),
        ((WIDE, IMGS), F32),
        ((IMGS, HALF * WIDE), BF16),
        ((HALF * WIDE, E), BF16),
        ((IMGS, E), F32),
        ((E, IMGS), F32),
        ((2, HALF, TEXTS, E), BF16),
        ((2, HALF, TEXTS, E), BF16),
        ((HALF + 1, 2, TEXTS, E), BF16),
        ((HALF + 1, 2, TEXTS, E), BF16),
        ((TS, PIECE, IMGS), BF16),
        ((TS, PIECE, IMGS), BF16),
        ((PIECE, IMGS), F32),
        ((TS, PIECE, IMGS), BF16),
        ((TS, PIECE, IMGS), BF16),
        ((WIDE, IMGS), F32),
        ((D, WIDE), F32),
        ((ZS, ZROWS, PIECE), BF16),
        ((ZS, ZROWS, PIECE), BF16),
        ((4, ZROWS, PIECE), F32),
    ]
    return pl.pallas_call(
        kernel,
        out_shape=(
            jax.ShapeDtypeStruct((TEXTS, E), F32),
            jax.ShapeDtypeStruct((D // 64, COLS), F32),
        ),
        in_specs=[vmem, vmem, hbm, hbm, vmem, hbm, hbm, hbm],
        out_specs=(vmem, vmem),
        scratch_shapes=[pltpu.VMEM(shape, kind) for shape, kind in scratch]
        + [pltpu.SemaphoreType.DMA((size,)) for size in (S_ALL, S_ALL, 5)],
        compiler_params=pltpu.CompilerParams(
            collective_id=0, has_side_effects=True, vmem_limit_bytes=56 * 1024 * 1024
        ),
    )(
        text_hidden,
        ln_gain,
        up_weight.T,
        down_weight,
        final_gain,
        head_weight,
        image_features,
        vision_weight.T,
    )


def solution(mesh):
    placed = (
        P("dp", None),
        P(),
        P(None, "tensor"),
        P("tensor", None),
        P(),
        P("tensor", None),
        P("dp", None),
        P(None, "tensor"),
    )
    return jax.shard_map(
        local,
        mesh=mesh,
        in_specs=placed,
        out_specs=(P(("dp", "tensor"), None), P("dp", "tensor")),
        check_vma=False,
    )
```

```python
import functools

import jax
import jax.numpy as jnp
from jax import lax
from jax.experimental import pallas as pl
from jax.experimental.pallas import tpu as pltpu
from jax.sharding import PartitionSpec as P

logit_scale = 100.0
logit_bias = -4.0
norm_eps = 1e-06
MESH = pl.DeviceIdType.MESH
F32 = jnp.float32
BF16 = jnp.bfloat16

D = 1152
E = 1152
ROWS = 160
TS = 8
ZS = 16
HALF = ZS // 2
FF_DEV = 4304 // TS
TEXTS = ROWS // TS
CHUNK = 2 * TEXTS
IMGS = 384
PIECE = E // (2 * TS)
COLS = E // TS
WIDE = 128
ZROWS = D // ZS


def mm(a, b):
    return jnp.dot(a, b, preferred_element_type=F32)


def mm_t(a, b):
    return lax.dot_general(a, b, (((1,), (1,)), ((), ())), preferred_element_type=F32)


def layer_norm(values, gain_row):
    center = values - jnp.mean(values, axis=1, keepdims=True)
    spread = jnp.mean(center * center, axis=1, keepdims=True)
    return center * lax.rsqrt(spread + norm_eps) * gain_row


S_FEAT = 0
S_IMG = 1
S_IMGC = S_IMG + TS
S_MIX = S_IMGC + 1
S_NRM = S_MIX + TS
S_HEAD = S_NRM + TS
S_YH = S_HEAD + TS
S_AG = S_YH + 1
S_RS = S_AG + 4 * HALF
S_GY = S_RS + 2 * HALF
S_CX = S_GY + 2 * HALF + 2
S_PX = S_CX + TS
S_VR = S_PX + TS
S_FX = S_VR + ZS
S_ALL = S_FX + 4
L_FEAT, L_UP, L_DOWN, L_HEAD, L_VIS = range(5)


def kernel(
    text_ref,
    ln_ref,
    up_ref,
    down_ref,
    fg_ref,
    head_ref,
    feat_ref,
    vis_ref,
    tg_ref,
    vg_ref,
    up_v,
    down_v,
    head_v,
    vis_v,
    feats,
    part_t,
    img_s,
    img_r,
    img_f,
    img_ut,
    img_u,
    inv_ref,
    rad_ref,
    mix_s,
    mix_f,
    mix_r,
    nrm_s,
    nrm_r,
    nrm_a,
    head_s,
    head_f,
    head_r,
    block_f,
    texts,
    grads,
    eg,
    rs_s,
    rs_r,
    gy_s,
    gy_r,
    cx_s,
    cx_r,
    px_f,
    px_s,
    px_r,
    emb_b,
    vg_all,
    vr_s,
    vr_r,
    fx,
    send_sem,
    recv_sem,
    load_sem,
):
    d = lax.axis_index("dp")
    t = lax.axis_index("tensor")
    z = d // 4
    yh = (d // 2) % 2
    c = d % 2
    base = d - 4 * z
    z_next = (lax.rem(z + 1, ZS) * 4 + base, t)
    z_prev = (lax.rem(z + ZS - 1, ZS) * 4 + base, t)
    yh_peer = (d + 2 - 4 * yh, t)
    c_peer = (d + 1 - 2 * c, t)
    q = 2 * yh + c

    def zmod(v):
        return lax.rem(v + 2 * ZS, ZS)

    def tpeer(k):
        return lax.rem(t + k, TS)

    def rcopy(src, dst, i_send, i_recv, dev):
        return pltpu.make_async_remote_copy(
            src_ref=src,
            dst_ref=dst,
            send_sem=send_sem.at[i_send],
            recv_sem=recv_sem.at[i_recv],
            device_id=dev,
            device_id_type=MESH,
        )

    barrier = pltpu.get_barrier_semaphore()
    z_peers = [(lax.rem(z + k, ZS) * 4 + base, t) for k in range(1, ZS)]
    greeted = z_peers + [(d, tpeer(k)) for k in range(1, TS)]
    fx_peers = [(4 * z + lax.rem(q + k, 4), t) for k in range(1, 4)]
    greeted = greeted + fx_peers
    for dev in greeted:
        pl.semaphore_signal(barrier, inc=1, device_id=dev, device_id_type=MESH)

    own_rows = pl.ds(pl.multiple_of(ROWS * c, 32), ROWS)
    other_rows = pl.ds(pl.multiple_of(ROWS * (1 - c), 32), ROWS)
    feats[2 * ROWS : IMGS, :] = jnp.zeros((IMGS - 2 * ROWS, D), BF16)
    loads = [
        pltpu.make_async_copy(src, dst, load_sem.at[at])
        for at, (src, dst) in enumerate(
            [
                (feat_ref, feats.at[own_rows]),
                (up_ref, up_v),
                (down_ref, down_v),
                (head_ref, head_v),
                (vis_ref, vis_v),
            ]
        )
    ]
    for at in (L_UP, L_DOWN, L_FEAT, L_VIS, L_HEAD):
        loads[at].start()

    hidden = text_ref[...].astype(F32)
    lifted = layer_norm(hidden, ln_ref[...].reshape(1, D)).astype(BF16)
    loads[L_UP].wait()
    active = jax.nn.gelu(mm_t(lifted, up_v[...]), approximate=True).astype(BF16)
    loads[L_DOWN].wait()
    mixed = mm(active, down_v[...])
    for j in range(TS):
        mix_s[j] = mixed[TEXTS * j : TEXTS * (j + 1)].astype(BF16)

    pl.semaphore_wait(barrier, len(greeted))

    def exchange_start(src, dst, sem):
        for k in range(1, TS):
            rcopy(src.at[tpeer(k)], dst.at[t], sem + k, sem + t, (d, tpeer(k))).start()

    def exchange_wait(src, dst, sem):
        for k in range(1, TS):
            j = tpeer(k)
            rcopy(src.at[j], dst.at[t], sem + k, sem + t, (d, j)).wait_send()
            rcopy(src.at[j], dst.at[j], sem + k, sem + j, (d, j)).wait_recv()

    exchange_start(mix_s, mix_r, S_MIX)
    loads[L_FEAT].wait()
    feat_copy = rcopy(feats.at[own_rows], feats.at[own_rows], S_FEAT, S_FEAT, c_peer)
    feat_copy.start()
    mix_r[t] = jnp.zeros((TEXTS, D), BF16)
    with_hidden = mixed + hidden
    for j in range(TS):
        mix_f[j] = with_hidden[TEXTS * j : TEXTS * (j + 1)]

    loads[L_VIS].wait()
    feat_copy.wait_send()
    rcopy(feats.at[other_rows], feats.at[other_rows], S_FEAT, S_FEAT, c_peer).wait_recv()
    part_t[...] = mm_t(vis_v[...], feats[...])
    img_s[...] = part_t[pl.ds(pl.multiple_of(PIECE * c, 8), PIECE), :].astype(BF16)
    for k in range(1, TS):
        rcopy(img_s, img_r.at[c, t], S_IMG + k, S_IMG + t, (d, tpeer(k))).start()
    img_r[c, t] = img_s[...]

    exchange_wait(mix_s, mix_r, S_MIX)
    total = mix_f[t]
    for j in range(TS):
        total = total + mix_r[j].astype(F32)
    normed = layer_norm(total, fg_ref[...].reshape(1, D)).astype(BF16).astype(F32)
    for j in range(TS):
        nrm_s[j] = normed[:, COLS * j : COLS * (j + 1)].astype(BF16)
    exchange_start(nrm_s, nrm_r, S_NRM)
    nrm_r[t] = nrm_s[t]

    exchange_wait(nrm_s, nrm_r, S_NRM)
    for j in range(TS):
        nrm_a[TEXTS * j : TEXTS * (j + 1), :] = nrm_r[j].astype(F32)
    loads[L_HEAD].wait()
    head_part = mm(nrm_a[...].astype(BF16), head_v[...])
    for j in range(TS):
        head_f[j] = head_part[TEXTS * j : TEXTS * (j + 1)]
        head_s[j] = head_part[TEXTS * j : TEXTS * (j + 1)].astype(BF16)
    exchange_start(head_s, head_r, S_HEAD)
    head_r[t] = jnp.zeros((TEXTS, E), BF16)

    for k in range(1, TS):
        j = tpeer(k)
        rcopy(img_s, img_r.at[c, t], S_IMG + k, S_IMG + t, (d, j)).wait_send()
        rcopy(img_s, img_r.at[c, j], S_IMG + k, S_IMG + j, (d, j)).wait_recv()
    imgc_copy = rcopy(img_r.at[c], img_r.at[c], S_IMGC, S_IMGC, c_peer)
    imgc_copy.start()

    imgc_copy.wait_send()
    rcopy(img_r.at[1 - c], img_r.at[1 - c], S_IMGC, S_IMGC, c_peer).wait_recv()
    for j in range(TS):
        for h in range(2):
            at = COLS * j + PIECE * h
            img_f[at : at + PIECE, :] = img_r[h, j].astype(F32)
    emb_t = img_f[...]
    inverse = lax.rsqrt(jnp.sum(emb_t * emb_t, axis=0, keepdims=True) + norm_eps)
    inv_ref[...] = inverse
    unit_t = emb_t * inverse
    img_f[...] = unit_t
    img_ut[...] = unit_t.astype(BF16)

    exchange_wait(head_s, head_r, S_HEAD)
    text_emb = head_f[t]
    for j in range(TS):
        text_emb = text_emb + head_r[j].astype(F32)
    text_unit = text_emb * lax.rsqrt(
        jnp.sum(text_emb * text_emb, axis=1, keepdims=True) + norm_eps
    )
    texts[0, 0, 0] = text_unit.astype(BF16)

    def is_first(s):
        return isinstance(s, int) and s == 1

    def ag_copy(s, way, half):
        source = texts.at[0, 0, half] if is_first(s) else texts.at[s - 1, way, half]
        sem = S_AG + 4 * (s - 1) + 2 * way + half
        return rcopy(source, texts.at[s, way, half], sem, sem, (z_next, z_prev)[way])

    yh_copy = rcopy(texts.at[0, 0, 0], texts.at[0, 0, 1], S_YH, S_YH, yh_peer)
    ag_copy(1, 0, 0).start()
    ag_copy(1, 1, 0).start()
    yh_copy.start()

    row_ids = lax.broadcasted_iota(jnp.int32, (CHUNK, IMGS), 0)
    col_ids = lax.broadcasted_iota(jnp.int32, (CHUNK, IMGS), 1)
    diagonal = ((row_ids < TEXTS) & (col_ids == row_ids + ROWS * c + TEXTS * t)).astype(F32)

    def gy_copy(s, way):
        sem = S_GY + 2 * s + way
        return rcopy(gy_s.at[s, way], gy_r.at[s, way], sem, sem, yh_peer)

    own_pieces = ((0, 0), (0, 1))
    far_pieces = ((0, 0), (1, 1))
    pair_pieces = ((0, 0), (0, 1), (1, 0), (1, 1))

    def weigh(s, pieces):
        rows = TEXTS * len(pieces)
        for at, (way, half) in enumerate(pieces):
            block_f[TEXTS * at : TEXTS * (at + 1), :] = texts[s, way, half].astype(F32)
        block = block_f[0:rows, :].astype(BF16)
        dots = mm(block, img_ut[...])
        weights = jax.nn.sigmoid(logit_scale * dots + logit_bias)
        if pieces is own_pieces:
            weights = weights - diagonal
        weights = (weights * (logit_scale / ROWS)).astype(BF16)
        radial = jnp.sum(weights.astype(F32) * dots, axis=0, keepdims=True)
        terms = lax.dot_general(
            block, weights, (((0,), (0,)), ((), ())), preferred_element_type=F32
        )
        if pieces is own_pieces:
            rad_ref[...] = radial
            eg[...] = terms
        else:
            rad_ref[...] += radial
            eg[...] += terms
        return weights

    def text_terms(s, pieces, weights):
        terms = mm(weights, img_u[...])
        for at, (way, half) in enumerate(pieces):
            part = terms[TEXTS * at : TEXTS * (at + 1)]
            slot = way if pieces is pair_pieces else 0
            if half == 0:
                grads[s, slot] = part
            else:
                gy_s[s, slot] = part.astype(BF16)
                gy_copy(s, slot).start()

    def forward(s, half):
        for way in range(2):
            ag_copy(s, way, half).wait_recv()
            if half == way:
                ag_copy(s + 1, way, half).start()
            else:

                @pl.when(s < HALF - 1)
                def _():
                    ag_copy(s + 1, way, half).start()

    yh_copy.wait()
    ag_copy(1, 0, 1).start()
    ag_copy(1, 1, 1).start()
    img_u[...] = img_f[...].T.astype(BF16)
    first_step = jnp.int32(1)
    forward(first_step, 0)
    own_weights = weigh(0, own_pieces)
    forward(first_step, 1)
    text_terms(0, own_pieces, own_weights)

    def ag_step(s, _):
        forward(s, 0)
        weights = weigh(s - 1, pair_pieces)
        forward(s, 1)
        text_terms(s - 1, pair_pieces, weights)
        return 0

    lax.fori_loop(2, HALF, ag_step, 0)
    text_terms(HALF - 1, pair_pieces, weigh(HALF - 1, pair_pieces))

    def rs_copy(way, s):
        sem = S_RS + 2 * (s - 1) + way
        return rcopy(rs_s.at[way, s - 1], rs_r.at[way, s - 1], sem, sem, (z_next, z_prev)[way])

    def rs_first(way):
        return 1 + way

    def rs_step(way, s):
        left = HALF + 1 - s
        slot = 0 if s == 1 else 1 - way
        gy_copy(left, slot).wait_recv()
        value = grads[left, slot] + gy_r[left, slot].astype(F32)
        if s > rs_first(way):
            rs_copy(way, s - 1).wait_recv()
            value = value + rs_r[way, s - 2].astype(F32)
        rs_s[way, s - 1] = value.astype(BF16)
        rs_copy(way, s).start()

    ag_copy(HALF, 0, 0).wait_recv()
    ag_copy(HALF, 1, 1).wait_recv()
    far_weights = weigh(HALF, far_pieces)

    radial = rad_ref[...]
    inverse = inv_ref[...]

    def emb_piece(j, half):
        rows = pl.ds(pl.multiple_of(COLS * j + PIECE * half, 8), PIECE)
        return (eg[rows, :] - img_f[rows, :] * radial) * inverse

    def cx_copy(k):
        j = tpeer(k)
        return rcopy(cx_s.at[j], cx_r.at[j], S_CX + k % TS, S_CX + k % TS, c_peer)

    for k in range(1, TS + 1):
        cx_s[tpeer(k)] = emb_piece(tpeer(k), 1 - c).astype(BF16)
        cx_copy(k).start()
    text_terms(HALF, far_pieces, far_weights)
    rs_step(1, 2)
    for k in range(1, TS + 1):
        j = tpeer(k)
        value = emb_piece(j, c)
        cx_copy(k).wait()
        value = value + cx_r[j].astype(F32)
        if k < TS:
            px_s[j] = value.astype(BF16)
            rcopy(px_s.at[j], px_r.at[t], S_PX + k, S_PX + t, (d, j)).start()
        else:
            px_f[...] = value
    px_r[t] = jnp.zeros((PIECE, IMGS), BF16)
    emb_b[PIECE:WIDE, :] = jnp.zeros((WIDE - PIECE, IMGS), F32)
    rs_step(0, 1)
    for s in range(2, 4):
        rs_step(0, s)
        rs_step(1, s + 1)
    exchange_wait(px_s, px_r, S_PX)
    emb_grad = px_f[...]
    for j in range(TS):
        emb_grad = emb_grad + px_r[j].astype(F32)
    emb_b[0:PIECE, :] = emb_grad
    vg_all[...] = mm(emb_b[...].astype(BF16), feats[...]).T

    def vr_copy(k):
        o = zmod(z + k)
        return rcopy(vr_s.at[o], vr_r.at[z], S_VR + k, S_VR + z, z_peers[k - 1])

    def vr_in(k):
        o = zmod(z + k)
        return rcopy(vr_s.at[o], vr_r.at[o], S_VR + k, S_VR + o, z_peers[k - 1])

    for o in range(ZS):
        vr_s[o] = vg_all[ZROWS * o : ZROWS * (o + 1), 0:PIECE].astype(BF16)
    far_first = sorted(range(1, ZS), key=lambda k: -min(k, ZS - k))
    for k in far_first:
        vr_copy(k).start()
    vr_r[z] = jnp.zeros((ZROWS, PIECE), BF16)

    for s in range(4, HALF + 1):
        rs_step(0, s)
        if s < HALF:
            rs_step(1, s + 1)
    gy_copy(0, 0).wait_recv()
    rs_copy(0, HALF).wait_recv()
    rs_copy(1, HALF).wait_recv()
    tg_ref[...] = (
        grads[0, 0]
        + gy_r[0, 0].astype(F32)
        + rs_r[0, HALF - 1].astype(F32)
        + rs_r[1, HALF - 1].astype(F32)
    )

    total_vg = vg_all[pl.ds(pl.multiple_of(ZROWS * z, 8), ZROWS), :][:, 0:PIECE]
    for k in far_first:
        vr_copy(k).wait_send()
        vr_in(k).wait_recv()
    for o in range(ZS):
        total_vg = total_vg + vr_r[o].astype(F32)
    fx[q] = total_vg
    for k in range(1, 4):
        rcopy(fx.at[q], fx.at[q], S_FX + k, S_FX + q, fx_peers[k - 1]).start()

    for half in range(2):
        for way in range(2):
            ag_copy(1, way, half).wait_send()

    def ag_drain(s, _):
        for half in range(2):
            for way in range(2):
                if half == way:
                    ag_copy(s, way, half).wait_send()
                else:

                    @pl.when(s < HALF)
                    def _():
                        ag_copy(s, way, half).wait_send()

        return 0

    lax.fori_loop(2, HALF + 1, ag_drain, 0)

    def gy_drain(s, _):
        gy_copy(s, 0).wait_send()
        gy_copy(s, 1).wait_send()
        return 0

    gy_copy(0, 0).wait_send()
    lax.fori_loop(1, HALF, gy_drain, 0)
    gy_copy(HALF, 0).wait_send()
    for s in range(1, HALF + 1):
        for way in range(2):
            if s >= rs_first(way):
                rs_copy(way, s).wait_send()

    for k in range(1, 4):
        o = lax.rem(q + k, 4)
        rcopy(fx.at[q], fx.at[q], S_FX + k, S_FX + q, fx_peers[k - 1]).wait_send()
        rcopy(fx.at[o], fx.at[o], S_FX + k, S_FX + o, fx_peers[k - 1]).wait_recv()
    left = fx[0] + fx[2]
    right = fx[1] + fx[3]
    for k in range(4):

        @pl.when(q == k)
        def _():
            vg_ref[:, 0:PIECE] = left[18 * k : 18 * (k + 1), 0:PIECE]
            vg_ref[:, PIECE:COLS] = right[18 * k : 18 * (k + 1), 0:PIECE]


def local(
    text_hidden,
    ln_gain,
    up_weight,
    down_weight,
    final_gain,
    head_weight,
    image_features,
    vision_weight,
):
    vmem = pl.BlockSpec(memory_space=pltpu.VMEM)
    hbm = pl.BlockSpec(memory_space=pl.ANY)
    scratch = [
        ((FF_DEV, D), BF16),
        ((FF_DEV, D), BF16),
        ((COLS, E), BF16),
        ((COLS, D), BF16),
        ((IMGS, D), BF16),
        ((COLS, IMGS), F32),
        ((PIECE, IMGS), BF16),
        ((2, TS, PIECE, IMGS), BF16),
        ((E, IMGS), F32),
        ((E, IMGS), BF16),
        ((IMGS, E), BF16),
        ((1, IMGS), F32),
        ((1, IMGS), F32),
        ((TS, TEXTS, D), BF16),
        ((TS, TEXTS, D), F32),
        ((TS, TEXTS, D), BF16),
        ((TS, TEXTS, COLS), BF16),
        ((TS, TEXTS, COLS), BF16),
        ((ROWS, COLS), F32),
        ((TS, TEXTS, E), BF16),
        ((TS, TEXTS, E), F32),
        ((TS, TEXTS, E), BF16),
        ((2 * CHUNK, E), F32),
        ((HALF + 1, 2, 2, TEXTS, E), BF16),
        ((HALF + 1, 2, TEXTS, E), F32),
        ((E, IMGS), F32),
        ((2, HALF, TEXTS, E), BF16),
        ((2, HALF, TEXTS, E), BF16),
        ((HALF + 1, 2, TEXTS, E), BF16),
        ((HALF + 1, 2, TEXTS, E), BF16),
        ((TS, PIECE, IMGS), BF16),
        ((TS, PIECE, IMGS), BF16),
        ((PIECE, IMGS), F32),
        ((TS, PIECE, IMGS), BF16),
        ((TS, PIECE, IMGS), BF16),
        ((WIDE, IMGS), F32),
        ((D, WIDE), F32),
        ((ZS, ZROWS, PIECE), BF16),
        ((ZS, ZROWS, PIECE), BF16),
        ((4, ZROWS, PIECE), F32),
    ]
    return pl.pallas_call(
        kernel,
        out_shape=(
            jax.ShapeDtypeStruct((TEXTS, E), F32),
            jax.ShapeDtypeStruct((D // 64, COLS), F32),
        ),
        in_specs=[vmem, vmem, hbm, hbm, vmem, hbm, hbm, hbm],
        out_specs=(vmem, vmem),
        scratch_shapes=[pltpu.VMEM(shape, kind) for shape, kind in scratch]
        + [pltpu.SemaphoreType.DMA((size,)) for size in (S_ALL, S_ALL, 5)],
        compiler_params=pltpu.CompilerParams(
            collective_id=0, has_side_effects=True, vmem_limit_bytes=56 * 1024 * 1024
        ),
    )(
        text_hidden,
        ln_gain,
        up_weight.T,
        down_weight,
        final_gain,
        head_weight,
        image_features,
        vision_weight.T,
    )


def solution(mesh):
    placed = (
        P("dp", None),
        P(),
        P(None, "tensor"),
        P("tensor", None),
        P(),
        P("tensor", None),
        P("dp", None),
        P(None, "tensor"),
    )
    return jax.shard_map(
        local,
        mesh=mesh,
        in_specs=placed,
        out_specs=(P(("dp", "tensor"), None), P("dp", "tensor")),
        check_vma=False,
    )
```

```python
import functools

import jax
import jax.numpy as jnp
from jax import lax
from jax.experimental import pallas as pl
from jax.experimental.pallas import tpu as pltpu
from jax.sharding import PartitionSpec as P

logit_scale = 100.0
logit_bias = -4.0
norm_eps = 1e-06
MESH = pl.DeviceIdType.MESH
F32 = jnp.float32
BF16 = jnp.bfloat16

D = 1152
E = 1152
ROWS = 160
TS = 8
ZS = 16
HALF = ZS // 2
FF_DEV = 4304 // TS
TEXTS = ROWS // TS
CHUNK = 2 * TEXTS
IMGS = 384
PIECE = E // (2 * TS)
COLS = E // TS
WIDE = 128
ZROWS = D // ZS


def mm(a, b):
    return jnp.dot(a, b, preferred_element_type=F32)


def mm_t(a, b):
    return lax.dot_general(a, b, (((1,), (1,)), ((), ())), preferred_element_type=F32)


def layer_norm(values, gain_row):
    center = values - jnp.mean(values, axis=1, keepdims=True)
    spread = jnp.mean(center * center, axis=1, keepdims=True)
    return center * lax.rsqrt(spread + norm_eps) * gain_row


S_FEAT = 0
S_IMG = 1
S_IMGC = S_IMG + TS
S_MIX = S_IMGC + 1
S_NRM = S_MIX + TS
S_HEAD = S_NRM + TS
S_YH = S_HEAD + TS
S_AG = S_YH + 1
S_RS = S_AG + 4 * HALF
S_GY = S_RS + 2 * HALF
S_FAR = S_GY + 2 * HALF + 2
S_CX = S_FAR + 1
S_PX = S_CX + TS
S_VRP = S_PX + TS
S_VRM = S_VRP + HALF
S_FX = S_VRM + HALF
S_ALL = S_FX + 4
L_FEAT, L_UP, L_DOWN, L_HEAD, L_VIS = range(5)


def kernel(
    text_ref,
    ln_ref,
    up_ref,
    down_ref,
    fg_ref,
    head_ref,
    feat_ref,
    vis_ref,
    tg_ref,
    vg_ref,
    up_v,
    down_v,
    head_v,
    vis_v,
    feats,
    part_t,
    img_s,
    img_r,
    img_f,
    img_ut,
    img_u,
    inv_ref,
    rad_ref,
    mix_s,
    mix_f,
    mix_r,
    nrm_s,
    nrm_r,
    nrm_a,
    head_s,
    head_f,
    head_r,
    block_f,
    texts,
    grads,
    eg,
    rs_s,
    rs_r,
    gy_s,
    gy_r,
    far_s,
    far_r,
    cx_s,
    cx_r,
    px_f,
    px_s,
    px_r,
    emb_b,
    vg_all,
    vr_s,
    vr_r,
    fx,
    send_sem,
    recv_sem,
    load_sem,
):
    d = lax.axis_index("dp")
    t = lax.axis_index("tensor")
    z = d // 4
    yh = (d // 2) % 2
    c = d % 2
    base = d - 4 * z
    z_next = (lax.rem(z + 1, ZS) * 4 + base, t)
    z_prev = (lax.rem(z + ZS - 1, ZS) * 4 + base, t)
    yh_peer = (d + 2 - 4 * yh, t)
    c_peer = (d + 1 - 2 * c, t)
    q = 2 * yh + c

    def zmod(v):
        return lax.rem(v + 2 * ZS, ZS)

    def tpeer(k):
        return lax.rem(t + k, TS)

    def rcopy(src, dst, i_send, i_recv, dev):
        return pltpu.make_async_remote_copy(
            src_ref=src,
            dst_ref=dst,
            send_sem=send_sem.at[i_send],
            recv_sem=recv_sem.at[i_recv],
            device_id=dev,
            device_id_type=MESH,
        )

    barrier = pltpu.get_barrier_semaphore()
    z_far = (lax.rem(z + HALF, ZS) * 4 + base, t)
    greeted = [z_next, z_prev, z_far] + [(d, tpeer(k)) for k in range(1, TS)]
    fx_peers = [(4 * z + lax.rem(q + k, 4), t) for k in range(1, 4)]
    greeted = greeted + fx_peers
    for dev in greeted:
        pl.semaphore_signal(barrier, inc=1, device_id=dev, device_id_type=MESH)

    own_rows = pl.ds(pl.multiple_of(ROWS * c, 32), ROWS)
    other_rows = pl.ds(pl.multiple_of(ROWS * (1 - c), 32), ROWS)
    feats[2 * ROWS : IMGS, :] = jnp.zeros((IMGS - 2 * ROWS, D), BF16)
    loads = [
        pltpu.make_async_copy(src, dst, load_sem.at[at])
        for at, (src, dst) in enumerate(
            [
                (feat_ref, feats.at[own_rows]),
                (up_ref, up_v),
                (down_ref, down_v),
                (head_ref, head_v),
                (vis_ref, vis_v),
            ]
        )
    ]
    for at in (L_UP, L_DOWN, L_FEAT, L_VIS, L_HEAD):
        loads[at].start()

    hidden = text_ref[...].astype(F32)
    lifted = layer_norm(hidden, ln_ref[...].reshape(1, D)).astype(BF16)
    loads[L_UP].wait()
    active = jax.nn.gelu(mm_t(lifted, up_v[...]), approximate=True).astype(BF16)
    loads[L_DOWN].wait()
    mixed = mm(active, down_v[...])
    for j in range(TS):
        mix_s[j] = mixed[TEXTS * j : TEXTS * (j + 1)].astype(BF16)

    pl.semaphore_wait(barrier, len(greeted))

    def exchange_start(src, dst, sem):
        for k in range(1, TS):
            rcopy(src.at[tpeer(k)], dst.at[t], sem + k, sem + t, (d, tpeer(k))).start()

    def exchange_wait(src, dst, sem):
        for k in range(1, TS):
            j = tpeer(k)
            rcopy(src.at[j], dst.at[t], sem + k, sem + t, (d, j)).wait_send()
            rcopy(src.at[j], dst.at[j], sem + k, sem + j, (d, j)).wait_recv()

    exchange_start(mix_s, mix_r, S_MIX)
    loads[L_FEAT].wait()
    feat_copy = rcopy(feats.at[own_rows], feats.at[own_rows], S_FEAT, S_FEAT, c_peer)
    feat_copy.start()
    mix_r[t] = jnp.zeros((TEXTS, D), BF16)
    with_hidden = mixed + hidden
    for j in range(TS):
        mix_f[j] = with_hidden[TEXTS * j : TEXTS * (j + 1)]

    loads[L_VIS].wait()
    feat_copy.wait_send()
    rcopy(feats.at[other_rows], feats.at[other_rows], S_FEAT, S_FEAT, c_peer).wait_recv()
    part_t[...] = mm_t(vis_v[...], feats[...])
    img_s[...] = part_t[pl.ds(pl.multiple_of(PIECE * c, 8), PIECE), :][:, 0 : 2 * ROWS].astype(BF16)
    for k in range(1, TS):
        rcopy(img_s, img_r.at[c, t], S_IMG + k, S_IMG + t, (d, tpeer(k))).start()
    img_r[c, t] = img_s[...]

    img_f[:, 2 * WIDE : IMGS] = jnp.zeros((E, IMGS - 2 * WIDE), F32)
    emb_b[...] = jnp.zeros_like(emb_b)
    exchange_wait(mix_s, mix_r, S_MIX)
    total = mix_f[t]
    for j in range(TS):
        total = total + mix_r[j].astype(F32)
    normed = layer_norm(total, fg_ref[...].reshape(1, D)).astype(BF16).astype(F32)
    for j in range(TS):
        nrm_s[j] = normed[:, COLS * j : COLS * (j + 1)].astype(BF16)
    exchange_start(nrm_s, nrm_r, S_NRM)
    nrm_r[t] = nrm_s[t]

    exchange_wait(nrm_s, nrm_r, S_NRM)
    for j in range(TS):
        nrm_a[TEXTS * j : TEXTS * (j + 1), :] = nrm_r[j].astype(F32)
    loads[L_HEAD].wait()
    head_part = mm(nrm_a[...].astype(BF16), head_v[...])
    for j in range(TS):
        head_f[j] = head_part[TEXTS * j : TEXTS * (j + 1)]
        head_s[j] = head_part[TEXTS * j : TEXTS * (j + 1)].astype(BF16)
    exchange_start(head_s, head_r, S_HEAD)
    head_r[t] = jnp.zeros((TEXTS, E), BF16)

    for k in range(1, TS):
        j = tpeer(k)
        rcopy(img_s, img_r.at[c, t], S_IMG + k, S_IMG + t, (d, j)).wait_send()
        rcopy(img_s, img_r.at[c, j], S_IMG + k, S_IMG + j, (d, j)).wait_recv()
    imgc_copy = rcopy(img_r.at[c], img_r.at[c], S_IMGC, S_IMGC, c_peer)
    imgc_copy.start()

    imgc_copy.wait_send()
    rcopy(img_r.at[1 - c], img_r.at[1 - c], S_IMGC, S_IMGC, c_peer).wait_recv()
    for j in range(TS):
        for h in range(2):
            at = COLS * j + PIECE * h
            img_f[at : at + PIECE, 0 : 2 * ROWS] = img_r[h, j].astype(F32)
    emb_t = img_f[...]
    inverse = lax.rsqrt(jnp.sum(emb_t * emb_t, axis=0, keepdims=True) + norm_eps)
    inv_ref[...] = inverse
    unit_t = emb_t * inverse
    img_f[...] = unit_t
    img_ut[...] = unit_t.astype(BF16)

    exchange_wait(head_s, head_r, S_HEAD)
    text_emb = head_f[t]
    for j in range(TS):
        text_emb = text_emb + head_r[j].astype(F32)
    text_unit = text_emb * lax.rsqrt(
        jnp.sum(text_emb * text_emb, axis=1, keepdims=True) + norm_eps
    )
    texts[0, 0, 0] = text_unit.astype(BF16)

    def is_first(s):
        return isinstance(s, int) and s == 1

    def ag_copy(s, way, half):
        source = texts.at[0, 0, half] if is_first(s) else texts.at[s - 1, way, half]
        sem = S_AG + 4 * (s - 1) + 2 * way + half
        return rcopy(source, texts.at[s, way, half], sem, sem, (z_next, z_prev)[way])

    yh_copy = rcopy(texts.at[0, 0, 0], texts.at[0, 0, 1], S_YH, S_YH, yh_peer)
    ag_copy(1, 0, 0).start()
    ag_copy(1, 1, 0).start()
    yh_copy.start()

    row_ids = lax.broadcasted_iota(jnp.int32, (CHUNK, IMGS), 0)
    col_ids = lax.broadcasted_iota(jnp.int32, (CHUNK, IMGS), 1)
    diagonal = ((row_ids < TEXTS) & (col_ids == row_ids + ROWS * c + TEXTS * t)).astype(F32)

    def gy_copy(s, way):
        sem = S_GY + 2 * s + way
        return rcopy(gy_s.at[s, way], gy_r.at[s, way], sem, sem, yh_peer)

    own_pieces = ((0, 0), (0, 1))
    far_pieces = ((0, 0), (1, 1))
    pair_pieces = ((0, 0), (0, 1), (1, 0), (1, 1))

    def weigh(s, pieces):
        rows = TEXTS * len(pieces)
        for at, (way, half) in enumerate(pieces):
            block_f[TEXTS * at : TEXTS * (at + 1), :] = texts[s, way, half].astype(F32)
        block = block_f[0:rows, :].astype(BF16)
        dots = mm(block, img_ut[...])
        weights = jax.nn.sigmoid(logit_scale * dots + logit_bias)
        if pieces is own_pieces:
            weights = weights - diagonal
        weights = (weights * (logit_scale / ROWS)).astype(BF16)
        radial = jnp.sum(weights.astype(F32) * dots, axis=0, keepdims=True)
        terms = lax.dot_general(
            block, weights, (((0,), (0,)), ((), ())), preferred_element_type=F32
        )
        if pieces is own_pieces:
            rad_ref[...] = radial
            eg[...] = terms
        else:
            rad_ref[...] += radial
            eg[...] += terms
        return weights

    def text_terms(s, pieces, weights):
        terms = mm(weights, img_u[...])
        for at, (way, half) in enumerate(pieces):
            part = terms[TEXTS * at : TEXTS * (at + 1)]
            slot = way if pieces is pair_pieces else 0
            if half == 0:
                grads[s, slot] = part
            else:
                gy_s[s, slot] = part.astype(BF16)
                gy_copy(s, slot).start()

    def forward(s, half):
        for way in range(2):
            ag_copy(s, way, half).wait_recv()
            if half == way:
                ag_copy(s + 1, way, half).start()
            else:

                @pl.when(s < HALF - 1)
                def _():
                    ag_copy(s + 1, way, half).start()

    yh_copy.wait()
    ag_copy(1, 0, 1).start()
    ag_copy(1, 1, 1).start()
    img_u[...] = img_f[...].T.astype(BF16)
    first_step = jnp.int32(1)
    forward(first_step, 0)
    own_weights = weigh(0, own_pieces)
    forward(first_step, 1)
    text_terms(0, own_pieces, own_weights)

    def ag_step(s, _):
        forward(s, 0)
        weights = weigh(s - 1, pair_pieces)
        forward(s, 1)
        text_terms(s - 1, pair_pieces, weights)
        return 0

    lax.fori_loop(2, HALF, ag_step, 0)
    text_terms(HALF - 1, pair_pieces, weigh(HALF - 1, pair_pieces))

    def rs_copy(way, s):
        sem = S_RS + 2 * (s - 1) + way
        return rcopy(rs_s.at[way, s - 1], rs_r.at[way, s - 1], sem, sem, (z_next, z_prev)[way])

    def rs_step(s):
        left = HALF + 1 - s
        for way in range(2):
            slot = 1 - way
            gy_copy(left, slot).wait_recv()
            value = grads[left, slot] + gy_r[left, slot].astype(F32)
            if s > 2:
                rs_copy(way, s - 1).wait_recv()
                value = value + rs_r[way, s - 2].astype(F32)
            rs_s[way, s - 1] = value.astype(BF16)
            rs_copy(way, s).start()

    far_copy = rcopy(far_s, far_r, S_FAR, S_FAR, z_far)

    rs_step(2)
    ag_copy(HALF, 0, 0).wait_recv()
    ag_copy(HALF, 1, 1).wait_recv()
    far_weights = weigh(HALF, far_pieces)

    radial = rad_ref[...]
    inverse = inv_ref[...]

    def emb_piece(j, half):
        rows = pl.ds(pl.multiple_of(COLS * j + PIECE * half, 8), PIECE)
        return ((eg[rows, :] - img_f[rows, :] * radial) * inverse)[:, 0 : 2 * ROWS]

    def cx_copy(k):
        j = tpeer(k)
        return rcopy(cx_s.at[j], cx_r.at[j], S_CX + k % TS, S_CX + k % TS, c_peer)

    for k in range(1, TS + 1):
        cx_s[tpeer(k)] = emb_piece(tpeer(k), 1 - c).astype(BF16)
        cx_copy(k).start()
    text_terms(HALF, far_pieces, far_weights)
    for k in range(1, TS + 1):
        j = tpeer(k)
        value = emb_piece(j, c)
        cx_copy(k).wait()
        value = value + cx_r[j].astype(F32)
        if k < TS:
            px_s[j] = value.astype(BF16)
            rcopy(px_s.at[j], px_r.at[t], S_PX + k, S_PX + t, (d, j)).start()
        else:
            px_f[...] = value
    px_r[t] = jnp.zeros((PIECE, 2 * ROWS), BF16)
    rs_step(3)
    gy_copy(HALF, 0).wait_recv()
    far_s[...] = (grads[HALF, 0] + gy_r[HALF, 0].astype(F32)).astype(BF16)
    far_copy.start()
    rs_step(4)
    rs_step(5)
    exchange_wait(px_s, px_r, S_PX)
    emb_grad = px_f[...]
    for j in range(TS):
        emb_grad = emb_grad + px_r[j].astype(F32)
    emb_b[0:PIECE, 0 : 2 * ROWS] = emb_grad
    vg_all[...] = mm(emb_b[...].astype(BF16), feats[...]).T

    def vr_copy(way, s):
        sem = (S_VRP, S_VRM)[way] + s - 1
        return rcopy(vr_s.at[way, s - 1], vr_r.at[way, s - 1], sem, sem, (z_next, z_prev)[way])

    def vg_chunk(owner):
        return vg_all[pl.ds(pl.multiple_of(ZROWS * owner, 8), ZROWS), :][:, 0:PIECE]

    def vr_step(way, s):
        owner = zmod(z + HALF + 1 - s) if way == 0 else zmod(z - HALF + s)
        value = vg_chunk(owner)
        if s > 1:
            vr_copy(way, s - 1).wait_recv()
            value = value + vr_r[way, s - 2]
        vr_s[way, s - 1] = value
        vr_copy(way, s).start()

    for s in range(1, HALF + 1):
        vr_step(0, s)
        if s < HALF:
            vr_step(1, s)
        if s + 5 <= HALF:
            rs_step(s + 5)
        if s == HALF - 3:
            far_copy.wait()
            gy_copy(0, 0).wait_recv()
            rs_copy(0, HALF).wait_recv()
            rs_copy(1, HALF).wait_recv()
            tg_ref[...] = (
                grads[0, 0]
                + gy_r[0, 0].astype(F32)
                + rs_r[0, HALF - 1].astype(F32)
                + rs_r[1, HALF - 1].astype(F32)
                + far_r[...].astype(F32)
            )

    vr_copy(0, HALF).wait_recv()
    vr_copy(1, HALF - 1).wait_recv()
    fx[q] = vg_chunk(z) + vr_r[0, HALF - 1] + vr_r[1, HALF - 2]
    for k in range(1, 4):
        rcopy(fx.at[q], fx.at[q], S_FX + k, S_FX + q, fx_peers[k - 1]).start()

    for half in range(2):
        for way in range(2):
            ag_copy(1, way, half).wait_send()

    def ag_drain(s, _):
        for half in range(2):
            for way in range(2):
                if half == way:
                    ag_copy(s, way, half).wait_send()
                else:

                    @pl.when(s < HALF)
                    def _():
                        ag_copy(s, way, half).wait_send()

        return 0

    lax.fori_loop(2, HALF + 1, ag_drain, 0)

    def gy_drain(s, _):
        gy_copy(s, 0).wait_send()
        gy_copy(s, 1).wait_send()
        return 0

    gy_copy(0, 0).wait_send()
    lax.fori_loop(1, HALF, gy_drain, 0)
    gy_copy(HALF, 0).wait_send()
    for s in range(1, HALF + 1):
        for way in range(2):
            if s > 1:
                rs_copy(way, s).wait_send()
            if s < HALF or way == 0:
                vr_copy(way, s).wait_send()

    for k in range(1, 4):
        o = lax.rem(q + k, 4)
        rcopy(fx.at[q], fx.at[q], S_FX + k, S_FX + q, fx_peers[k - 1]).wait_send()
        rcopy(fx.at[o], fx.at[o], S_FX + k, S_FX + o, fx_peers[k - 1]).wait_recv()
    left = fx[0] + fx[2]
    right = fx[1] + fx[3]
    for k in range(4):

        @pl.when(q == k)
        def _():
            vg_ref[:, 0:PIECE] = left[18 * k : 18 * (k + 1), 0:PIECE]
            vg_ref[:, PIECE:COLS] = right[18 * k : 18 * (k + 1), 0:PIECE]


def local(
    text_hidden,
    ln_gain,
    up_weight,
    down_weight,
    final_gain,
    head_weight,
    image_features,
    vision_weight,
):
    vmem = pl.BlockSpec(memory_space=pltpu.VMEM)
    hbm = pl.BlockSpec(memory_space=pl.ANY)
    scratch = [
        ((FF_DEV, D), BF16),
        ((FF_DEV, D), BF16),
        ((COLS, E), BF16),
        ((COLS, D), BF16),
        ((IMGS, D), BF16),
        ((COLS, IMGS), F32),
        ((PIECE, 2 * ROWS), BF16),
        ((2, TS, PIECE, 2 * ROWS), BF16),
        ((E, IMGS), F32),
        ((E, IMGS), BF16),
        ((IMGS, E), BF16),
        ((1, IMGS), F32),
        ((1, IMGS), F32),
        ((TS, TEXTS, D), BF16),
        ((TS, TEXTS, D), F32),
        ((TS, TEXTS, D), BF16),
        ((TS, TEXTS, COLS), BF16),
        ((TS, TEXTS, COLS), BF16),
        ((ROWS, COLS), F32),
        ((TS, TEXTS, E), BF16),
        ((TS, TEXTS, E), F32),
        ((TS, TEXTS, E), BF16),
        ((2 * CHUNK, E), F32),
        ((HALF + 1, 2, 2, TEXTS, E), BF16),
        ((HALF + 1, 2, TEXTS, E), F32),
        ((E, IMGS), F32),
        ((2, HALF, TEXTS, E), BF16),
        ((2, HALF, TEXTS, E), BF16),
        ((HALF + 1, 2, TEXTS, E), BF16),
        ((HALF + 1, 2, TEXTS, E), BF16),
        ((TEXTS, E), BF16),
        ((TEXTS, E), BF16),
        ((TS, PIECE, 2 * ROWS), BF16),
        ((TS, PIECE, 2 * ROWS), BF16),
        ((PIECE, 2 * ROWS), F32),
        ((TS, PIECE, 2 * ROWS), BF16),
        ((TS, PIECE, 2 * ROWS), BF16),
        ((WIDE, IMGS), F32),
        ((D, WIDE), F32),
        ((2, HALF, ZROWS, PIECE), F32),
        ((2, HALF, ZROWS, PIECE), F32),
        ((4, ZROWS, PIECE), F32),
    ]
    return pl.pallas_call(
        kernel,
        out_shape=(
            jax.ShapeDtypeStruct((TEXTS, E), F32),
            jax.ShapeDtypeStruct((D // 64, COLS), F32),
        ),
        in_specs=[vmem, vmem, hbm, hbm, vmem, hbm, hbm, hbm],
        out_specs=(vmem, vmem),
        scratch_shapes=[pltpu.VMEM(shape, kind) for shape, kind in scratch]
        + [pltpu.SemaphoreType.DMA((size,)) for size in (S_ALL, S_ALL, 5)],
        compiler_params=pltpu.CompilerParams(
            collective_id=0, has_side_effects=True, vmem_limit_bytes=56 * 1024 * 1024
        ),
    )(
        text_hidden,
        ln_gain,
        up_weight.T,
        down_weight,
        final_gain,
        head_weight,
        image_features,
        vision_weight.T,
    )


def solution(mesh):
    placed = (
        P("dp", None),
        P(),
        P(None, "tensor"),
        P("tensor", None),
        P(),
        P("tensor", None),
        P("dp", None),
        P(None, "tensor"),
    )
    return jax.shard_map(
        local,
        mesh=mesh,
        in_specs=placed,
        out_specs=(P(("dp", "tensor"), None), P("dp", "tensor")),
        check_vma=False,
    )
```

```python
import functools

import jax
import jax.numpy as jnp
from jax import lax
from jax.experimental import pallas as pl
from jax.experimental.pallas import tpu as pltpu
from jax.sharding import PartitionSpec as P

logit_scale = 100.0
logit_bias = -4.0
norm_eps = 1e-06
MESH = pl.DeviceIdType.MESH
F32 = jnp.float32
BF16 = jnp.bfloat16

D = 1152
E = 1152
ROWS = 160
TS = 8
ZS = 16
HALF = ZS // 2
FF_DEV = 4304 // TS
TEXTS = ROWS // TS
SLOT = 24
CHUNK = 2 * SLOT
IMGS = 384
PIECE = E // (2 * TS)
COLS = E // TS
WIDE = 128
ZROWS = D // ZS


def mm(a, b):
    return jnp.dot(a, b, preferred_element_type=F32)


def mm_t(a, b):
    return lax.dot_general(a, b, (((1,), (1,)), ((), ())), preferred_element_type=F32)


def layer_norm(values, gain_row):
    center = values - jnp.mean(values, axis=1, keepdims=True)
    spread = jnp.mean(center * center, axis=1, keepdims=True)
    return center * lax.rsqrt(spread + norm_eps) * gain_row


S_FEAT = 0
S_IMG = 1
S_IMGC = S_IMG + TS
S_MIX = S_IMGC + 1
S_NRM = S_MIX + TS
S_HEAD = S_NRM + TS
S_YH = S_HEAD + TS
S_AG = S_YH + 1
S_RS = S_AG + 4 * HALF
S_GY = S_RS + 2 * HALF
S_CX = S_GY + 2 * HALF + 2
S_PX = S_CX + TS
S_VRP = S_PX + TS
S_VRM = S_VRP + HALF
S_FX = S_VRM + HALF
S_ALL = S_FX + 4
L_FEAT, L_UP, L_DOWN, L_HEAD, L_VIS = range(5)


def kernel(
    text_ref,
    ln_ref,
    up_ref,
    down_ref,
    fg_ref,
    head_ref,
    feat_ref,
    vis_ref,
    tg_ref,
    vg_ref,
    up_v,
    down_v,
    head_v,
    vis_v,
    feats,
    part_t,
    img_s,
    img_r,
    img_f,
    img_ut,
    img_u,
    inv_ref,
    rad_ref,
    mix_s,
    mix_f,
    mix_r,
    nrm_s,
    nrm_r,
    nrm_a,
    head_s,
    head_f,
    head_r,
    block_f,
    texts,
    grads,
    eg,
    rs_s,
    rs_r,
    gy_s,
    gy_r,
    cx_s,
    cx_r,
    px_f,
    px_s,
    px_r,
    emb_b,
    vg_all,
    vr_s,
    vr_r,
    fx,
    send_sem,
    recv_sem,
    load_sem,
):
    d = lax.axis_index("dp")
    t = lax.axis_index("tensor")
    z = d // 4
    yh = (d // 2) % 2
    c = d % 2
    base = d - 4 * z
    z_next = (lax.rem(z + 1, ZS) * 4 + base, t)
    z_prev = (lax.rem(z + ZS - 1, ZS) * 4 + base, t)
    yh_peer = (d + 2 - 4 * yh, t)
    c_peer = (d + 1 - 2 * c, t)
    q = 2 * yh + c

    def zmod(v):
        return lax.rem(v + 2 * ZS, ZS)

    def tpeer(k):
        return lax.rem(t + k, TS)

    def rcopy(src, dst, i_send, i_recv, dev):
        return pltpu.make_async_remote_copy(
            src_ref=src,
            dst_ref=dst,
            send_sem=send_sem.at[i_send],
            recv_sem=recv_sem.at[i_recv],
            device_id=dev,
            device_id_type=MESH,
        )

    barrier = pltpu.get_barrier_semaphore()
    greeted = [z_next, z_prev] + [(d, tpeer(k)) for k in range(1, TS)]
    fx_peers = [(4 * z + lax.rem(q + k, 4), t) for k in range(1, 4)]
    greeted = greeted + fx_peers
    for dev in greeted:
        pl.semaphore_signal(barrier, inc=1, device_id=dev, device_id_type=MESH)

    own_rows = pl.ds(pl.multiple_of(ROWS * c, 32), ROWS)
    other_rows = pl.ds(pl.multiple_of(ROWS * (1 - c), 32), ROWS)
    feats[2 * ROWS : IMGS, :] = jnp.zeros((IMGS - 2 * ROWS, D), BF16)
    loads = [
        pltpu.make_async_copy(src, dst, load_sem.at[at])
        for at, (src, dst) in enumerate(
            [
                (feat_ref, feats.at[own_rows]),
                (up_ref, up_v),
                (down_ref, down_v),
                (head_ref, head_v),
                (vis_ref, vis_v),
            ]
        )
    ]
    for at in (L_UP, L_DOWN, L_FEAT, L_VIS, L_HEAD):
        loads[at].start()

    hidden = text_ref[...].astype(F32)
    lifted = layer_norm(hidden, ln_ref[...].reshape(1, D)).astype(BF16)
    loads[L_UP].wait()
    active = jax.nn.gelu(mm_t(lifted, up_v[...]), approximate=True).astype(BF16)
    loads[L_DOWN].wait()
    mixed = mm(active, down_v[...])
    for j in range(TS):
        mix_s[j, 0:TEXTS] = mixed[TEXTS * j : TEXTS * (j + 1)].astype(BF16)
        mix_s[j, TEXTS:SLOT] = jnp.zeros((SLOT - TEXTS, D), BF16)

    pl.semaphore_wait(barrier, len(greeted))

    def exchange_start(src, dst, sem):
        for k in range(1, TS):
            rcopy(src.at[tpeer(k)], dst.at[t], sem + k, sem + t, (d, tpeer(k))).start()

    def exchange_wait(src, dst, sem):
        for k in range(1, TS):
            j = tpeer(k)
            rcopy(src.at[j], dst.at[t], sem + k, sem + t, (d, j)).wait_send()
            rcopy(src.at[j], dst.at[j], sem + k, sem + j, (d, j)).wait_recv()

    exchange_start(mix_s, mix_r, S_MIX)
    loads[L_FEAT].wait()
    feat_copy = rcopy(feats.at[own_rows], feats.at[own_rows], S_FEAT, S_FEAT, c_peer)
    feat_copy.start()
    mix_r[t] = jnp.zeros((SLOT, D), BF16)
    with_hidden = mixed + hidden
    for j in range(TS):
        mix_f[j, 0:TEXTS] = with_hidden[TEXTS * j : TEXTS * (j + 1)]
        mix_f[j, TEXTS:SLOT] = jnp.zeros((SLOT - TEXTS, D), F32)

    loads[L_VIS].wait()
    feat_copy.wait_send()
    rcopy(feats.at[other_rows], feats.at[other_rows], S_FEAT, S_FEAT, c_peer).wait_recv()
    part_t[...] = mm_t(vis_v[...], feats[...])
    img_s[...] = part_t[pl.ds(pl.multiple_of(PIECE * c, 8), PIECE), :].astype(BF16)
    for k in range(1, TS):
        rcopy(img_s, img_r.at[c, t], S_IMG + k, S_IMG + t, (d, tpeer(k))).start()
    img_r[c, t] = img_s[...]

    exchange_wait(mix_s, mix_r, S_MIX)
    total = mix_f[t]
    for j in range(TS):
        total = total + mix_r[j].astype(F32)
    normed = layer_norm(total, fg_ref[...].reshape(1, D)).astype(BF16).astype(F32)
    for j in range(TS):
        nrm_s[j, :, 0:COLS] = normed[:, COLS * j : COLS * (j + 1)].astype(BF16)
    exchange_start(nrm_s, nrm_r, S_NRM)
    nrm_r[t] = nrm_s[t]

    exchange_wait(nrm_s, nrm_r, S_NRM)
    for j in range(TS):
        nrm_a[SLOT * j : SLOT * (j + 1), :] = nrm_r[j].astype(F32)[:, 0:COLS]
    loads[L_HEAD].wait()
    head_part = mm(nrm_a[...].astype(BF16), head_v[...])
    for j in range(TS):
        head_f[j] = head_part[SLOT * j : SLOT * (j + 1)]
        head_s[j] = head_part[SLOT * j : SLOT * (j + 1)].astype(BF16)
    exchange_start(head_s, head_r, S_HEAD)
    head_r[t] = jnp.zeros((SLOT, E), BF16)

    for k in range(1, TS):
        j = tpeer(k)
        rcopy(img_s, img_r.at[c, t], S_IMG + k, S_IMG + t, (d, j)).wait_send()
        rcopy(img_s, img_r.at[c, j], S_IMG + k, S_IMG + j, (d, j)).wait_recv()
    imgc_copy = rcopy(img_r.at[c], img_r.at[c], S_IMGC, S_IMGC, c_peer)
    imgc_copy.start()

    imgc_copy.wait_send()
    rcopy(img_r.at[1 - c], img_r.at[1 - c], S_IMGC, S_IMGC, c_peer).wait_recv()
    for j in range(TS):
        for h in range(2):
            at = COLS * j + PIECE * h
            img_f[at : at + PIECE, :] = img_r[h, j].astype(F32)
    emb_t = img_f[...]
    inverse = lax.rsqrt(jnp.sum(emb_t * emb_t, axis=0, keepdims=True) + norm_eps)
    inv_ref[...] = inverse
    unit_t = emb_t * inverse
    img_f[...] = unit_t
    img_ut[...] = unit_t.astype(BF16)

    exchange_wait(head_s, head_r, S_HEAD)
    text_emb = head_f[t]
    for j in range(TS):
        text_emb = text_emb + head_r[j].astype(F32)
    text_unit = text_emb * lax.rsqrt(
        jnp.sum(text_emb * text_emb, axis=1, keepdims=True) + norm_eps
    )
    texts[0, 0, 0] = text_unit.astype(BF16)

    def is_first(s):
        return isinstance(s, int) and s == 1

    def ag_copy(s, way, half):
        source = texts.at[0, 0, half] if is_first(s) else texts.at[s - 1, way, half]
        sem = S_AG + 4 * (s - 1) + 2 * way + half
        return rcopy(source, texts.at[s, way, half], sem, sem, (z_next, z_prev)[way])

    yh_copy = rcopy(texts.at[0, 0, 0], texts.at[0, 0, 1], S_YH, S_YH, yh_peer)
    ag_copy(1, 0, 0).start()
    ag_copy(1, 1, 0).start()
    yh_copy.start()

    row_ids = lax.broadcasted_iota(jnp.int32, (CHUNK, IMGS), 0)
    col_ids = lax.broadcasted_iota(jnp.int32, (CHUNK, IMGS), 1)
    diagonal = ((row_ids < TEXTS) & (col_ids == row_ids + ROWS * c + TEXTS * t)).astype(F32)

    def gy_copy(s, way):
        sem = S_GY + 2 * s + way
        return rcopy(gy_s.at[s, way], gy_r.at[s, way], sem, sem, yh_peer)

    own_pieces = ((0, 0), (0, 1))
    far_pieces = ((0, 0), (1, 1))
    pair_pieces = ((0, 0), (0, 1), (1, 0), (1, 1))

    def weigh(s, pieces):
        rows = SLOT * len(pieces)
        for at, (way, half) in enumerate(pieces):
            block_f[SLOT * at : SLOT * (at + 1), :] = texts[s, way, half].astype(F32)
        block = block_f[0:rows, :].astype(BF16)
        dots = mm(block, img_ut[...])
        weights = jax.nn.sigmoid(logit_scale * dots + logit_bias)
        if pieces is own_pieces:
            weights = weights - diagonal
        weights = (weights * (logit_scale / ROWS)).astype(BF16)
        radial = jnp.sum(weights.astype(F32) * dots, axis=0, keepdims=True)
        terms = lax.dot_general(
            block, weights, (((0,), (0,)), ((), ())), preferred_element_type=F32
        )
        if pieces is own_pieces:
            rad_ref[...] = radial
            eg[...] = terms
        else:
            rad_ref[...] += radial
            eg[...] += terms
        return weights

    def text_terms(s, pieces, weights):
        terms = mm(weights, img_u[...])
        for at, (way, half) in enumerate(pieces):
            part = terms[SLOT * at : SLOT * (at + 1)]
            slot = way if pieces is pair_pieces else 0
            if half == 0:
                grads[s, slot] = part
            else:
                gy_s[s, slot] = part.astype(BF16)
                gy_copy(s, slot).start()

    def forward(s, half):
        for way in range(2):
            ag_copy(s, way, half).wait_recv()
            if half == way:
                ag_copy(s + 1, way, half).start()
            else:

                @pl.when(s < HALF - 1)
                def _():
                    ag_copy(s + 1, way, half).start()

    yh_copy.wait()
    ag_copy(1, 0, 1).start()
    ag_copy(1, 1, 1).start()
    img_u[...] = img_f[...].T.astype(BF16)
    first_step = jnp.int32(1)
    forward(first_step, 0)
    own_weights = weigh(0, own_pieces)
    forward(first_step, 1)
    text_terms(0, own_pieces, own_weights)

    def ag_step(s, _):
        forward(s, 0)
        weights = weigh(s - 1, pair_pieces)
        forward(s, 1)
        text_terms(s - 1, pair_pieces, weights)
        return 0

    lax.fori_loop(2, HALF, ag_step, 0)
    text_terms(HALF - 1, pair_pieces, weigh(HALF - 1, pair_pieces))

    def rs_copy(way, s):
        sem = S_RS + 2 * (s - 1) + way
        return rcopy(rs_s.at[way, s - 1], rs_r.at[way, s - 1], sem, sem, (z_next, z_prev)[way])

    def rs_first(way):
        return 1 + way

    def rs_step(way, s):
        left = HALF + 1 - s
        slot = 0 if s == 1 else 1 - way
        gy_copy(left, slot).wait_recv()
        value = grads[left, slot] + gy_r[left, slot].astype(F32)
        if s > rs_first(way):
            rs_copy(way, s - 1).wait_recv()
            value = value + rs_r[way, s - 2].astype(F32)
        rs_s[way, s - 1] = value.astype(BF16)
        rs_copy(way, s).start()

    ag_copy(HALF, 0, 0).wait_recv()
    ag_copy(HALF, 1, 1).wait_recv()
    text_terms(HALF, far_pieces, weigh(HALF, far_pieces))

    radial = rad_ref[...]
    inverse = inv_ref[...]

    def emb_piece(j, half):
        rows = pl.ds(pl.multiple_of(COLS * j + PIECE * half, 8), PIECE)
        return (eg[rows, :] - img_f[rows, :] * radial) * inverse

    def cx_copy(k):
        j = tpeer(k)
        return rcopy(cx_s.at[j], cx_r.at[j], S_CX + k % TS, S_CX + k % TS, c_peer)

    for k in range(1, TS + 1):
        cx_s[tpeer(k)] = emb_piece(tpeer(k), 1 - c).astype(BF16)
        cx_copy(k).start()
    rs_step(0, 1)
    rs_step(1, 2)
    for k in range(1, TS + 1):
        j = tpeer(k)
        value = emb_piece(j, c)
        cx_copy(k).wait()
        value = value + cx_r[j].astype(F32)
        if k < TS:
            px_s[j] = value.astype(BF16)
            rcopy(px_s.at[j], px_r.at[t], S_PX + k, S_PX + t, (d, j)).start()
        else:
            px_f[...] = value
    px_r[t] = jnp.zeros((PIECE, IMGS), BF16)
    emb_b[PIECE:WIDE, :] = jnp.zeros((WIDE - PIECE, IMGS), F32)
    for s in range(2, 4):
        rs_step(0, s)
        rs_step(1, s + 1)
    exchange_wait(px_s, px_r, S_PX)
    emb_grad = px_f[...]
    for j in range(TS):
        emb_grad = emb_grad + px_r[j].astype(F32)
    emb_b[0:PIECE, :] = emb_grad
    vg_all[...] = mm(emb_b[...].astype(BF16), feats[...]).T

    def vr_copy(way, s):
        sem = (S_VRP, S_VRM)[way] + s - 1
        return rcopy(vr_s.at[way, s - 1], vr_r.at[way, s - 1], sem, sem, (z_next, z_prev)[way])

    def vg_chunk(owner):
        return vg_all[pl.ds(pl.multiple_of(ZROWS * owner, 8), ZROWS), :]

    def vr_step(way, s):
        owner = zmod(z + HALF + 1 - s) if way == 0 else zmod(z - HALF + s)
        value = vg_chunk(owner)
        if s > 1:
            vr_copy(way, s - 1).wait_recv()
            value = value + vr_r[way, s - 2]
        vr_s[way, s - 1] = value
        vr_copy(way, s).start()

    for s in range(1, HALF + 1):
        vr_step(0, s)
        if s < HALF:
            vr_step(1, s)
        if s + 3 <= HALF:
            rs_step(0, s + 3)
        if s + 4 <= HALF:
            rs_step(1, s + 4)
        if s == HALF - 2:
            gy_copy(0, 0).wait_recv()
            rs_copy(0, HALF).wait_recv()
            rs_copy(1, HALF).wait_recv()
            total_tg = (
                grads[0, 0]
                + gy_r[0, 0].astype(F32)
                + rs_r[0, HALF - 1].astype(F32)
                + rs_r[1, HALF - 1].astype(F32)
            )
            tg_ref[...] = total_tg[0:TEXTS]

    vr_copy(0, HALF).wait_recv()
    vr_copy(1, HALF - 1).wait_recv()
    fx[q] = vg_chunk(z) + vr_r[0, HALF - 1] + vr_r[1, HALF - 2]
    for k in range(1, 4):
        rcopy(fx.at[q], fx.at[q], S_FX + k, S_FX + q, fx_peers[k - 1]).start()

    for half in range(2):
        for way in range(2):
            ag_copy(1, way, half).wait_send()

    def ag_drain(s, _):
        for half in range(2):
            for way in range(2):
                if half == way:
                    ag_copy(s, way, half).wait_send()
                else:

                    @pl.when(s < HALF)
                    def _():
                        ag_copy(s, way, half).wait_send()

        return 0

    lax.fori_loop(2, HALF + 1, ag_drain, 0)

    def gy_drain(s, _):
        gy_copy(s, 0).wait_send()
        gy_copy(s, 1).wait_send()
        return 0

    gy_copy(0, 0).wait_send()
    lax.fori_loop(1, HALF, gy_drain, 0)
    gy_copy(HALF, 0).wait_send()
    for s in range(1, HALF + 1):
        for way in range(2):
            if s >= rs_first(way):
                rs_copy(way, s).wait_send()
            if s < HALF or way == 0:
                vr_copy(way, s).wait_send()

    for k in range(1, 4):
        o = lax.rem(q + k, 4)
        rcopy(fx.at[q], fx.at[q], S_FX + k, S_FX + q, fx_peers[k - 1]).wait_send()
        rcopy(fx.at[o], fx.at[o], S_FX + k, S_FX + o, fx_peers[k - 1]).wait_recv()
    left = fx[0] + fx[2]
    right = fx[1] + fx[3]
    for k in range(4):

        @pl.when(q == k)
        def _():
            vg_ref[:, 0:PIECE] = left[18 * k : 18 * (k + 1), 0:PIECE]
            vg_ref[:, PIECE:COLS] = right[18 * k : 18 * (k + 1), 0:PIECE]


def local(
    text_hidden,
    ln_gain,
    up_weight,
    down_weight,
    final_gain,
    head_weight,
    image_features,
    vision_weight,
):
    vmem = pl.BlockSpec(memory_space=pltpu.VMEM)
    hbm = pl.BlockSpec(memory_space=pl.ANY)
    scratch = [
        ((FF_DEV, D), BF16),
        ((FF_DEV, D), BF16),
        ((COLS, E), BF16),
        ((COLS, D), BF16),
        ((IMGS, D), BF16),
        ((COLS, IMGS), F32),
        ((PIECE, IMGS), BF16),
        ((2, TS, PIECE, IMGS), BF16),
        ((E, IMGS), F32),
        ((E, IMGS), BF16),
        ((IMGS, E), BF16),
        ((1, IMGS), F32),
        ((1, IMGS), F32),
        ((TS, SLOT, D), BF16),
        ((TS, SLOT, D), F32),
        ((TS, SLOT, D), BF16),
        ((TS, SLOT, 2 * WIDE), BF16),
        ((TS, SLOT, 2 * WIDE), BF16),
        ((TS * SLOT, COLS), F32),
        ((TS, SLOT, E), BF16),
        ((TS, SLOT, E), F32),
        ((TS, SLOT, E), BF16),
        ((2 * CHUNK, E), F32),
        ((HALF + 1, 2, 2, SLOT, E), BF16),
        ((HALF + 1, 2, SLOT, E), F32),
        ((E, IMGS), F32),
        ((2, HALF, SLOT, E), BF16),
        ((2, HALF, SLOT, E), BF16),
        ((HALF + 1, 2, SLOT, E), BF16),
        ((HALF + 1, 2, SLOT, E), BF16),
        ((TS, PIECE, IMGS), BF16),
        ((TS, PIECE, IMGS), BF16),
        ((PIECE, IMGS), F32),
        ((TS, PIECE, IMGS), BF16),
        ((TS, PIECE, IMGS), BF16),
        ((WIDE, IMGS), F32),
        ((D, WIDE), F32),
        ((2, HALF, ZROWS, WIDE), F32),
        ((2, HALF, ZROWS, WIDE), F32),
        ((4, ZROWS, WIDE), F32),
    ]
    return pl.pallas_call(
        kernel,
        out_shape=(
            jax.ShapeDtypeStruct((TEXTS, E), F32),
            jax.ShapeDtypeStruct((D // 64, COLS), F32),
        ),
        in_specs=[vmem, vmem, hbm, hbm, vmem, hbm, hbm, hbm],
        out_specs=(vmem, vmem),
        scratch_shapes=[pltpu.VMEM(shape, kind) for shape, kind in scratch]
        + [pltpu.SemaphoreType.DMA((size,)) for size in (S_ALL, S_ALL, 5)],
        compiler_params=pltpu.CompilerParams(
            collective_id=0, has_side_effects=True, vmem_limit_bytes=56 * 1024 * 1024
        ),
    )(
        text_hidden,
        ln_gain,
        up_weight.T,
        down_weight,
        final_gain,
        head_weight,
        image_features,
        vision_weight.T,
    )


def solution(mesh):
    placed = (
        P("dp", None),
        P(),
        P(None, "tensor"),
        P("tensor", None),
        P(),
        P("tensor", None),
        P("dp", None),
        P(None, "tensor"),
    )
    return jax.shard_map(
        local,
        mesh=mesh,
        in_specs=placed,
        out_specs=(P(("dp", "tensor"), None), P("dp", "tensor")),
        check_vma=False,
    )
```

```python
import functools

import jax
import jax.numpy as jnp
from jax import lax
from jax.experimental import pallas as pl
from jax.experimental.pallas import tpu as pltpu
from jax.sharding import PartitionSpec as P

logit_scale = 100.0
logit_bias = -4.0
norm_eps = 1e-06
MESH = pl.DeviceIdType.MESH
F32 = jnp.float32
BF16 = jnp.bfloat16

D = 1152
E = 1152
ROWS = 160
TS = 8
ZS = 16
HALF = ZS // 2
FF_DEV = 4304 // TS
TEXTS = ROWS // TS
SLOT = 24
CHUNK = 2 * SLOT
IMGS = 384
PIECE = E // (2 * TS)
COLS = E // TS
WIDE = 128
ZROWS = D // ZS


def mm(a, b):
    return jnp.dot(a, b, preferred_element_type=F32)


def mm_t(a, b):
    return lax.dot_general(a, b, (((1,), (1,)), ((), ())), preferred_element_type=F32)


def layer_norm(values, gain_row):
    center = values - jnp.mean(values, axis=1, keepdims=True)
    spread = jnp.mean(center * center, axis=1, keepdims=True)
    return center * lax.rsqrt(spread + norm_eps) * gain_row


S_FEAT = 0
S_IMG = 1
S_IMGC = S_IMG + TS
S_MIX = S_IMGC + 1
S_NRM = S_MIX + TS
S_HEAD = S_NRM + TS
S_YH = S_HEAD + TS
S_AG = S_YH + 1
S_RS = S_AG + 4 * HALF
S_GY = S_RS + 2 * HALF
S_CX = S_GY + 2 * HALF + 2
S_PX = S_CX + TS
S_VRP = S_PX + TS
S_VRM = S_VRP + HALF
S_FX = S_VRM + HALF
S_ALL = S_FX + 4
L_FEAT, L_UP, L_DOWN, L_HEAD, L_VIS = range(5)


def kernel(
    text_ref,
    ln_ref,
    up_ref,
    down_ref,
    fg_ref,
    head_ref,
    feat_ref,
    vis_ref,
    tg_ref,
    vg_ref,
    up_v,
    down_v,
    head_v,
    vis_v,
    feats,
    part_t,
    img_s,
    img_r,
    img_f,
    img_ut,
    img_u,
    inv_ref,
    rad_ref,
    mix_s,
    mix_f,
    mix_r,
    nrm_s,
    nrm_r,
    nrm_a,
    head_s,
    head_f,
    head_r,
    block_f,
    texts,
    grads,
    eg,
    rs_s,
    rs_r,
    gy_s,
    gy_r,
    cx_s,
    cx_r,
    px_f,
    px_s,
    px_r,
    emb_b,
    vg_all,
    vr_s,
    vr_r,
    fx,
    send_sem,
    recv_sem,
    load_sem,
):
    d = lax.axis_index("dp")
    t = lax.axis_index("tensor")
    z = d // 4
    yh = (d // 2) % 2
    c = d % 2
    base = d - 4 * z
    z_next = (lax.rem(z + 1, ZS) * 4 + base, t)
    z_prev = (lax.rem(z + ZS - 1, ZS) * 4 + base, t)
    yh_peer = (d + 2 - 4 * yh, t)
    c_peer = (d + 1 - 2 * c, t)
    q = 2 * yh + c

    def zmod(v):
        return lax.rem(v + 2 * ZS, ZS)

    def tpeer(k):
        return lax.rem(t + k, TS)

    def rcopy(src, dst, i_send, i_recv, dev):
        return pltpu.make_async_remote_copy(
            src_ref=src,
            dst_ref=dst,
            send_sem=send_sem.at[i_send],
            recv_sem=recv_sem.at[i_recv],
            device_id=dev,
            device_id_type=MESH,
        )

    barrier = pltpu.get_barrier_semaphore()
    greeted = [z_next, z_prev] + [(d, tpeer(k)) for k in range(1, TS)]
    fx_peers = [(4 * z + lax.rem(q + k, 4), t) for k in range(1, 4)]
    greeted = greeted + fx_peers
    for dev in greeted:
        pl.semaphore_signal(barrier, inc=1, device_id=dev, device_id_type=MESH)

    own_rows = pl.ds(pl.multiple_of(ROWS * c, 32), ROWS)
    other_rows = pl.ds(pl.multiple_of(ROWS * (1 - c), 32), ROWS)
    feats[2 * ROWS : IMGS, :] = jnp.zeros((IMGS - 2 * ROWS, D), BF16)
    loads = [
        pltpu.make_async_copy(src, dst, load_sem.at[at])
        for at, (src, dst) in enumerate(
            [
                (feat_ref, feats.at[own_rows]),
                (up_ref, up_v),
                (down_ref, down_v),
                (head_ref, head_v),
                (vis_ref, vis_v),
            ]
        )
    ]
    for at in (L_UP, L_DOWN, L_FEAT, L_VIS, L_HEAD):
        loads[at].start()

    hidden = text_ref[...].astype(F32)
    lifted = layer_norm(hidden, ln_ref[...].reshape(1, D)).astype(BF16)
    loads[L_UP].wait()
    active = jax.nn.gelu(mm_t(lifted, up_v[...]), approximate=True).astype(BF16)
    loads[L_DOWN].wait()
    mixed = mm(active, down_v[...])
    for j in range(TS):
        mix_s[j, 0:TEXTS] = mixed[TEXTS * j : TEXTS * (j + 1)].astype(BF16)
        mix_s[j, TEXTS:SLOT] = jnp.zeros((SLOT - TEXTS, D), BF16)

    pl.semaphore_wait(barrier, len(greeted))

    def exchange_start(src, dst, sem):
        for k in range(1, TS):
            rcopy(src.at[tpeer(k)], dst.at[t], sem + k, sem + t, (d, tpeer(k))).start()

    def exchange_wait(src, dst, sem):
        for k in range(1, TS):
            j = tpeer(k)
            rcopy(src.at[j], dst.at[t], sem + k, sem + t, (d, j)).wait_send()
            rcopy(src.at[j], dst.at[j], sem + k, sem + j, (d, j)).wait_recv()

    exchange_start(mix_s, mix_r, S_MIX)
    loads[L_FEAT].wait()
    feat_copy = rcopy(feats.at[own_rows], feats.at[own_rows], S_FEAT, S_FEAT, c_peer)
    feat_copy.start()
    mix_r[t] = jnp.zeros((SLOT, D), BF16)
    with_hidden = mixed + hidden
    for j in range(TS):
        mix_f[j, 0:TEXTS] = with_hidden[TEXTS * j : TEXTS * (j + 1)]
        mix_f[j, TEXTS:SLOT] = jnp.zeros((SLOT - TEXTS, D), F32)

    loads[L_VIS].wait()
    feat_copy.wait_send()
    rcopy(feats.at[other_rows], feats.at[other_rows], S_FEAT, S_FEAT, c_peer).wait_recv()
    part_t[...] = mm_t(vis_v[...], feats[...])
    img_s[...] = part_t[pl.ds(pl.multiple_of(PIECE * c, 8), PIECE), :].astype(BF16)
    for k in range(1, TS):
        rcopy(img_s, img_r.at[c, t], S_IMG + k, S_IMG + t, (d, tpeer(k))).start()
    img_r[c, t] = img_s[...]

    exchange_wait(mix_s, mix_r, S_MIX)
    total = mix_f[t]
    for j in range(TS):
        total = total + mix_r[j].astype(F32)
    normed = layer_norm(total, fg_ref[...].reshape(1, D)).astype(BF16).astype(F32)
    for j in range(TS):
        nrm_s[j, :, 0:COLS] = normed[:, COLS * j : COLS * (j + 1)].astype(BF16)
    exchange_start(nrm_s, nrm_r, S_NRM)
    nrm_r[t] = nrm_s[t]

    exchange_wait(nrm_s, nrm_r, S_NRM)
    for j in range(TS):
        nrm_a[SLOT * j : SLOT * (j + 1), :] = nrm_r[j].astype(F32)[:, 0:COLS]
    loads[L_HEAD].wait()
    head_part = mm(nrm_a[...].astype(BF16), head_v[...])
    for j in range(TS):
        head_f[j] = head_part[SLOT * j : SLOT * (j + 1)]
        head_s[j] = head_part[SLOT * j : SLOT * (j + 1)].astype(BF16)
    exchange_start(head_s, head_r, S_HEAD)
    head_r[t] = jnp.zeros((SLOT, E), BF16)

    for k in range(1, TS):
        j = tpeer(k)
        rcopy(img_s, img_r.at[c, t], S_IMG + k, S_IMG + t, (d, j)).wait_send()
        rcopy(img_s, img_r.at[c, j], S_IMG + k, S_IMG + j, (d, j)).wait_recv()
    imgc_copy = rcopy(img_r.at[c], img_r.at[c], S_IMGC, S_IMGC, c_peer)
    imgc_copy.start()

    imgc_copy.wait_send()
    rcopy(img_r.at[1 - c], img_r.at[1 - c], S_IMGC, S_IMGC, c_peer).wait_recv()
    for j in range(TS):
        for h in range(2):
            at = COLS * j + PIECE * h
            img_f[at : at + PIECE, :] = img_r[h, j].astype(F32)
    emb_t = img_f[...]
    inverse = lax.rsqrt(jnp.sum(emb_t * emb_t, axis=0, keepdims=True) + norm_eps)
    inv_ref[...] = inverse
    unit_t = emb_t * inverse
    img_f[...] = unit_t
    img_ut[...] = unit_t.astype(BF16)

    exchange_wait(head_s, head_r, S_HEAD)
    text_emb = head_f[t]
    for j in range(TS):
        text_emb = text_emb + head_r[j].astype(F32)
    text_unit = text_emb * lax.rsqrt(
        jnp.sum(text_emb * text_emb, axis=1, keepdims=True) + norm_eps
    )
    texts[0, 0, 0] = text_unit.astype(BF16)

    def is_first(s):
        return isinstance(s, int) and s == 1

    def ag_copy(s, way, half):
        source = texts.at[0, 0, half] if is_first(s) else texts.at[s - 1, way, half]
        sem = S_AG + 4 * (s - 1) + 2 * way + half
        return rcopy(source, texts.at[s, way, half], sem, sem, (z_next, z_prev)[way])

    yh_copy = rcopy(texts.at[0, 0, 0], texts.at[0, 0, 1], S_YH, S_YH, yh_peer)
    ag_copy(1, 0, 0).start()
    ag_copy(1, 1, 0).start()
    yh_copy.start()

    row_ids = lax.broadcasted_iota(jnp.int32, (CHUNK, IMGS), 0)
    col_ids = lax.broadcasted_iota(jnp.int32, (CHUNK, IMGS), 1)
    diagonal = ((row_ids < TEXTS) & (col_ids == row_ids + ROWS * c + TEXTS * t)).astype(F32)

    def gy_copy(s, way):
        sem = S_GY + 2 * s + way
        return rcopy(gy_s.at[s, way], gy_r.at[s, way], sem, sem, yh_peer)

    own_pieces = ((0, 0), (0, 1))
    far_pieces = ((0, 0), (1, 1))
    pair_pieces = ((0, 0), (0, 1), (1, 0), (1, 1))

    def weigh(s, pieces):
        rows = SLOT * len(pieces)
        for at, (way, half) in enumerate(pieces):
            block_f[SLOT * at : SLOT * (at + 1), :] = texts[s, way, half].astype(F32)
        block = block_f[0:rows, :].astype(BF16)
        dots = mm(block, img_ut[...])
        weights = jax.nn.sigmoid(logit_scale * dots + logit_bias)
        if pieces is own_pieces:
            weights = weights - diagonal
        weights = (weights * (logit_scale / ROWS)).astype(BF16)
        radial = jnp.sum(weights.astype(F32) * dots, axis=0, keepdims=True)
        terms = lax.dot_general(
            block, weights, (((0,), (0,)), ((), ())), preferred_element_type=F32
        )
        if pieces is own_pieces:
            rad_ref[...] = radial
            eg[...] = terms
        else:
            rad_ref[...] += radial
            eg[...] += terms
        return weights

    def text_terms(s, pieces, weights):
        terms = mm(weights, img_u[...])
        for at, (way, half) in enumerate(pieces):
            part = terms[SLOT * at : SLOT * (at + 1)]
            slot = way if pieces is pair_pieces else 0
            if half == 0:
                grads[s, slot] = part
            else:
                gy_s[s, slot] = part.astype(BF16)
                gy_copy(s, slot).start()

    def forward(s, half):
        for way in range(2):
            ag_copy(s, way, half).wait_recv()
            if half == way:
                ag_copy(s + 1, way, half).start()
            else:

                @pl.when(s < HALF - 1)
                def _():
                    ag_copy(s + 1, way, half).start()

    yh_copy.wait()
    ag_copy(1, 0, 1).start()
    ag_copy(1, 1, 1).start()
    img_u[...] = img_f[...].T.astype(BF16)
    first_step = jnp.int32(1)
    forward(first_step, 0)
    own_weights = weigh(0, own_pieces)
    forward(first_step, 1)
    text_terms(0, own_pieces, own_weights)

    def ag_step(s, _):
        forward(s, 0)
        weights = weigh(s - 1, pair_pieces)
        forward(s, 1)
        text_terms(s - 1, pair_pieces, weights)
        return 0

    lax.fori_loop(2, HALF, ag_step, 0)
    text_terms(HALF - 1, pair_pieces, weigh(HALF - 1, pair_pieces))

    def rs_copy(way, s):
        sem = S_RS + 2 * (s - 1) + way
        return rcopy(rs_s.at[way, s - 1], rs_r.at[way, s - 1], sem, sem, (z_next, z_prev)[way])

    def rs_first(way):
        return 1 + way

    def rs_step(way, s):
        left = HALF + 1 - s
        slot = 0 if s == 1 else 1 - way
        gy_copy(left, slot).wait_recv()
        value = grads[left, slot] + gy_r[left, slot].astype(F32)
        if s > rs_first(way):
            rs_copy(way, s - 1).wait_recv()
            value = value + rs_r[way, s - 2].astype(F32)
        rs_s[way, s - 1] = value.astype(BF16)
        rs_copy(way, s).start()

    ag_copy(HALF, 0, 0).wait_recv()
    ag_copy(HALF, 1, 1).wait_recv()
    far_weights = weigh(HALF, far_pieces)

    radial = rad_ref[...]
    inverse = inv_ref[...]

    def emb_piece(j, half):
        rows = pl.ds(pl.multiple_of(COLS * j + PIECE * half, 8), PIECE)
        return (eg[rows, :] - img_f[rows, :] * radial) * inverse

    def cx_copy(k):
        j = tpeer(k)
        return rcopy(cx_s.at[j], cx_r.at[j], S_CX + k % TS, S_CX + k % TS, c_peer)

    for k in range(1, TS + 1):
        cx_s[tpeer(k)] = emb_piece(tpeer(k), 1 - c).astype(BF16)
        cx_copy(k).start()
    text_terms(HALF, far_pieces, far_weights)
    rs_step(1, 2)
    rs_step(0, 1)
    for k in range(1, TS + 1):
        j = tpeer(k)
        value = emb_piece(j, c)
        cx_copy(k).wait()
        value = value + cx_r[j].astype(F32)
        if k < TS:
            px_s[j] = value.astype(BF16)
            rcopy(px_s.at[j], px_r.at[t], S_PX + k, S_PX + t, (d, j)).start()
        else:
            px_f[...] = value
    px_r[t] = jnp.zeros((PIECE, IMGS), BF16)
    emb_b[PIECE:WIDE, :] = jnp.zeros((WIDE - PIECE, IMGS), F32)
    for s in range(2, 4):
        rs_step(0, s)
        rs_step(1, s + 1)
    exchange_wait(px_s, px_r, S_PX)
    emb_grad = px_f[...]
    for j in range(TS):
        emb_grad = emb_grad + px_r[j].astype(F32)
    emb_b[0:PIECE, :] = emb_grad
    vg_all[...] = mm(emb_b[...].astype(BF16), feats[...]).T

    def vr_copy(way, s):
        sem = (S_VRP, S_VRM)[way] + s - 1
        return rcopy(vr_s.at[way, s - 1], vr_r.at[way, s - 1], sem, sem, (z_next, z_prev)[way])

    def vg_chunk(owner):
        return vg_all[pl.ds(pl.multiple_of(ZROWS * owner, 8), ZROWS), :]

    def vr_step(way, s):
        owner = zmod(z + HALF + 1 - s) if way == 0 else zmod(z - HALF + s)
        value = vg_chunk(owner)
        if s > 1:
            vr_copy(way, s - 1).wait_recv()
            value = value + vr_r[way, s - 2].astype(F32)
        vr_s[way, s - 1] = value.astype(BF16)
        vr_copy(way, s).start()

    for s in range(1, HALF + 1):
        vr_step(0, s)
        if s < HALF:
            vr_step(1, s)
        if s + 3 <= HALF:
            rs_step(0, s + 3)
        if s + 4 <= HALF:
            rs_step(1, s + 4)
        if s == HALF - 2:
            gy_copy(0, 0).wait_recv()
            rs_copy(0, HALF).wait_recv()
            rs_copy(1, HALF).wait_recv()
            total_tg = (
                grads[0, 0]
                + gy_r[0, 0].astype(F32)
                + rs_r[0, HALF - 1].astype(F32)
                + rs_r[1, HALF - 1].astype(F32)
            )
            tg_ref[...] = total_tg[0:TEXTS]

    vr_copy(0, HALF).wait_recv()
    vr_copy(1, HALF - 1).wait_recv()
    fx[q] = vg_chunk(z) + vr_r[0, HALF - 1].astype(F32) + vr_r[1, HALF - 2].astype(F32)
    for k in range(1, 4):
        rcopy(fx.at[q], fx.at[q], S_FX + k, S_FX + q, fx_peers[k - 1]).start()

    for half in range(2):
        for way in range(2):
            ag_copy(1, way, half).wait_send()

    def ag_drain(s, _):
        for half in range(2):
            for way in range(2):
                if half == way:
                    ag_copy(s, way, half).wait_send()
                else:

                    @pl.when(s < HALF)
                    def _():
                        ag_copy(s, way, half).wait_send()

        return 0

    lax.fori_loop(2, HALF + 1, ag_drain, 0)

    def gy_drain(s, _):
        gy_copy(s, 0).wait_send()
        gy_copy(s, 1).wait_send()
        return 0

    gy_copy(0, 0).wait_send()
    lax.fori_loop(1, HALF, gy_drain, 0)
    gy_copy(HALF, 0).wait_send()
    for s in range(1, HALF + 1):
        for way in range(2):
            if s >= rs_first(way):
                rs_copy(way, s).wait_send()
            if s < HALF or way == 0:
                vr_copy(way, s).wait_send()

    for k in range(1, 4):
        o = lax.rem(q + k, 4)
        rcopy(fx.at[q], fx.at[q], S_FX + k, S_FX + q, fx_peers[k - 1]).wait_send()
        rcopy(fx.at[o], fx.at[o], S_FX + k, S_FX + o, fx_peers[k - 1]).wait_recv()
    left = fx[0] + fx[2]
    right = fx[1] + fx[3]
    for k in range(4):

        @pl.when(q == k)
        def _():
            vg_ref[:, 0:PIECE] = left[18 * k : 18 * (k + 1), 0:PIECE]
            vg_ref[:, PIECE:COLS] = right[18 * k : 18 * (k + 1), 0:PIECE]


def local(
    text_hidden,
    ln_gain,
    up_weight,
    down_weight,
    final_gain,
    head_weight,
    image_features,
    vision_weight,
):
    vmem = pl.BlockSpec(memory_space=pltpu.VMEM)
    hbm = pl.BlockSpec(memory_space=pl.ANY)
    scratch = [
        ((FF_DEV, D), BF16),
        ((FF_DEV, D), BF16),
        ((COLS, E), BF16),
        ((COLS, D), BF16),
        ((IMGS, D), BF16),
        ((COLS, IMGS), F32),
        ((PIECE, IMGS), BF16),
        ((2, TS, PIECE, IMGS), BF16),
        ((E, IMGS), F32),
        ((E, IMGS), BF16),
        ((IMGS, E), BF16),
        ((1, IMGS), F32),
        ((1, IMGS), F32),
        ((TS, SLOT, D), BF16),
        ((TS, SLOT, D), F32),
        ((TS, SLOT, D), BF16),
        ((TS, SLOT, 2 * WIDE), BF16),
        ((TS, SLOT, 2 * WIDE), BF16),
        ((TS * SLOT, COLS), F32),
        ((TS, SLOT, E), BF16),
        ((TS, SLOT, E), F32),
        ((TS, SLOT, E), BF16),
        ((2 * CHUNK, E), F32),
        ((HALF + 1, 2, 2, SLOT, E), BF16),
        ((HALF + 1, 2, SLOT, E), F32),
        ((E, IMGS), F32),
        ((2, HALF, SLOT, E), BF16),
        ((2, HALF, SLOT, E), BF16),
        ((HALF + 1, 2, SLOT, E), BF16),
        ((HALF + 1, 2, SLOT, E), BF16),
        ((TS, PIECE, IMGS), BF16),
        ((TS, PIECE, IMGS), BF16),
        ((PIECE, IMGS), F32),
        ((TS, PIECE, IMGS), BF16),
        ((TS, PIECE, IMGS), BF16),
        ((WIDE, IMGS), F32),
        ((D, WIDE), F32),
        ((2, HALF, ZROWS, WIDE), BF16),
        ((2, HALF, ZROWS, WIDE), BF16),
        ((4, ZROWS, WIDE), F32),
    ]
    return pl.pallas_call(
        kernel,
        out_shape=(
            jax.ShapeDtypeStruct((TEXTS, E), F32),
            jax.ShapeDtypeStruct((D // 64, COLS), F32),
        ),
        in_specs=[vmem, vmem, hbm, hbm, vmem, hbm, hbm, hbm],
        out_specs=(vmem, vmem),
        scratch_shapes=[pltpu.VMEM(shape, kind) for shape, kind in scratch]
        + [pltpu.SemaphoreType.DMA((size,)) for size in (S_ALL, S_ALL, 5)],
        compiler_params=pltpu.CompilerParams(
            collective_id=0, has_side_effects=True, vmem_limit_bytes=56 * 1024 * 1024
        ),
    )(
        text_hidden,
        ln_gain,
        up_weight.T,
        down_weight,
        final_gain,
        head_weight,
        image_features,
        vision_weight.T,
    )


def solution(mesh):
    placed = (
        P("dp", None),
        P(),
        P(None, "tensor"),
        P("tensor", None),
        P(),
        P("tensor", None),
        P("dp", None),
        P(None, "tensor"),
    )
    return jax.shard_map(
        local,
        mesh=mesh,
        in_specs=placed,
        out_specs=(P(("dp", "tensor"), None), P("dp", "tensor")),
        check_vma=False,
    )
```

```python
import functools

import jax
import jax.numpy as jnp
from jax import lax
from jax.experimental import pallas as pl
from jax.experimental.pallas import tpu as pltpu
from jax.sharding import PartitionSpec as P

logit_scale = 100.0
logit_bias = -4.0
norm_eps = 1e-06
MESH = pl.DeviceIdType.MESH
F32 = jnp.float32
BF16 = jnp.bfloat16

D = 1152
E = 1152
ROWS = 160
TS = 8
ZS = 16
HALF = ZS // 2
FF_DEV = 4304 // TS
TEXTS = ROWS // TS
SLOT = 24
CHUNK = 2 * SLOT
IMGS = 384
PIECE = E // (2 * TS)
COLS = E // TS
WIDE = 128
ZROWS = D // ZS


def mm(a, b):
    return jnp.dot(a, b, preferred_element_type=F32)


def mm_t(a, b):
    return lax.dot_general(a, b, (((1,), (1,)), ((), ())), preferred_element_type=F32)


def layer_norm(values, gain_row):
    center = values - jnp.mean(values, axis=1, keepdims=True)
    spread = jnp.mean(center * center, axis=1, keepdims=True)
    return center * lax.rsqrt(spread + norm_eps) * gain_row


S_FEAT = 0
S_IMG = 1
S_IMGC = S_IMG + TS
S_MIX = S_IMGC + 1
S_NRM = S_MIX + TS
S_HEAD = S_NRM + TS
S_YH = S_HEAD + TS
S_AG = S_YH + 1
S_RS = S_AG + 4 * HALF
S_GY = S_RS + 2 * HALF
S_FAR = S_GY + 2 * HALF + 2
S_CX = S_FAR + 1
S_PX = S_CX + TS
S_VRP = S_PX + TS
S_VRM = S_VRP + HALF
S_FX = S_VRM + HALF
S_ALL = S_FX + 4
L_FEAT, L_UP, L_DOWN, L_HEAD, L_VIS = range(5)


def kernel(
    text_ref,
    ln_ref,
    up_ref,
    down_ref,
    fg_ref,
    head_ref,
    feat_ref,
    vis_ref,
    tg_ref,
    vg_ref,
    up_v,
    down_v,
    head_v,
    vis_v,
    feats,
    part_t,
    img_s,
    img_r,
    img_f,
    img_ut,
    img_u,
    inv_ref,
    rad_ref,
    mix_s,
    mix_f,
    mix_r,
    nrm_s,
    nrm_r,
    nrm_a,
    head_s,
    head_f,
    head_r,
    block_f,
    texts,
    grads,
    eg,
    rs_s,
    rs_r,
    gy_s,
    gy_r,
    far_s,
    far_r,
    cx_s,
    cx_r,
    px_f,
    px_s,
    px_r,
    emb_b,
    vg_all,
    vr_s,
    vr_r,
    fx,
    send_sem,
    recv_sem,
    load_sem,
):
    d = lax.axis_index("dp")
    t = lax.axis_index("tensor")
    z = d // 4
    yh = (d // 2) % 2
    c = d % 2
    base = d - 4 * z
    z_next = (lax.rem(z + 1, ZS) * 4 + base, t)
    z_prev = (lax.rem(z + ZS - 1, ZS) * 4 + base, t)
    yh_peer = (d + 2 - 4 * yh, t)
    c_peer = (d + 1 - 2 * c, t)
    q = 2 * yh + c

    def zmod(v):
        return lax.rem(v + 2 * ZS, ZS)

    def tpeer(k):
        return lax.rem(t + k, TS)

    def rcopy(src, dst, i_send, i_recv, dev):
        return pltpu.make_async_remote_copy(
            src_ref=src,
            dst_ref=dst,
            send_sem=send_sem.at[i_send],
            recv_sem=recv_sem.at[i_recv],
            device_id=dev,
            device_id_type=MESH,
        )

    barrier = pltpu.get_barrier_semaphore()
    z_far = (lax.rem(z + HALF, ZS) * 4 + base, t)
    greeted = [z_next, z_prev, z_far] + [(d, tpeer(k)) for k in range(1, TS)]
    fx_peers = [(4 * z + lax.rem(q + k, 4), t) for k in range(1, 4)]
    greeted = greeted + fx_peers
    for dev in greeted:
        pl.semaphore_signal(barrier, inc=1, device_id=dev, device_id_type=MESH)

    own_rows = pl.ds(pl.multiple_of(ROWS * c, 32), ROWS)
    other_rows = pl.ds(pl.multiple_of(ROWS * (1 - c), 32), ROWS)
    feats[2 * ROWS : IMGS, :] = jnp.zeros((IMGS - 2 * ROWS, D), BF16)
    loads = [
        pltpu.make_async_copy(src, dst, load_sem.at[at])
        for at, (src, dst) in enumerate(
            [
                (feat_ref, feats.at[own_rows]),
                (up_ref, up_v),
                (down_ref, down_v),
                (head_ref, head_v),
                (vis_ref, vis_v),
            ]
        )
    ]
    for at in (L_UP, L_DOWN, L_FEAT, L_VIS, L_HEAD):
        loads[at].start()

    hidden = text_ref[...].astype(F32)
    lifted = layer_norm(hidden, ln_ref[...].reshape(1, D)).astype(BF16)
    loads[L_UP].wait()
    active = jax.nn.gelu(mm_t(lifted, up_v[...]), approximate=True).astype(BF16)
    loads[L_DOWN].wait()
    mixed = mm(active, down_v[...])
    for j in range(TS):
        mix_s[j, 0:TEXTS] = mixed[TEXTS * j : TEXTS * (j + 1)].astype(BF16)
        mix_s[j, TEXTS:SLOT] = jnp.zeros((SLOT - TEXTS, D), BF16)

    pl.semaphore_wait(barrier, len(greeted))

    def exchange_start(src, dst, sem):
        for k in range(1, TS):
            rcopy(src.at[tpeer(k)], dst.at[t], sem + k, sem + t, (d, tpeer(k))).start()

    def exchange_wait(src, dst, sem):
        for k in range(1, TS):
            j = tpeer(k)
            rcopy(src.at[j], dst.at[t], sem + k, sem + t, (d, j)).wait_send()
            rcopy(src.at[j], dst.at[j], sem + k, sem + j, (d, j)).wait_recv()

    exchange_start(mix_s, mix_r, S_MIX)
    loads[L_FEAT].wait()
    feat_copy = rcopy(feats.at[own_rows], feats.at[own_rows], S_FEAT, S_FEAT, c_peer)
    feat_copy.start()
    mix_r[t] = jnp.zeros((SLOT, D), BF16)
    with_hidden = mixed + hidden
    for j in range(TS):
        mix_f[j, 0:TEXTS] = with_hidden[TEXTS * j : TEXTS * (j + 1)]
        mix_f[j, TEXTS:SLOT] = jnp.zeros((SLOT - TEXTS, D), F32)

    loads[L_VIS].wait()
    feat_copy.wait_send()
    rcopy(feats.at[other_rows], feats.at[other_rows], S_FEAT, S_FEAT, c_peer).wait_recv()
    part_t[...] = mm_t(vis_v[...], feats[...])
    img_s[...] = part_t[pl.ds(pl.multiple_of(PIECE * c, 8), PIECE), :].astype(BF16)
    for k in range(1, TS):
        rcopy(img_s, img_r.at[c, t], S_IMG + k, S_IMG + t, (d, tpeer(k))).start()
    img_r[c, t] = img_s[...]

    exchange_wait(mix_s, mix_r, S_MIX)
    total = mix_f[t]
    for j in range(TS):
        total = total + mix_r[j].astype(F32)
    normed = layer_norm(total, fg_ref[...].reshape(1, D)).astype(BF16).astype(F32)
    for j in range(TS):
        nrm_s[j, :, 0:COLS] = normed[:, COLS * j : COLS * (j + 1)].astype(BF16)
    exchange_start(nrm_s, nrm_r, S_NRM)
    nrm_r[t] = nrm_s[t]

    exchange_wait(nrm_s, nrm_r, S_NRM)
    for j in range(TS):
        nrm_a[SLOT * j : SLOT * (j + 1), :] = nrm_r[j].astype(F32)[:, 0:COLS]
    loads[L_HEAD].wait()
    head_part = mm(nrm_a[...].astype(BF16), head_v[...])
    for j in range(TS):
        head_f[j] = head_part[SLOT * j : SLOT * (j + 1)]
        head_s[j] = head_part[SLOT * j : SLOT * (j + 1)].astype(BF16)
    exchange_start(head_s, head_r, S_HEAD)
    head_r[t] = jnp.zeros((SLOT, E), BF16)

    for k in range(1, TS):
        j = tpeer(k)
        rcopy(img_s, img_r.at[c, t], S_IMG + k, S_IMG + t, (d, j)).wait_send()
        rcopy(img_s, img_r.at[c, j], S_IMG + k, S_IMG + j, (d, j)).wait_recv()
    imgc_copy = rcopy(img_r.at[c], img_r.at[c], S_IMGC, S_IMGC, c_peer)
    imgc_copy.start()

    imgc_copy.wait_send()
    rcopy(img_r.at[1 - c], img_r.at[1 - c], S_IMGC, S_IMGC, c_peer).wait_recv()
    for j in range(TS):
        for h in range(2):
            at = COLS * j + PIECE * h
            img_f[at : at + PIECE, :] = img_r[h, j].astype(F32)
    emb_t = img_f[...]
    inverse = lax.rsqrt(jnp.sum(emb_t * emb_t, axis=0, keepdims=True) + norm_eps)
    inv_ref[...] = inverse
    unit_t = emb_t * inverse
    img_f[...] = unit_t
    img_ut[...] = unit_t.astype(BF16)

    exchange_wait(head_s, head_r, S_HEAD)
    text_emb = head_f[t]
    for j in range(TS):
        text_emb = text_emb + head_r[j].astype(F32)
    text_unit = text_emb * lax.rsqrt(
        jnp.sum(text_emb * text_emb, axis=1, keepdims=True) + norm_eps
    )
    texts[0, 0, 0] = text_unit.astype(BF16)

    def is_first(s):
        return isinstance(s, int) and s == 1

    def ag_copy(s, way, half):
        source = texts.at[0, 0, half] if is_first(s) else texts.at[s - 1, way, half]
        sem = S_AG + 4 * (s - 1) + 2 * way + half
        return rcopy(source, texts.at[s, way, half], sem, sem, (z_next, z_prev)[way])

    yh_copy = rcopy(texts.at[0, 0, 0], texts.at[0, 0, 1], S_YH, S_YH, yh_peer)
    ag_copy(1, 0, 0).start()
    ag_copy(1, 1, 0).start()
    yh_copy.start()

    row_ids = lax.broadcasted_iota(jnp.int32, (CHUNK, IMGS), 0)
    col_ids = lax.broadcasted_iota(jnp.int32, (CHUNK, IMGS), 1)
    diagonal = ((row_ids < TEXTS) & (col_ids == row_ids + ROWS * c + TEXTS * t)).astype(F32)

    def gy_copy(s, way):
        sem = S_GY + 2 * s + way
        return rcopy(gy_s.at[s, way], gy_r.at[s, way], sem, sem, yh_peer)

    own_pieces = ((0, 0), (0, 1))
    far_pieces = ((0, 0), (1, 1))
    pair_pieces = ((0, 0), (0, 1), (1, 0), (1, 1))

    def weigh(s, pieces):
        rows = SLOT * len(pieces)
        for at, (way, half) in enumerate(pieces):
            block_f[SLOT * at : SLOT * (at + 1), :] = texts[s, way, half].astype(F32)
        block = block_f[0:rows, :].astype(BF16)
        dots = mm(block, img_ut[...])
        weights = jax.nn.sigmoid(logit_scale * dots + logit_bias)
        if pieces is own_pieces:
            weights = weights - diagonal
        weights = (weights * (logit_scale / ROWS)).astype(BF16)
        radial = jnp.sum(weights.astype(F32) * dots, axis=0, keepdims=True)
        terms = lax.dot_general(
            block, weights, (((0,), (0,)), ((), ())), preferred_element_type=F32
        )
        if pieces is own_pieces:
            rad_ref[...] = radial
            eg[...] = terms
        else:
            rad_ref[...] += radial
            eg[...] += terms
        return weights

    def text_terms(s, pieces, weights):
        terms = mm(weights, img_u[...])
        for at, (way, half) in enumerate(pieces):
            part = terms[SLOT * at : SLOT * (at + 1)]
            slot = way if pieces is pair_pieces else 0
            if half == 0:
                grads[s, slot] = part
            else:
                gy_s[s, slot] = part.astype(BF16)
                gy_copy(s, slot).start()

    def forward(s, half):
        for way in range(2):
            ag_copy(s, way, half).wait_recv()
            if half == way:
                ag_copy(s + 1, way, half).start()
            else:

                @pl.when(s < HALF - 1)
                def _():
                    ag_copy(s + 1, way, half).start()

    yh_copy.wait()
    ag_copy(1, 0, 1).start()
    ag_copy(1, 1, 1).start()
    img_u[...] = img_f[...].T.astype(BF16)
    first_step = jnp.int32(1)
    forward(first_step, 0)
    own_weights = weigh(0, own_pieces)
    forward(first_step, 1)
    text_terms(0, own_pieces, own_weights)

    def ag_step(s, _):
        forward(s, 0)
        weights = weigh(s - 1, pair_pieces)
        forward(s, 1)
        text_terms(s - 1, pair_pieces, weights)
        return 0

    lax.fori_loop(2, HALF, ag_step, 0)
    text_terms(HALF - 1, pair_pieces, weigh(HALF - 1, pair_pieces))

    def rs_copy(way, s):
        sem = S_RS + 2 * (s - 1) + way
        return rcopy(rs_s.at[way, s - 1], rs_r.at[way, s - 1], sem, sem, (z_next, z_prev)[way])

    def rs_step(s):
        left = HALF + 1 - s
        for way in range(2):
            slot = 1 - way
            gy_copy(left, slot).wait_recv()
            value = grads[left, slot] + gy_r[left, slot].astype(F32)
            if s > 2:
                rs_copy(way, s - 1).wait_recv()
                value = value + rs_r[way, s - 2].astype(F32)
            rs_s[way, s - 1] = value.astype(BF16)
            rs_copy(way, s).start()

    far_copy = rcopy(far_s, far_r, S_FAR, S_FAR, z_far)

    ag_copy(HALF, 0, 0).wait_recv()
    ag_copy(HALF, 1, 1).wait_recv()
    far_weights = weigh(HALF, far_pieces)

    radial = rad_ref[...]
    inverse = inv_ref[...]

    def emb_piece(j, half):
        rows = pl.ds(pl.multiple_of(COLS * j + PIECE * half, 8), PIECE)
        return (eg[rows, :] - img_f[rows, :] * radial) * inverse

    def cx_copy(k):
        j = tpeer(k)
        return rcopy(cx_s.at[j], cx_r.at[j], S_CX + k % TS, S_CX + k % TS, c_peer)

    for k in range(1, TS + 1):
        cx_s[tpeer(k)] = emb_piece(tpeer(k), 1 - c).astype(BF16)
        cx_copy(k).start()
    rs_step(2)
    text_terms(HALF, far_pieces, far_weights)
    for k in range(1, TS + 1):
        j = tpeer(k)
        value = emb_piece(j, c)
        cx_copy(k).wait()
        value = value + cx_r[j].astype(F32)
        if k < TS:
            px_s[j] = value.astype(BF16)
            rcopy(px_s.at[j], px_r.at[t], S_PX + k, S_PX + t, (d, j)).start()
        else:
            px_f[...] = value
    px_r[t] = jnp.zeros((PIECE, IMGS), BF16)
    emb_b[PIECE:WIDE, :] = jnp.zeros((WIDE - PIECE, IMGS), F32)
    rs_step(3)
    gy_copy(HALF, 0).wait_recv()
    far_s[...] = (grads[HALF, 0] + gy_r[HALF, 0].astype(F32)).astype(BF16)
    far_copy.start()
    rs_step(4)
    exchange_wait(px_s, px_r, S_PX)
    emb_grad = px_f[...]
    for j in range(TS):
        emb_grad = emb_grad + px_r[j].astype(F32)
    emb_b[0:PIECE, :] = emb_grad
    vg_all[...] = mm(emb_b[...].astype(BF16), feats[...]).T

    def vr_copy(way, s):
        sem = (S_VRP, S_VRM)[way] + s - 1
        return rcopy(vr_s.at[way, s - 1], vr_r.at[way, s - 1], sem, sem, (z_next, z_prev)[way])

    def vg_chunk(owner):
        return vg_all[pl.ds(pl.multiple_of(ZROWS * owner, 8), ZROWS), :]

    def vr_step(way, s):
        owner = zmod(z + HALF + 1 - s) if way == 0 else zmod(z - HALF + s)
        value = vg_chunk(owner)
        if s > 1:
            vr_copy(way, s - 1).wait_recv()
            value = value + vr_r[way, s - 2]
        vr_s[way, s - 1] = value
        vr_copy(way, s).start()

    for s in range(1, HALF + 1):
        vr_step(0, s)
        if s < HALF:
            vr_step(1, s)
        if s + 4 <= HALF:
            rs_step(s + 4)
        if s == HALF - 3:
            far_copy.wait()
            gy_copy(0, 0).wait_recv()
            rs_copy(0, HALF).wait_recv()
            rs_copy(1, HALF).wait_recv()
            total_tg = (
                grads[0, 0]
                + gy_r[0, 0].astype(F32)
                + rs_r[0, HALF - 1].astype(F32)
                + rs_r[1, HALF - 1].astype(F32)
                + far_r[...].astype(F32)
            )
            tg_ref[...] = total_tg[0:TEXTS]

    vr_copy(0, HALF).wait_recv()
    vr_copy(1, HALF - 1).wait_recv()
    fx[q] = vg_chunk(z) + vr_r[0, HALF - 1] + vr_r[1, HALF - 2]
    for k in range(1, 4):
        rcopy(fx.at[q], fx.at[q], S_FX + k, S_FX + q, fx_peers[k - 1]).start()

    for half in range(2):
        for way in range(2):
            ag_copy(1, way, half).wait_send()

    def ag_drain(s, _):
        for half in range(2):
            for way in range(2):
                if half == way:
                    ag_copy(s, way, half).wait_send()
                else:

                    @pl.when(s < HALF)
                    def _():
                        ag_copy(s, way, half).wait_send()

        return 0

    lax.fori_loop(2, HALF + 1, ag_drain, 0)

    def gy_drain(s, _):
        gy_copy(s, 0).wait_send()
        gy_copy(s, 1).wait_send()
        return 0

    gy_copy(0, 0).wait_send()
    lax.fori_loop(1, HALF, gy_drain, 0)
    gy_copy(HALF, 0).wait_send()
    for s in range(1, HALF + 1):
        for way in range(2):
            if s > 1:
                rs_copy(way, s).wait_send()
            if s < HALF or way == 0:
                vr_copy(way, s).wait_send()

    for k in range(1, 4):
        o = lax.rem(q + k, 4)
        rcopy(fx.at[q], fx.at[q], S_FX + k, S_FX + q, fx_peers[k - 1]).wait_send()
        rcopy(fx.at[o], fx.at[o], S_FX + k, S_FX + o, fx_peers[k - 1]).wait_recv()
    left = fx[0] + fx[2]
    right = fx[1] + fx[3]
    for k in range(4):

        @pl.when(q == k)
        def _():
            vg_ref[:, 0:PIECE] = left[18 * k : 18 * (k + 1), 0:PIECE]
            vg_ref[:, PIECE:COLS] = right[18 * k : 18 * (k + 1), 0:PIECE]


def local(
    text_hidden,
    ln_gain,
    up_weight,
    down_weight,
    final_gain,
    head_weight,
    image_features,
    vision_weight,
):
    vmem = pl.BlockSpec(memory_space=pltpu.VMEM)
    hbm = pl.BlockSpec(memory_space=pl.ANY)
    scratch = [
        ((FF_DEV, D), BF16),
        ((FF_DEV, D), BF16),
        ((COLS, E), BF16),
        ((COLS, D), BF16),
        ((IMGS, D), BF16),
        ((COLS, IMGS), F32),
        ((PIECE, IMGS), BF16),
        ((2, TS, PIECE, IMGS), BF16),
        ((E, IMGS), F32),
        ((E, IMGS), BF16),
        ((IMGS, E), BF16),
        ((1, IMGS), F32),
        ((1, IMGS), F32),
        ((TS, SLOT, D), BF16),
        ((TS, SLOT, D), F32),
        ((TS, SLOT, D), BF16),
        ((TS, SLOT, 2 * WIDE), BF16),
        ((TS, SLOT, 2 * WIDE), BF16),
        ((TS * SLOT, COLS), F32),
        ((TS, SLOT, E), BF16),
        ((TS, SLOT, E), F32),
        ((TS, SLOT, E), BF16),
        ((2 * CHUNK, E), F32),
        ((HALF + 1, 2, 2, SLOT, E), BF16),
        ((HALF + 1, 2, SLOT, E), F32),
        ((E, IMGS), F32),
        ((2, HALF, SLOT, E), BF16),
        ((2, HALF, SLOT, E), BF16),
        ((HALF + 1, 2, SLOT, E), BF16),
        ((HALF + 1, 2, SLOT, E), BF16),
        ((SLOT, E), BF16),
        ((SLOT, E), BF16),
        ((TS, PIECE, IMGS), BF16),
        ((TS, PIECE, IMGS), BF16),
        ((PIECE, IMGS), F32),
        ((TS, PIECE, IMGS), BF16),
        ((TS, PIECE, IMGS), BF16),
        ((WIDE, IMGS), F32),
        ((D, WIDE), F32),
        ((2, HALF, ZROWS, WIDE), F32),
        ((2, HALF, ZROWS, WIDE), F32),
        ((4, ZROWS, WIDE), F32),
    ]
    return pl.pallas_call(
        kernel,
        out_shape=(
            jax.ShapeDtypeStruct((TEXTS, E), F32),
            jax.ShapeDtypeStruct((D // 64, COLS), F32),
        ),
        in_specs=[vmem, vmem, hbm, hbm, vmem, hbm, hbm, hbm],
        out_specs=(vmem, vmem),
        scratch_shapes=[pltpu.VMEM(shape, kind) for shape, kind in scratch]
        + [pltpu.SemaphoreType.DMA((size,)) for size in (S_ALL, S_ALL, 5)],
        compiler_params=pltpu.CompilerParams(
            collective_id=0, has_side_effects=True, vmem_limit_bytes=56 * 1024 * 1024
        ),
    )(
        text_hidden,
        ln_gain,
        up_weight.T,
        down_weight,
        final_gain,
        head_weight,
        image_features,
        vision_weight.T,
    )


def solution(mesh):
    placed = (
        P("dp", None),
        P(),
        P(None, "tensor"),
        P("tensor", None),
        P(),
        P("tensor", None),
        P("dp", None),
        P(None, "tensor"),
    )
    return jax.shard_map(
        local,
        mesh=mesh,
        in_specs=placed,
        out_specs=(P(("dp", "tensor"), None), P("dp", "tensor")),
        check_vma=False,
    )
```
